32 devices in a mesh: front: 8 (over y, x, core), row: 4 (over z).
Axes of the slice: x: 2, y: 2, z: 4, core: 2. Of those that a mesh axis runs over, the one named last changes fastest.
Arguments:
- rhs_front: bfloat16 [16384, 384], P(('front', 'row')), may hold values from -6 to 6
- rhs_root: float32 [12288, 384], P('row'), may hold values from -6 to 6
- pivot_inverse: bfloat16 [16384, 2048], P(('front', 'row')), may hold values from -0.125 to 0.125
- border_coupling: bfloat16 [49152, 2048], P(('front', 'row')), may hold values from -0.125 to 0.125
- root_inverse: bfloat16 [12288, 12288], P('front', 'row'), may hold values from -0.0546875 to 0.0546875
- border_map: int32 [8, 48], P('front', 'row'), may hold values from 0 to 95, as said below
Outputs:
- front_solution: float32 [16384, 384], P(('front', 'row'))
- root_solution: float32 [12288, 384], P(('front', 'row'))
The draws below stay inside these ranges and needn't reach their ends.
Inputs may be any that keep to these rules, and one draw needn't show every extreme that they name: `border_map`: for each front and each index r of row, the 12 border blocks held at that index name distinct root blocks, all among blocks r * 24 to (r + 1) * 24 - 1; a root block may be named by many fronts or by none.
All inputs are finite; a program needn't handle non-finite values.
Results may differ from the reference program's by a relative error of at most 0.0075.
Values may be sent and summed in bfloat16 or wider, within the bound.
No kernel may reach another device: no remote copies, remote signals or barrier semaphores. Data moves between devices by JAX's collectives and lax.ppermute only.
A program may use at most 64 MiB of HBM per device.

```python
import jax
import jax.numpy as jnp
from jax import lax

PIV = 2048
BORD = 6144
ROOT = 12288
BLK = 128
NRHS = 384
FRONTS = 8
BORD_BLK = 12
SPAN_BLK = 24


def draw_border_map(key, part):
    span_blocks = SPAN_BLK
    per_device = BORD_BLK
    row_slices = BORD // BLK // BORD_BLK
    slice_count = FRONTS * row_slices
    jitter = jax.random.randint(jax.random.fold_in(key, 11), (slice_count, span_blocks), 0, 4096)
    favour = jax.random.randint(jax.random.fold_in(key, 12), (span_blocks,), 0, 3)
    favour = favour.at[0].set(3).at[span_blocks - 1].set(4)
    scores = (jitter + favour[None, :] * 1024) * span_blocks + jnp.arange(span_blocks, dtype=jnp.int32)[None, :]
    top_scores, chosen = lax.top_k(scores, per_device)
    offsets = jnp.arange(slice_count, dtype=jnp.int32) % row_slices * span_blocks
    return (chosen.astype(jnp.int32) + offsets[:, None]).reshape(FRONTS, per_device * row_slices)


def block_levels(key, dims, split, low, high):
    loudness = 1.0
    for dim, shards_of in split:
        steps = jax.random.uniform(jax.random.fold_in(jax.random.fold_in(key, 6), dim), (shards_of,), jnp.float32, low / len(split), high / len(split))
        loudness = loudness * jnp.repeat(jnp.exp(steps), dims[dim] // shards_of).reshape((-1,) + (1,) * (len(dims) - 1 - dim))
    return loudness


def noise(own_key, shape, width, limit, pieces=(), held_as=jnp.bfloat16):
    gain = block_levels(own_key, shape, pieces, -0.22, 0.18) if pieces else 1.0
    entries = jax.random.normal(own_key, shape, jnp.float32) * width * gain
    return jnp.minimum(jnp.maximum(entries, -limit), limit).astype(held_as)


def setup_inputs(seed: int = 0) -> dict:
    arg_keys = jax.random.split(jax.random.key(seed), 7)
    return {
        "rhs_front": noise(arg_keys[0], (FRONTS * PIV, NRHS), 1.0, 6.0, ((0, 32),)),
        "rhs_root": noise(arg_keys[1], (ROOT, NRHS), 1.0, 6.0, ((0, 4),), jnp.float32),
        "pivot_inverse": noise(arg_keys[2], (FRONTS * PIV, PIV), PIV ** -0.5, 0.125, ((0, 32),)),
        "border_coupling": noise(arg_keys[3], (FRONTS * BORD, PIV), PIV ** -0.5, 0.125, ((0, 32),)),
        "root_inverse": noise(arg_keys[4], (ROOT, ROOT), ROOT ** -0.5, 0.0546875, ((0, 8), (1, 4))),
        "border_map": draw_border_map(jax.random.fold_in(arg_keys[6], 71), 0),
    }


def reference(rhs_front, rhs_root, pivot_inverse, border_coupling, root_inverse, border_map):
    front_count = border_map.shape[0]
    block_count = BORD // BLK
    rhs_three = rhs_front.reshape(front_count, PIV, NRHS)
    pinv_three = pivot_inverse.reshape(front_count, PIV, PIV)
    coupling_three = border_coupling.reshape(front_count, BORD, PIV)

    def forward(items):
        pinv_one, coupling_one, rhs_one = items
        inner = jnp.dot(pinv_one, rhs_one, preferred_element_type=jnp.float32)
        contrib = jnp.dot(coupling_one, inner.astype(jnp.bfloat16), preferred_element_type=jnp.float32)
        return inner, contrib

    inner_all, contrib_all = lax.map(forward, (pinv_three, coupling_three, rhs_three))
    blocks = contrib_all.reshape(front_count * block_count, BLK * NRHS)
    assembled = jax.ops.segment_sum(blocks, border_map.reshape(-1), num_segments=ROOT // BLK)
    schur_rhs = (rhs_root - assembled.reshape(ROOT, NRHS)).astype(jnp.bfloat16)
    root_solution = jnp.dot(root_inverse, schur_rhs, preferred_element_type=jnp.float32)
    root_half = root_solution.astype(jnp.bfloat16)
    root_blocks = root_half.reshape(ROOT // BLK, BLK, NRHS)

    def backward(items):
        pinv_one, coupling_one, inner_one, index_row = items
        picked = jnp.take(root_blocks, index_row, axis=0).reshape(BORD, NRHS)
        pulled = lax.dot_general(coupling_one, picked, (((0,), (0,)), ((), ())), preferred_element_type=jnp.float32).astype(jnp.bfloat16)
        return inner_one - jnp.dot(pinv_one, pulled, preferred_element_type=jnp.float32)

    solved = lax.map(backward, (pinv_three, coupling_three, inner_all, border_map))
    return solved.reshape(front_count * PIV, NRHS), root_solution
```

```python
import functools

import jax
import jax.numpy as jnp
from jax import lax
from jax.sharding import PartitionSpec as P

BLK = 128
F32 = jnp.float32
BF16 = jnp.bfloat16


def shift(x, axis, size, by):
    return lax.ppermute(x, axis, [(i, (i + by) % size) for i in range(size)])


def gather_row(x, n, at):
    length = x.shape[0]
    whole = lax.dynamic_update_slice_in_dim(
        jnp.zeros((n * length,) + x.shape[1:], x.dtype), x, at * length, 0
    )
    up, down = x, x
    for step in range(1, n // 2 + 1):
        up = shift(up, "row", n, 1)
        whole = lax.dynamic_update_slice_in_dim(whole, up, (at - step) % n * length, 0)
        if step < n - step:
            down = shift(down, "row", n, -1)
            whole = lax.dynamic_update_slice_in_dim(whole, down, (at + step) % n * length, 0)
    return whole


def scatter_row(partial, n, at):
    length = partial.shape[0] // n

    def block(offset):
        return lax.dynamic_slice_in_dim(partial, (at + offset) % n * length, length, 0)

    total = block(0)
    for sign, far in ((-1, n // 2), (1, (n - 1) // 2)):
        running = None
        for step in range(far, 0, -1):
            mine = block(sign * step)
            running = mine if running is None else running.astype(F32) + mine
            running = shift(running.astype(BF16), "row", n, sign)
        if running is not None:
            total = total + running.astype(F32)
    return total


def per_device(n_front, n_row, rhs_front, rhs_root, pivot_inverse, border_coupling, root_inverse, border_map):
    row_at = lax.axis_index("row")
    front_at = lax.axis_index("front")
    width = rhs_front.shape[1]

    inner = jnp.dot(pivot_inverse, gather_row(rhs_front, n_row, row_at), preferred_element_type=F32)
    inner_half = inner.astype(BF16)
    contrib = jnp.dot(
        border_coupling, gather_row(inner_half, n_row, row_at), preferred_element_type=F32
    ).astype(BF16)
    block_local = border_map.shape[1]
    span_rows = root_inverse.shape[1]
    span_blocks = span_rows // BLK
    local_index = border_map[0] - row_at * span_blocks
    select = (local_index[None, :] == jnp.arange(span_blocks, dtype=jnp.int32)[:, None]).astype(BF16)
    dense = jnp.einsum(
        "kj,jcn->kcn", select, contrib.reshape(block_local, BLK, width), preferred_element_type=F32
    ).astype(BF16).reshape(span_rows, width)
    shares = lax.psum_scatter(dense, "front", scatter_dimension=0, tiled=True).astype(F32)
    own_rhs = lax.dynamic_slice_in_dim(rhs_root, front_at * shares.shape[0], shares.shape[0], 0)
    schur_piece = (own_rhs - shares).astype(BF16)
    schur_rhs = lax.all_gather(schur_piece, "front", axis=0, tiled=True)
    root_solution = scatter_row(
        jnp.dot(root_inverse, schur_rhs, preferred_element_type=F32), n_row, row_at
    )
    root_half = root_solution.astype(BF16)
    if n_front == 2 * n_row:
        perm = [
            ((chip * 2 + core) * n_row + row, (row * 2 + core) * n_row + chip)
            for chip in range(n_row)
            for core in range(2)
            for row in range(n_row)
        ]
        moved = lax.ppermute(root_half, ("front", "row"), perm)
        ranged = lax.all_gather(moved, "front", axis=0, tiled=True)
        ranged = ranged.reshape(n_row, 2, root_half.shape[0], width).swapaxes(0, 1)
        ranged = ranged.reshape(span_rows, width)
    else:
        gathered = lax.all_gather(root_half, ("front", "row"), axis=0, tiled=True)
        ranged = lax.dynamic_slice_in_dim(gathered, row_at * span_rows, span_rows, 0)
    picked = jnp.einsum(
        "kj,kcn->jcn", select, ranged.reshape(span_blocks, BLK, width), preferred_element_type=F32
    )
    picked = picked.astype(BF16).reshape(block_local * BLK, width)
    pulled = scatter_row(
        lax.dot_general(border_coupling, picked, (((0,), (0,)), ((), ())), preferred_element_type=F32),
        n_row,
        row_at,
    ).astype(BF16)
    correction = jnp.dot(pivot_inverse, gather_row(pulled, n_row, row_at), preferred_element_type=F32)
    return (inner - correction, root_solution)


def solution(mesh):
    in_specs = (
        P(("front", "row"), None),
        P("row", None),
        P(("front", "row"), None),
        P(("front", "row"), None),
        P("front", "row"),
        P("front", "row"),
    )
    out_specs = (P(("front", "row"), None), P(("front", "row"), None))
    body = functools.partial(per_device, mesh.shape["front"], mesh.shape["row"])
    return jax.shard_map(body, mesh=mesh, in_specs=in_specs, out_specs=out_specs, check_vma=False)
```

```python
import functools

import jax
import jax.numpy as jnp
from jax import lax
from jax.experimental import pallas as pl
from jax.experimental.pallas import tpu as pltpu
from jax.sharding import PartitionSpec as P

BLK = 128
F32 = jnp.float32
BF16 = jnp.bfloat16
VMEM = pl.BlockSpec(memory_space=pltpu.VMEM)
ANY = pl.BlockSpec(memory_space=pl.ANY)
VMEM_LIMIT = 56 * 1024 * 1024


def dot(a, b, contract=((1,), (0,))):
    return lax.dot_general(a, b, (contract, ((), ())), preferred_element_type=F32)


def kernel_call(body, out_shape, grid, n_scalars, in_specs, out_specs, scratch, flops, nbytes):
    return pl.pallas_call(
        body,
        out_shape=out_shape,
        grid_spec=pltpu.PrefetchScalarGridSpec(
            num_scalar_prefetch=n_scalars,
            grid=grid,
            in_specs=in_specs,
            out_specs=out_specs,
            scratch_shapes=scratch,
        ),
        compiler_params=pltpu.CompilerParams(vmem_limit_bytes=VMEM_LIMIT),
        cost_estimate=pl.CostEstimate(flops=flops, bytes_accessed=nbytes, transcendentals=0),
    )


def whole(shape):
    return pl.BlockSpec(shape, lambda *_: (0,) * len(shape))


def shift(x, size, by):
    return lax.ppermute(x, "row", [(i, (i + by) % size) for i in range(size)])


def swap(x, size, by):
    return lax.ppermute(x, "front", [(i, i ^ by) for i in range(size)])


def gather_row(x, n):
    found = [(0, x)]
    up, down = x, x
    for step in range(1, n // 2 + 1):
        up = shift(up, n, 1)
        found.append((-step, up))
        if step < n - step:
            down = shift(down, n, -1)
            found.append((step, down))
    return found


def gather_front(x, n):
    found = {0: x, 1: swap(x, n, 1)}
    for d in range(2, n, 2):
        found[d] = swap(x, n, d)
    for d in range(2, n, 2):
        found[d + 1] = swap(found[d], n, 1)
    return [found[d] for d in range(n)]


def far_offsets(n):
    first = [-(n // 2)] + ([(n - 1) // 2] if n > 2 else [])
    later = [o for o in range(-(n // 2) + 1, (n - 1) // 2) if o]
    return first, later


def scatter_row(first, later, own, n):
    total = own
    for sign, far in ((-1, n // 2), (1, (n - 1) // 2)):
        running = None
        for step in range(far, 0, -1):
            if running is None:
                running = first[sign * step]
            else:
                running = (running.astype(F32) + later[sign * step]).astype(BF16)
            running = shift(running, n, sign)
        if running is not None:
            total = total + running.astype(F32)
    return total


def accumulate(at_ref, a_ref, offsets, x_refs, n_row, contract=((1,), (0,))):
    depth = a_ref.shape[1] // n_row
    total = None
    for offset, x_ref in zip(offsets, x_refs):
        owner = lax.rem(at_ref[0] + (offset + n_row), n_row)
        columns = pl.ds(pl.multiple_of(owner * depth, depth), depth)
        part = dot(a_ref[:, columns], x_ref[...], contract)
        total = part if total is None else total + part
    return total


def pivot_forward(at, pivot, found, n_row):
    rows, width = pivot.shape[0], found[0][1].shape[1]
    offsets = [o for o, _ in found]

    def body(at_ref, a_ref, *refs):
        total = accumulate(at_ref, a_ref, offsets, refs[: len(offsets)], n_row)
        refs[-2][...] = total
        refs[-1][...] = total.astype(BF16)

    return kernel_call(
        body,
        [jax.ShapeDtypeStruct((rows, width), F32), jax.ShapeDtypeStruct((rows, width), BF16)],
        (1,),
        1,
        [whole(pivot.shape)] + [whole(x.shape) for _, x in found],
        [whole((rows, width))] * 2,
        [],
        2 * pivot.size * width,
        2 * pivot.size,
    )(at, pivot, *[x for _, x in found])


def pivot_backward(at, pivot, found, inner, n_row):
    rows, width = inner.shape
    offsets = [o for o, _ in found]

    def body(at_ref, a_ref, inner_ref, *refs):
        total = accumulate(at_ref, a_ref, offsets, refs[: len(offsets)], n_row, ((1,), (1,)))
        refs[-1][...] = inner_ref[...] - total

    return kernel_call(
        body,
        jax.ShapeDtypeStruct((rows, width), F32),
        (1,),
        1,
        [whole(pivot.shape), whole(inner.shape)] + [whole(x.shape) for _, x in found],
        whole((rows, width)),
        [],
        2 * pivot.size * width,
        2 * pivot.size,
    )(at, pivot, inner, *[x for _, x in found])


def border_forward(at, local_index, coupling, found, n_row, n_front, span_rows):
    rows, depth = coupling.shape
    width = found[0][1].shape[1]
    offsets = [o for o, _ in found]
    blocks = rows // BLK
    per_step = next(k for k in (4, 3, 2, 1) if blocks % k == 0)
    piece_blocks = span_rows // n_front // BLK

    def body(at_ref, index_ref, a_ref, *refs):
        send_ref, keep_ref = refs[-2], refs[-1]
        step = pl.program_id(0)

        @pl.when(step == 0)
        def _():
            send_ref[...] = jnp.zeros_like(send_ref)
            keep_ref[...] = jnp.zeros_like(keep_ref)

        total = accumulate(at_ref, a_ref, offsets, refs[: len(offsets)], n_row).astype(BF16)
        for j in range(per_step):
            target = index_ref[step * per_step + j]
            away = lax.bitwise_xor(lax.div(target, piece_blocks), at_ref[1])
            slot = lax.shift_right_logical(away, 1) * piece_blocks + lax.rem(target, piece_blocks)
            place = pl.ds(pl.multiple_of(slot * BLK, BLK), BLK)
            block = total[j * BLK : (j + 1) * BLK]

            @pl.when(lax.rem(away, 2) == 1)
            def _():
                send_ref[place, :] = block

            @pl.when(lax.rem(away, 2) == 0)
            def _():
                keep_ref[place, :] = block

    half = jax.ShapeDtypeStruct((span_rows // 2, width), BF16)
    return kernel_call(
        body,
        [half, half],
        (blocks // per_step,),
        2,
        [pl.BlockSpec((per_step * BLK, depth), lambda i, *_: (i, 0))] + [whole(x.shape) for _, x in found],
        [whole(half.shape)] * 2,
        [],
        2 * coupling.size * width,
        2 * coupling.size,
    )(at, local_index, coupling, *[x for _, x in found])


def root_products(at, inverse, pieces, offsets, kinds, n_row, n_front):
    span_rows = inverse.shape[1]
    rows = inverse.shape[0] // n_row
    width = pieces[0].shape[1]
    piece_rows = pieces[0].shape[0]
    count = len(offsets)
    owners = (at[0] + jnp.array([o + n_row for o in offsets], jnp.int32)) % n_row

    def body(at_ref, owner_ref, a_ref, *refs):
        piece_refs, out_refs = refs[:n_front], refs[n_front : n_front + count]
        x_ref, sems = refs[-2], refs[-1]
        step = pl.program_id(0)

        @pl.when(step == 0)
        def _():
            copies = []
            for d in range(n_front):
                start = lax.bitwise_xor(at_ref[1], d) * piece_rows
                place = pl.ds(pl.multiple_of(start, piece_rows), piece_rows)
                copies.append(pltpu.make_async_copy(piece_refs[d], x_ref.at[place], sems.at[d]))
            for copy in copies:
                copy.start()
            for copy in copies:
                copy.wait()

        total = dot(a_ref[...], x_ref[...])
        for i in range(count):

            @pl.when(step == i)
            def _():
                out_refs[i][...] = total.astype(out_refs[i].dtype)

    return kernel_call(
        body,
        [jax.ShapeDtypeStruct((rows, width), kind) for kind in kinds],
        (count,),
        2,
        [pl.BlockSpec((rows, span_rows), lambda i, at_ref, owner_ref: (owner_ref[i], 0))] + [ANY] * n_front,
        [whole((rows, width))] * count,
        [pltpu.VMEM((span_rows, width), BF16), pltpu.SemaphoreType.DMA((n_front,))],
        2 * rows * span_rows * width * count,
        2 * rows * span_rows * count,
    )(at, owners, inverse, *pieces)


def border_backward(at, local_index, coupling, pieces, offsets, kinds, n_row, n_front):
    rows, depth = coupling.shape
    width = pieces[0].shape[1]
    piece_rows = pieces[0].shape[0]
    quarter = piece_rows // n_row
    span_rows = piece_rows * n_front
    columns = depth // n_row
    blocks = rows // BLK
    count = len(offsets)
    owners = (at[0] + jnp.array([o + n_row for o in offsets], jnp.int32)) % n_row

    def body(at_ref, index_ref, owner_ref, a_ref, *refs):
        piece_refs, out_refs = refs[:n_front], refs[n_front : n_front + count]
        span_ref, picked_ref, sems = refs[-3], refs[-2], refs[-1]
        step = pl.program_id(0)

        @pl.when(step == 0)
        def _():
            copies = []
            for d in range(n_front):
                there = lax.bitwise_xor(at_ref[1], d)
                chip, core = lax.shift_right_logical(there, 1), lax.rem(there, 2)
                for k in range(n_row):
                    start = core * (span_rows // 2) + lax.bitwise_xor(chip, k) * piece_rows + k * quarter
                    place = pl.ds(pl.multiple_of(start, quarter), quarter)
                    copies.append(
                        pltpu.make_async_copy(
                            piece_refs[d].at[pl.ds(k * quarter, quarter)],
                            span_ref.at[place],
                            sems.at[d * n_row + k],
                        )
                    )
            for copy in copies:
                copy.start()
            for copy in copies:
                copy.wait()
            for j in range(blocks):
                source = pl.ds(pl.multiple_of(index_ref[j] * BLK, BLK), BLK)
                picked_ref[pl.ds(j * BLK, BLK), :] = span_ref[source, :]

        total = dot(picked_ref[...], a_ref[...], ((0,), (0,)))
        for i in range(count):

            @pl.when(step == i)
            def _():
                out_refs[i][...] = total.astype(out_refs[i].dtype)

    return kernel_call(
        body,
        [jax.ShapeDtypeStruct((width, columns), kind) for kind in kinds],
        (count,),
        3,
        [pl.BlockSpec((rows, columns), lambda i, at_ref, index_ref, owner_ref: (0, owner_ref[i]))]
        + [ANY] * n_front,
        [whole((width, columns))] * count,
        [
            pltpu.VMEM((span_rows, width), BF16),
            pltpu.VMEM((rows, width), BF16),
            pltpu.SemaphoreType.DMA((n_front * n_row,)),
        ],
        2 * rows * columns * width * count,
        2 * rows * columns * count,
    )(at, local_index, owners, coupling, *pieces)


def solve(n_front, n_row, rhs_front, rhs_root, pivot_inverse, border_coupling, root_inverse, border_map):
    row_at = lax.axis_index("row").astype(jnp.int32)
    front_at = lax.axis_index("front").astype(jnp.int32)
    at = jnp.stack([row_at, front_at])
    span_rows = root_inverse.shape[1]
    piece_rows = span_rows // n_front
    local_index = border_map[0] - row_at * (span_rows // BLK)
    first_at, later_at = far_offsets(n_row)

    inner, inner_half = pivot_forward(at, pivot_inverse, gather_row(rhs_front, n_row), n_row)
    send, keep = border_forward(
        at, local_index, border_coupling, gather_row(inner_half, n_row), n_row, n_front, span_rows
    )
    came = swap(send, n_front, 1)

    def pair(i):
        rows = slice(i * piece_rows, (i + 1) * piece_rows)
        return keep[rows].astype(F32) + came[rows].astype(F32)

    shares = pair(0)
    for d in range(2, n_front, 2):
        shares = shares + swap(pair(d // 2).astype(BF16), n_front, d).astype(F32)
    own_rhs = lax.dynamic_slice_in_dim(rhs_root, front_at * piece_rows, piece_rows, 0)
    pieces = gather_front((own_rhs - shares).astype(BF16), n_front)

    def root(offsets, kind):
        outs = root_products(at, root_inverse, pieces, offsets, [kind] * len(offsets), n_row, n_front)
        return dict(zip(offsets, outs))

    first = root(first_at, BF16)
    rest = root(later_at + [0], F32)
    root_solution = scatter_row(first, rest, rest[0], n_row)
    root_half = root_solution.astype(BF16)
    quarter = root_half.shape[0] // n_row
    moved = []
    for k in range(n_row):
        perm = [
            ((chip * 2 + core) * n_row + row, ((row ^ k) * 2 + core) * n_row + chip)
            for chip in range(n_row)
            for core in range(2)
            for row in range(n_row)
        ]
        moved.append(lax.ppermute(root_half[k * quarter : (k + 1) * quarter], ("front", "row"), perm))
    spans = gather_front(jnp.concatenate(moved, axis=0), n_front)

    def border(offsets, kind):
        outs = border_backward(
            at, local_index, border_coupling, spans, offsets, [kind] * len(offsets), n_row, n_front
        )
        return dict(zip(offsets, outs))

    first = border(first_at, BF16)
    rest = border(later_at + [0], F32)
    pulled = scatter_row(first, rest, rest[0], n_row).astype(BF16)
    front_solution = pivot_backward(at, pivot_inverse, gather_row(pulled, n_row), inner, n_row)
    return front_solution, root_solution


def solve_plain(n_front, n_row, rhs_front, rhs_root, pivot_inverse, border_coupling, root_inverse, border_map):
    row_at = lax.axis_index("row")
    front_at = lax.axis_index("front")
    width = rhs_front.shape[1]
    inner = dot(pivot_inverse, lax.all_gather(rhs_front, "row", axis=0, tiled=True))
    contrib = dot(border_coupling, lax.all_gather(inner.astype(BF16), "row", axis=0, tiled=True))
    block_local = border_map.shape[1]
    span_rows = root_inverse.shape[1]
    span_blocks = span_rows // BLK
    local_index = border_map[0] - row_at * span_blocks
    select = (local_index[None, :] == jnp.arange(span_blocks, dtype=jnp.int32)[:, None]).astype(F32)
    dense = jnp.einsum(
        "kj,jcn->kcn", select, contrib.reshape(block_local, BLK, width), precision=lax.Precision.HIGHEST
    ).reshape(span_rows, width)
    shares = lax.psum_scatter(dense, "front", scatter_dimension=0, tiled=True)
    own_rhs = lax.dynamic_slice_in_dim(rhs_root, front_at * shares.shape[0], shares.shape[0], 0)
    schur_rhs = lax.all_gather((own_rhs - shares).astype(BF16), "front", axis=0, tiled=True)
    root_solution = lax.psum_scatter(dot(root_inverse, schur_rhs), "row", scatter_dimension=0, tiled=True)
    gathered = lax.all_gather(root_solution.astype(BF16), ("front", "row"), axis=0, tiled=True)
    ranged = lax.dynamic_slice_in_dim(gathered, row_at * span_rows, span_rows, 0)
    picked = jnp.take(ranged.reshape(span_blocks, BLK, width), local_index, axis=0)
    picked = picked.reshape(block_local * BLK, width)
    pulled = lax.psum_scatter(
        dot(border_coupling, picked, ((0,), (0,))), "row", scatter_dimension=0, tiled=True
    ).astype(BF16)
    correction = dot(pivot_inverse, lax.all_gather(pulled, "row", axis=0, tiled=True))
    return inner - correction, root_solution


def solution(mesh):
    in_specs = (
        P(("front", "row"), None),
        P("row", None),
        P(("front", "row"), None),
        P(("front", "row"), None),
        P("front", "row"),
        P("front", "row"),
    )
    out_specs = (P(("front", "row"), None), P(("front", "row"), None))
    n_front, n_row = mesh.shape["front"], mesh.shape["row"]

    def per_device(*arrays):
        root_inverse, width = arrays[4], arrays[0].shape[1]
        fits = (
            n_front == 2 * n_row
            and n_front & (n_front - 1) == 0
            and n_row > 2
            and root_inverse.shape[1] % (n_front * BLK) == 0
            and root_inverse.shape[0] == n_row * (root_inverse.shape[1] // n_front)
            and root_inverse.shape[1] % (n_front * n_row * 16) == 0
            and arrays[2].shape[1] % (n_row * BLK) == 0
            and width % BLK == 0
        )
        return (solve if fits else solve_plain)(n_front, n_row, *arrays)

    return jax.shard_map(per_device, mesh=mesh, in_specs=in_specs, out_specs=out_specs, check_vma=False)
```

```python
import functools

import jax
import jax.numpy as jnp
from jax import lax
from jax.experimental import pallas as pl
from jax.experimental.pallas import tpu as pltpu
from jax.sharding import PartitionSpec as P

BLK = 128
F32 = jnp.float32
BF16 = jnp.bfloat16
VMEM = pl.BlockSpec(memory_space=pltpu.VMEM)
ANY = pl.BlockSpec(memory_space=pl.ANY)
VMEM_LIMIT = 56 * 1024 * 1024


def dot(a, b, contract=((1,), (0,))):
    return lax.dot_general(a, b, (contract, ((), ())), preferred_element_type=F32)


def kernel_call(body, out_shape, grid, n_scalars, in_specs, out_specs, scratch, flops, nbytes):
    return pl.pallas_call(
        body,
        out_shape=out_shape,
        grid_spec=pltpu.PrefetchScalarGridSpec(
            num_scalar_prefetch=n_scalars,
            grid=grid,
            in_specs=in_specs,
            out_specs=out_specs,
            scratch_shapes=scratch,
        ),
        compiler_params=pltpu.CompilerParams(vmem_limit_bytes=VMEM_LIMIT),
        cost_estimate=pl.CostEstimate(flops=flops, bytes_accessed=nbytes, transcendentals=0),
    )


def whole(shape):
    return pl.BlockSpec(shape, lambda *_: (0,) * len(shape))


def shift(x, size, by):
    return lax.ppermute(x, "row", [(i, (i + by) % size) for i in range(size)])


def swap(x, size, by):
    return lax.ppermute(x, "front", [(i, i ^ by) for i in range(size)])


def gather_row(x, n):
    found = [(0, x)]
    up, down = x, x
    for step in range(1, n // 2 + 1):
        up = shift(up, n, 1)
        found.append((-step, up))
        if step < n - step:
            down = shift(down, n, -1)
            found.append((step, down))
    return found


def gather_front(x, n):
    found = {0: x, 1: swap(x, n, 1)}
    for d in range(2, n, 2):
        found[d] = swap(x, n, d)
    for d in range(2, n, 2):
        found[d + 1] = swap(found[d], n, 1)
    return [found[d] for d in range(n)]


def far_offsets(n):
    first = [-(n // 2)] + ([(n - 1) // 2] if n > 2 else [])
    later = [o for o in range(-(n // 2) + 1, (n - 1) // 2) if o]
    return first, later


def scatter_row(first, later, own, n):
    total = own
    for sign, far in ((-1, n // 2), (1, (n - 1) // 2)):
        running = None
        for step in range(far, 0, -1):
            if running is None:
                running = first[sign * step]
            else:
                running = (running.astype(F32) + later[sign * step]).astype(BF16)
            running = shift(running, n, sign)
        if running is not None:
            total = total + running.astype(F32)
    return total


def accumulate(at_ref, a_ref, offsets, x_refs, n_row, contract=((1,), (0,))):
    depth = a_ref.shape[1] // n_row
    total = None
    for offset, x_ref in zip(offsets, x_refs):
        owner = lax.rem(at_ref[0] + (offset + n_row), n_row)
        columns = pl.ds(pl.multiple_of(owner * depth, depth), depth)
        part = dot(a_ref[:, columns], x_ref[...], contract)
        total = part if total is None else total + part
    return total


def pivot_forward(at, pivot, found, n_row):
    rows, width = pivot.shape[0], found[0][1].shape[1]
    offsets = [o for o, _ in found]

    def body(at_ref, a_ref, *refs):
        total = accumulate(at_ref, a_ref, offsets, refs[: len(offsets)], n_row)
        refs[-2][...] = total
        refs[-1][...] = total.astype(BF16)

    return kernel_call(
        body,
        [jax.ShapeDtypeStruct((rows, width), F32), jax.ShapeDtypeStruct((rows, width), BF16)],
        (1,),
        1,
        [whole(pivot.shape)] + [whole(x.shape) for _, x in found],
        [whole((rows, width))] * 2,
        [],
        2 * pivot.size * width,
        2 * pivot.size,
    )(at, pivot, *[x for _, x in found])


def pivot_backward(at, pivot, found, inner, n_row):
    rows, width = inner.shape
    offsets = [o for o, _ in found]

    def body(at_ref, a_ref, inner_ref, *refs):
        total = accumulate(at_ref, a_ref, offsets, refs[: len(offsets)], n_row, ((1,), (1,)))
        refs[-1][...] = inner_ref[...] - total

    return kernel_call(
        body,
        jax.ShapeDtypeStruct((rows, width), F32),
        (1,),
        1,
        [whole(pivot.shape), whole(inner.shape)] + [whole(x.shape) for _, x in found],
        whole((rows, width)),
        [],
        2 * pivot.size * width,
        2 * pivot.size,
    )(at, pivot, inner, *[x for _, x in found])


def border_forward(at, local_index, coupling, found, n_row, n_front, span_rows):
    rows, depth = coupling.shape
    width = found[0][1].shape[1]
    offsets = [o for o, _ in found]
    blocks = rows // BLK
    per_step = next(k for k in (4, 3, 2, 1) if blocks % k == 0)
    piece_blocks = span_rows // n_front // BLK

    def body(at_ref, index_ref, a_ref, *refs):
        send_ref, keep_ref = refs[-2], refs[-1]
        step = pl.program_id(0)

        @pl.when(step == 0)
        def _():
            send_ref[...] = jnp.zeros_like(send_ref)
            keep_ref[...] = jnp.zeros_like(keep_ref)

        total = accumulate(at_ref, a_ref, offsets, refs[: len(offsets)], n_row).astype(BF16)
        for j in range(per_step):
            target = index_ref[step * per_step + j]
            away = lax.bitwise_xor(lax.div(target, piece_blocks), at_ref[1])
            slot = lax.shift_right_logical(away, 1) * piece_blocks + lax.rem(target, piece_blocks)
            place = pl.ds(pl.multiple_of(slot * BLK, BLK), BLK)
            block = total[j * BLK : (j + 1) * BLK]

            @pl.when(lax.rem(away, 2) == 1)
            def _():
                send_ref[place, :] = block

            @pl.when(lax.rem(away, 2) == 0)
            def _():
                keep_ref[place, :] = block

    half = jax.ShapeDtypeStruct((span_rows // 2, width), BF16)
    return kernel_call(
        body,
        [half, half],
        (blocks // per_step,),
        2,
        [pl.BlockSpec((per_step * BLK, depth), lambda i, *_: (i, 0))] + [whole(x.shape) for _, x in found],
        [whole(half.shape)] * 2,
        [],
        2 * coupling.size * width,
        2 * coupling.size,
    )(at, local_index, coupling, *[x for _, x in found])


def root_products(at, inverse, pieces, offsets, kinds, n_row, n_front):
    span_rows = inverse.shape[1]
    rows = inverse.shape[0] // n_row
    width = pieces[0].shape[1]
    piece_rows = pieces[0].shape[0]
    count = len(offsets)
    owners = (at[0] + jnp.array([o + n_row for o in offsets], jnp.int32)) % n_row

    def body(at_ref, owner_ref, a_ref, *refs):
        piece_refs, out_refs = refs[:n_front], refs[n_front : n_front + count]
        x_ref, sems = refs[-2], refs[-1]
        step = pl.program_id(0)

        @pl.when(step == 0)
        def _():
            copies = []
            for d in range(n_front):
                start = lax.bitwise_xor(at_ref[1], d) * piece_rows
                place = pl.ds(pl.multiple_of(start, piece_rows), piece_rows)
                copies.append(pltpu.make_async_copy(piece_refs[d], x_ref.at[place], sems.at[d]))
            for copy in copies:
                copy.start()
            for copy in copies:
                copy.wait()

        total = dot(a_ref[...], x_ref[...])
        for i in range(count):

            @pl.when(step == i)
            def _():
                out_refs[i][...] = total.astype(out_refs[i].dtype)

    return kernel_call(
        body,
        [jax.ShapeDtypeStruct((rows, width), kind) for kind in kinds],
        (count,),
        2,
        [pl.BlockSpec((rows, span_rows), lambda i, at_ref, owner_ref: (owner_ref[i], 0))] + [ANY] * n_front,
        [whole((rows, width))] * count,
        [pltpu.VMEM((span_rows, width), BF16), pltpu.SemaphoreType.DMA((n_front,))],
        2 * rows * span_rows * width * count,
        2 * rows * span_rows * count,
    )(at, owners, inverse, *pieces)


def border_backward(at, local_index, coupling, pieces, offsets, kinds, n_row, n_front):
    rows, depth = coupling.shape
    width = pieces[0].shape[1]
    piece_rows = pieces[0].shape[0]
    quarter = piece_rows // n_row
    span_rows = piece_rows * n_front
    columns = depth // n_row
    blocks = rows // BLK
    count = len(offsets)
    owners = (at[0] + jnp.array([o + n_row for o in offsets], jnp.int32)) % n_row

    def body(at_ref, index_ref, owner_ref, a_ref, *refs):
        piece_refs, out_refs = refs[:n_front], refs[n_front : n_front + count]
        span_ref, picked_ref, sems = refs[-3], refs[-2], refs[-1]
        step = pl.program_id(0)

        @pl.when(step == 0)
        def _():
            copies = []
            for d in range(n_front):
                there = lax.bitwise_xor(at_ref[1], d)
                chip, core = lax.shift_right_logical(there, 1), lax.rem(there, 2)
                for k in range(n_row):
                    start = core * (span_rows // 2) + lax.bitwise_xor(chip, k) * piece_rows + k * quarter
                    place = pl.ds(pl.multiple_of(start, quarter), quarter)
                    copies.append(
                        pltpu.make_async_copy(
                            piece_refs[d].at[pl.ds(k * quarter, quarter)],
                            span_ref.at[place],
                            sems.at[d * n_row + k],
                        )
                    )
            for copy in copies:
                copy.start()
            for copy in copies:
                copy.wait()
            for j in range(blocks):
                source = pl.ds(pl.multiple_of(index_ref[j] * BLK, BLK), BLK)
                picked_ref[pl.ds(j * BLK, BLK), :] = span_ref[source, :]

        total = dot(picked_ref[...], a_ref[...], ((0,), (0,)))
        for i in range(count):

            @pl.when(step == i)
            def _():
                out_refs[i][...] = total.astype(out_refs[i].dtype)

    return kernel_call(
        body,
        [jax.ShapeDtypeStruct((width, columns), kind) for kind in kinds],
        (count,),
        3,
        [pl.BlockSpec((rows, columns), lambda i, at_ref, index_ref, owner_ref: (0, owner_ref[i]))]
        + [ANY] * n_front,
        [whole((width, columns))] * count,
        [
            pltpu.VMEM((span_rows, width), BF16),
            pltpu.VMEM((rows, width), BF16),
            pltpu.SemaphoreType.DMA((n_front * n_row,)),
        ],
        2 * rows * columns * width * count,
        2 * rows * columns * count,
    )(at, local_index, owners, coupling, *pieces)


def solve(n_front, n_row, rhs_front, rhs_root, pivot_inverse, border_coupling, root_inverse, border_map):
    row_at = lax.axis_index("row").astype(jnp.int32)
    front_at = lax.axis_index("front").astype(jnp.int32)
    at = jnp.stack([row_at, front_at])
    span_rows = root_inverse.shape[1]
    piece_rows = span_rows // n_front
    local_index = border_map[0] - row_at * (span_rows // BLK)
    first_at, later_at = far_offsets(n_row)

    inner, inner_half = pivot_forward(at, pivot_inverse, gather_row(rhs_front, n_row), n_row)
    send, keep = border_forward(
        at, local_index, border_coupling, gather_row(inner_half, n_row), n_row, n_front, span_rows
    )
    came = swap(send, n_front, 1)

    def pair(i):
        rows = slice(i * piece_rows, (i + 1) * piece_rows)
        return keep[rows].astype(F32) + came[rows].astype(F32)

    shares = pair(0)
    for d in range(2, n_front, 2):
        shares = shares + swap(pair(d // 2).astype(BF16), n_front, d).astype(F32)
    own_rhs = lax.dynamic_slice_in_dim(rhs_root, front_at * piece_rows, piece_rows, 0)
    pieces = gather_front((own_rhs - shares).astype(BF16), n_front)

    def root(offsets, kind):
        outs = root_products(at, root_inverse, pieces, offsets, [kind] * len(offsets), n_row, n_front)
        return dict(zip(offsets, outs))

    first = root(first_at, BF16)
    rest = root(later_at + [0], F32)
    root_solution = scatter_row(first, rest, rest[0], n_row)
    root_half = root_solution.astype(BF16)
    quarter = root_half.shape[0] // n_row
    moved = []
    for k in range(n_row):
        perm = [
            ((chip * 2 + core) * n_row + row, ((row ^ k) * 2 + core) * n_row + chip)
            for chip in range(n_row)
            for core in range(2)
            for row in range(n_row)
        ]
        moved.append(lax.ppermute(root_half[k * quarter : (k + 1) * quarter], ("front", "row"), perm))
    spans = gather_front(jnp.concatenate(moved, axis=0), n_front)

    def border(offsets, kind):
        outs = border_backward(
            at, local_index, border_coupling, spans, offsets, [kind] * len(offsets), n_row, n_front
        )
        return dict(zip(offsets, outs))

    first = border(first_at, BF16)
    rest = border(later_at + [0], F32)
    pulled = scatter_row(first, rest, rest[0], n_row).astype(BF16)
    front_solution = pivot_backward(at, pivot_inverse, gather_row(pulled, n_row), inner, n_row)
    return front_solution, root_solution


def solve_plain(n_front, n_row, rhs_front, rhs_root, pivot_inverse, border_coupling, root_inverse, border_map):
    row_at = lax.axis_index("row")
    front_at = lax.axis_index("front")
    width = rhs_front.shape[1]
    inner = dot(pivot_inverse, lax.all_gather(rhs_front, "row", axis=0, tiled=True))
    contrib = dot(border_coupling, lax.all_gather(inner.astype(BF16), "row", axis=0, tiled=True))
    block_local = border_map.shape[1]
    span_rows = root_inverse.shape[1]
    span_blocks = span_rows // BLK
    local_index = border_map[0] - row_at * span_blocks
    select = (local_index[None, :] == jnp.arange(span_blocks, dtype=jnp.int32)[:, None]).astype(F32)
    dense = jnp.einsum(
        "kj,jcn->kcn", select, contrib.reshape(block_local, BLK, width), precision=lax.Precision.HIGHEST
    ).reshape(span_rows, width)
    shares = lax.psum_scatter(dense, "front", scatter_dimension=0, tiled=True)
    own_rhs = lax.dynamic_slice_in_dim(rhs_root, front_at * shares.shape[0], shares.shape[0], 0)
    schur_rhs = lax.all_gather((own_rhs - shares).astype(BF16), "front", axis=0, tiled=True)
    root_solution = lax.psum_scatter(dot(root_inverse, schur_rhs), "row", scatter_dimension=0, tiled=True)
    gathered = lax.all_gather(root_solution.astype(BF16), ("front", "row"), axis=0, tiled=True)
    ranged = lax.dynamic_slice_in_dim(gathered, row_at * span_rows, span_rows, 0)
    picked = jnp.take(ranged.reshape(span_blocks, BLK, width), local_index, axis=0)
    picked = picked.reshape(block_local * BLK, width)
    pulled = lax.psum_scatter(
        dot(border_coupling, picked, ((0,), (0,))), "row", scatter_dimension=0, tiled=True
    ).astype(BF16)
    correction = dot(pivot_inverse, lax.all_gather(pulled, "row", axis=0, tiled=True))
    return inner - correction, root_solution


def solution(mesh):
    in_specs = (
        P(("front", "row"), None),
        P("row", None),
        P(("front", "row"), None),
        P(("front", "row"), None),
        P("front", "row"),
        P("front", "row"),
    )
    out_specs = (P(("front", "row"), None), P(("front", "row"), None))
    n_front, n_row = mesh.shape["front"], mesh.shape["row"]

    def per_device(*arrays):
        root_inverse, width = arrays[4], arrays[0].shape[1]
        fits = (
            n_front == 2 * n_row
            and n_front & (n_front - 1) == 0
            and n_row > 2
            and root_inverse.shape[1] % (n_front * BLK) == 0
            and root_inverse.shape[0] == n_row * (root_inverse.shape[1] // n_front)
            and root_inverse.shape[1] % (n_front * n_row * 16) == 0
            and arrays[2].shape[1] % (n_row * BLK) == 0
            and width % BLK == 0
        )
        if not fits:
            return solve_plain(n_front, n_row, *arrays)
        cut = width * 2 // 3 // BLK * BLK
        parts = [
            solve(n_front, n_row, arrays[0][:, low:high], arrays[1][:, low:high], *arrays[2:])
            for low, high in ((0, cut), (cut, width))
            if high > low
        ]
        return tuple(jnp.concatenate(outs, axis=1) for outs in zip(*parts))

    return jax.shard_map(per_device, mesh=mesh, in_specs=in_specs, out_specs=out_specs, check_vma=False)
```

```python
import math

import jax
import jax.numpy as jnp
from jax import lax
from jax.experimental import pallas as pl
from jax.experimental.pallas import tpu as pltpu
from jax.sharding import PartitionSpec as P

BLK = 128
F32 = jnp.float32
BF16 = jnp.bfloat16
VMEM = pl.BlockSpec(memory_space=pltpu.VMEM)
ANY = pl.BlockSpec(memory_space=pl.ANY)


def dot(a, b, contract=((1,), (0,))):
    return lax.dot_general(a, b, (contract, ((), ())), preferred_element_type=F32)


def spec_bytes(specs):
    return sum(4 * math.prod(s.block_shape) for s in jax.tree.leaves(specs) if s.block_shape is not None)


def kernel_call(body, out_shape, grid, n_scalars, in_specs, out_specs, scratch, flops, nbytes):
    held = sum(2 * math.prod(s.shape) for s in scratch if s.dtype == BF16)
    limit = spec_bytes(in_specs) + 3 * spec_bytes(out_specs) + held + 4 * 1024 * 1024
    return pl.pallas_call(
        body,
        out_shape=out_shape,
        grid_spec=pltpu.PrefetchScalarGridSpec(
            num_scalar_prefetch=n_scalars,
            grid=grid,
            in_specs=in_specs,
            out_specs=out_specs,
            scratch_shapes=scratch,
        ),
        compiler_params=pltpu.CompilerParams(vmem_limit_bytes=limit),
        cost_estimate=pl.CostEstimate(flops=flops, bytes_accessed=nbytes, transcendentals=0),
    )


def whole(shape):
    return pl.BlockSpec(shape, lambda *_: (0,) * len(shape))


def shift(x, size, by):
    return lax.ppermute(x, "row", [(i, (i + by) % size) for i in range(size)])


def swap(x, size, by):
    return lax.ppermute(x, "front", [(i, i ^ by) for i in range(size)])


def gather_row(x, n):
    found = [(0, x)]
    up, down = x, x
    for step in range(1, n // 2 + 1):
        up = shift(up, n, 1)
        found.append((-step, up))
        if step < n - step:
            down = shift(down, n, -1)
            found.append((step, down))
    return found


def gather_front(x, n):
    found = {0: x, 1: swap(x, n, 1)}
    for d in range(2, n, 2):
        found[d] = swap(x, n, d)
    for d in range(2, n, 2):
        found[d + 1] = swap(found[d], n, 1)
    return [found[d] for d in range(n)]


def far_offsets(n):
    first = [-(n // 2)] + ([(n - 1) // 2] if n > 2 else [])
    later = [o for o in range(-(n // 2) + 1, (n - 1) // 2) if o]
    return first, later


def scatter_row(first, later, own, n):
    total = own
    for sign, far in ((-1, n // 2), (1, (n - 1) // 2)):
        running = None
        for step in range(far, 0, -1):
            if running is None:
                running = first[sign * step]
            else:
                running = (running.astype(F32) + later[sign * step]).astype(BF16)
            running = shift(running, n, sign)
        if running is not None:
            total = total + running.astype(F32)
    return total


def owner(at_ref, offset, n_row):
    return lax.rem(at_ref[0] + (offset + n_row), n_row)


def column_specs(rows, depth, offsets, n_row, moving=False):
    return [
        pl.BlockSpec((rows, depth), lambda i, at_ref, *_, o=o: (i if moving else 0, owner(at_ref, o, n_row)))
        for o in offsets
    ]


def products(a_refs, x_refs, contract):
    total = None
    for a_ref, x_ref in zip(a_refs, x_refs):
        part = dot(a_ref[...], x_ref[...], contract)
        total = part if total is None else total + part
    return total


def pivot_products(at, pivot, found, n_row, contract, finish, outs, extra=()):
    rows, depth = pivot.shape[0], pivot.shape[1] // n_row
    count = len(found)
    width = outs[0].shape[1]

    def body(at_ref, *refs):
        total = products(refs[:count], refs[count : 2 * count], contract)
        extras = refs[2 * count : 2 * count + len(extra)]
        for ref, value in zip(refs[2 * count + len(extra) :], finish(total, *[e[...] for e in extras])):
            ref[...] = value

    return kernel_call(
        body,
        outs,
        (1,),
        1,
        column_specs(rows, depth, [o for o, _ in found], n_row)
        + [whole(x.shape) for _, x in found]
        + [whole(e.shape) for e in extra],
        [whole(o.shape) for o in outs],
        [],
        2 * rows * depth * width * count,
        2 * rows * depth * count,
    )(at, *[pivot] * count, *[x for _, x in found], *extra)


def border_partial(at, coupling, found, n_row):
    rows, depth = coupling.shape[0], coupling.shape[1] // n_row
    count, width = len(found), found[0][1].shape[1]
    tile = rows // border_steps(rows)

    def body(at_ref, *refs):
        refs[-1][...] = products(refs[:count], refs[count : 2 * count], ((1,), (0,)))

    return kernel_call(
        body,
        jax.ShapeDtypeStruct((rows, width), F32),
        (rows // tile,),
        1,
        column_specs(tile, depth, [o for o, _ in found], n_row, True) + [whole(x.shape) for _, x in found],
        pl.BlockSpec((tile, width), lambda i, *_: (i, 0)),
        [],
        2 * rows * depth * width * count,
        2 * rows * depth * count,
    )(at, *[coupling] * count, *[x for _, x in found])


def border_steps(rows):
    blocks = rows // BLK
    return blocks // next(k for k in (4, 3, 2, 1) if blocks % k == 0)


def border_scatter(at, local_index, coupling, found, partial, n_row, n_front, span_rows):
    rows, depth = coupling.shape[0], coupling.shape[1] // n_row
    count, width = len(found), found[0][1].shape[1]
    tile = rows // border_steps(rows)
    piece_blocks = span_rows // n_front // BLK

    def body(at_ref, index_ref, *refs):
        partial_ref, send_ref, keep_ref = refs[-3], refs[-2], refs[-1]
        step = pl.program_id(0)

        @pl.when(step == 0)
        def _():
            send_ref[...] = jnp.zeros_like(send_ref)
            keep_ref[...] = jnp.zeros_like(keep_ref)

        total = products(refs[:count], refs[count : 2 * count], ((1,), (0,)))
        total = (partial_ref[...] + total).astype(BF16)
        for j in range(tile // BLK):
            target = index_ref[step * (tile // BLK) + j]
            there = lax.div(target, piece_blocks)
            slot = lax.shift_right_logical(there, 1) * piece_blocks + lax.rem(target, piece_blocks)
            place = pl.ds(pl.multiple_of(slot * BLK, BLK), BLK)
            block = total[j * BLK : (j + 1) * BLK]
            away = lax.rem(there + at_ref[1], 2)

            @pl.when(away == 1)
            def _():
                send_ref[place, :] = block

            @pl.when(away == 0)
            def _():
                keep_ref[place, :] = block

    half = jax.ShapeDtypeStruct((span_rows // 2, width), BF16)
    return kernel_call(
        body,
        [half, half],
        (rows // tile,),
        2,
        column_specs(tile, depth, [o for o, _ in found], n_row, True)
        + [whole(x.shape) for _, x in found]
        + [pl.BlockSpec((tile, width), lambda i, *_: (i, 0))],
        [whole(half.shape)] * 2,
        [],
        2 * rows * depth * width * count,
        2 * rows * depth * count,
    )(at, local_index, *[coupling] * count, *[x for _, x in found], partial)


def root_products(at, inverse, pieces, offsets, kinds, n_row, n_front):
    span_rows = inverse.shape[1]
    rows = inverse.shape[0] // n_row
    piece_rows, width = pieces[0].shape
    count = len(offsets)

    def row_block(i, at_ref):
        offset = offsets[0]
        for k in range(1, count):
            offset = jnp.where(i == k, offsets[k], offset)
        return owner(at_ref, offset, n_row), 0

    def body(at_ref, a_ref, *refs):
        piece_refs, out_refs = refs[:n_front], refs[n_front : n_front + count]
        x_ref, sems = refs[-2], refs[-1]
        step = pl.program_id(0)

        @pl.when(step == 0)
        def _():
            copies = []
            for d in range(n_front):
                start = lax.bitwise_xor(at_ref[1], d) * piece_rows
                place = pl.ds(pl.multiple_of(start, piece_rows), piece_rows)
                copies.append(pltpu.make_async_copy(piece_refs[d], x_ref.at[place], sems.at[d]))
            for copy in copies:
                copy.start()
            for copy in copies:
                copy.wait()

        total = dot(a_ref[...], x_ref[...])
        for i in range(count):

            @pl.when(step == i)
            def _():
                out_refs[i][...] = total.astype(out_refs[i].dtype)

    return kernel_call(
        body,
        [jax.ShapeDtypeStruct((rows, width), kind) for kind in kinds],
        (count,),
        1,
        [pl.BlockSpec((rows, span_rows), row_block)] + [ANY] * n_front,
        [whole((rows, width))] * count,
        [pltpu.VMEM((span_rows, width), BF16), pltpu.SemaphoreType.DMA((n_front,))],
        2 * rows * span_rows * width * count,
        2 * rows * span_rows * count,
    )(at, inverse, *pieces)


def border_pick(at, local_index, coupling, pieces, offset, n_row, n_front):
    rows, depth = coupling.shape[0], coupling.shape[1] // n_row
    piece_rows, width = pieces[0].shape
    quarter = piece_rows // n_row
    span_rows = piece_rows * n_front

    def body(at_ref, index_ref, a_ref, *refs):
        piece_refs, out_ref, picked_ref = refs[:n_front], refs[n_front], refs[n_front + 1]
        span_ref, sems = refs[-2], refs[-1]
        copies = []
        for d in range(n_front):
            there = lax.bitwise_xor(at_ref[1], d)
            chip, core = lax.shift_right_logical(there, 1), lax.rem(there, 2)
            for k in range(n_row):
                start = core * (span_rows // 2) + k * piece_rows + chip * quarter
                place = pl.ds(pl.multiple_of(start, quarter), quarter)
                copies.append(
                    pltpu.make_async_copy(
                        piece_refs[d].at[pl.ds(k * quarter, quarter)], span_ref.at[place], sems.at[d * n_row + k]
                    )
                )
        for copy in copies:
            copy.start()
        for copy in copies:
            copy.wait()
        for j in range(rows // BLK):
            source = pl.ds(pl.multiple_of(index_ref[j] * BLK, BLK), BLK)
            picked_ref[:, pl.ds(j * BLK, BLK)] = jnp.transpose(span_ref[source, :])
        out_ref[...] = dot(picked_ref[...], a_ref[...]).astype(BF16)

    return kernel_call(
        body,
        [jax.ShapeDtypeStruct((width, depth), BF16), jax.ShapeDtypeStruct((width, rows), BF16)],
        (1,),
        2,
        column_specs(rows, depth, [offset], n_row) + [ANY] * n_front,
        [whole((width, depth)), whole((width, rows))],
        [pltpu.VMEM((span_rows, width), BF16), pltpu.SemaphoreType.DMA((n_front * n_row,))],
        2 * rows * depth * width,
        2 * rows * depth,
    )(at, local_index, coupling, *pieces)


def border_backward(at, coupling, picked, offsets, kinds, n_row):
    rows, depth = coupling.shape[0], coupling.shape[1] // n_row
    width, count = picked.shape[0], len(offsets)

    def body(at_ref, x_ref, *refs):
        for a_ref, out_ref in zip(refs[:count], refs[count:]):
            out_ref[...] = dot(x_ref[...], a_ref[...]).astype(out_ref.dtype)

    return kernel_call(
        body,
        [jax.ShapeDtypeStruct((width, depth), kind) for kind in kinds],
        (1,),
        1,
        [whole(picked.shape)] + column_specs(rows, depth, offsets, n_row),
        [whole((width, depth))] * count,
        [],
        2 * rows * depth * width * count,
        2 * rows * depth * count,
    )(at, picked, *[coupling] * count)


def solve(n_front, n_row, rhs_front, rhs_root, pivot_inverse, border_coupling, root_inverse, border_map):
    row_at = lax.axis_index("row").astype(jnp.int32)
    front_at = lax.axis_index("front").astype(jnp.int32)
    at = jnp.stack([row_at, front_at])
    span_rows = root_inverse.shape[1]
    piece_rows, width = span_rows // n_front, rhs_front.shape[1]
    local_index = border_map[0] - row_at * (span_rows // BLK)
    first_at, later_at = far_offsets(n_row)
    chips = [[2 * chip + core for chip in range(n_front // 2)] for core in range(2)]
    block = jax.ShapeDtypeStruct((pivot_inverse.shape[0], width), F32)
    half = jax.ShapeDtypeStruct(block.shape, BF16)
    straight, across = ((1,), (0,)), ((1,), (1,))

    found = gather_row(rhs_front, n_row)
    early, last = found[:-1], found[-1:]
    partial = pivot_products(at, pivot_inverse, early, n_row, straight, lambda t: [t], [block])
    inner, inner_half = pivot_products(
        at,
        pivot_inverse,
        last,
        n_row,
        straight,
        lambda t, p: [t + p, (t + p).astype(BF16)],
        [block, half],
        partial,
    )
    found = gather_row(inner_half, n_row)
    early, last = found[:-1], found[-1:]
    partial = border_partial(at, border_coupling, early, n_row)
    send, keep = border_scatter(
        at, local_index, border_coupling, last, partial, n_row, n_front, span_rows
    )
    both = (keep.astype(F32) + swap(send, n_front, 1).astype(F32)).astype(BF16)
    shares = lax.all_to_all(
        both.reshape(n_front // 2, piece_rows, width), "front", 0, 0, axis_index_groups=chips
    )
    own_rhs = lax.dynamic_slice_in_dim(rhs_root, front_at * piece_rows, piece_rows, 0)
    pieces = gather_front((own_rhs - shares.astype(F32).sum(axis=0)).astype(BF16), n_front)

    def root(offsets, kind):
        outs = root_products(at, root_inverse, pieces, offsets, [kind] * len(offsets), n_row, n_front)
        return dict(zip(offsets, outs))

    first = {}
    for offset in first_at:
        first.update(root([offset], BF16))
    rest = root(later_at + [0], F32)
    root_solution = scatter_row(first, rest, rest[0], n_row)
    quarters = root_solution.astype(BF16).reshape(n_row, piece_rows // n_row, width)
    quarters = lax.all_to_all(quarters, "front", 0, 0, axis_index_groups=chips)
    quarters = lax.all_to_all(quarters, "row", 0, 0)
    spans = gather_front(quarters.reshape(piece_rows, width), n_front)

    out, picked = border_pick(at, local_index, border_coupling, spans, first_at[0], n_row, n_front)
    first = {first_at[0]: out}
    for offset in first_at[1:]:
        first[offset] = border_backward(at, border_coupling, picked, [offset], [BF16], n_row)[0]
    offsets = later_at + [0]
    rest = dict(zip(offsets, border_backward(at, border_coupling, picked, offsets, [F32] * len(offsets), n_row)))
    pulled = scatter_row(first, rest, rest[0], n_row).astype(BF16)
    found = gather_row(pulled, n_row)
    early, last = found[:-1], found[-1:]
    partial = pivot_products(
        at, pivot_inverse, early, n_row, across, lambda t, i: [i - t], [block], [inner]
    )
    front_solution = pivot_products(
        at, pivot_inverse, last, n_row, across, lambda t, p: [p - t], [block], partial
    )
    return front_solution[0], root_solution


def solve_plain(n_front, n_row, rhs_front, rhs_root, pivot_inverse, border_coupling, root_inverse, border_map):
    row_at = lax.axis_index("row")
    front_at = lax.axis_index("front")
    width = rhs_front.shape[1]
    inner = dot(pivot_inverse, lax.all_gather(rhs_front, "row", axis=0, tiled=True))
    contrib = dot(border_coupling, lax.all_gather(inner.astype(BF16), "row", axis=0, tiled=True))
    block_local = border_map.shape[1]
    span_rows = root_inverse.shape[1]
    span_blocks = span_rows // BLK
    local_index = border_map[0] - row_at * span_blocks
    select = (local_index[None, :] == jnp.arange(span_blocks, dtype=jnp.int32)[:, None]).astype(F32)
    dense = jnp.einsum(
        "kj,jcn->kcn", select, contrib.reshape(block_local, BLK, width), precision=lax.Precision.HIGHEST
    ).reshape(span_rows, width)
    shares = lax.psum_scatter(dense, "front", scatter_dimension=0, tiled=True)
    own_rhs = lax.dynamic_slice_in_dim(rhs_root, front_at * shares.shape[0], shares.shape[0], 0)
    schur_rhs = lax.all_gather((own_rhs - shares).astype(BF16), "front", axis=0, tiled=True)
    root_solution = lax.psum_scatter(dot(root_inverse, schur_rhs), "row", scatter_dimension=0, tiled=True)
    gathered = lax.all_gather(root_solution.astype(BF16), ("front", "row"), axis=0, tiled=True)
    ranged = lax.dynamic_slice_in_dim(gathered, row_at * span_rows, span_rows, 0)
    picked = jnp.take(ranged.reshape(span_blocks, BLK, width), local_index, axis=0)
    picked = picked.reshape(block_local * BLK, width)
    pulled = lax.psum_scatter(
        dot(border_coupling, picked, ((0,), (0,))), "row", scatter_dimension=0, tiled=True
    ).astype(BF16)
    correction = dot(pivot_inverse, lax.all_gather(pulled, "row", axis=0, tiled=True))
    return inner - correction, root_solution


def solution(mesh):
    in_specs = (
        P(("front", "row"), None),
        P("row", None),
        P(("front", "row"), None),
        P(("front", "row"), None),
        P("front", "row"),
        P("front", "row"),
    )
    out_specs = (P(("front", "row"), None), P(("front", "row"), None))
    n_front, n_row = mesh.shape["front"], mesh.shape["row"]

    def per_device(*arrays):
        root_inverse, width = arrays[4], arrays[0].shape[1]
        fits = (
            n_front == 2 * n_row
            and n_front & (n_front - 1) == 0
            and n_row > 2
            and root_inverse.shape[1] % (n_front * BLK) == 0
            and root_inverse.shape[0] == n_row * (root_inverse.shape[1] // n_front)
            and root_inverse.shape[1] % (n_front * n_row * 16) == 0
            and arrays[2].shape[1] % (n_row * BLK) == 0
            and width % BLK == 0
        )
        return (solve if fits else solve_plain)(n_front, n_row, *arrays)

    return jax.shard_map(per_device, mesh=mesh, in_specs=in_specs, out_specs=out_specs, check_vma=False)
```

```python
import math

import jax
import jax.numpy as jnp
from jax import lax
from jax.experimental import pallas as pl
from jax.experimental.pallas import tpu as pltpu
from jax.sharding import PartitionSpec as P

BLK = 128
F32 = jnp.float32
BF16 = jnp.bfloat16
VMEM = pl.BlockSpec(memory_space=pltpu.VMEM)
ANY = pl.BlockSpec(memory_space=pl.ANY)


def dot(a, b, contract=((1,), (0,))):
    return lax.dot_general(a, b, (contract, ((), ())), preferred_element_type=F32)


def spec_bytes(specs):
    return sum(4 * math.prod(s.block_shape) for s in jax.tree.leaves(specs) if s.block_shape is not None)


def kernel_call(body, out_shape, grid, n_scalars, in_specs, out_specs, scratch, flops, nbytes):
    held = sum(2 * math.prod(s.shape) for s in scratch if s.dtype == BF16)
    limit = spec_bytes(in_specs) + 3 * spec_bytes(out_specs) + held + 4 * 1024 * 1024
    return pl.pallas_call(
        body,
        out_shape=out_shape,
        grid_spec=pltpu.PrefetchScalarGridSpec(
            num_scalar_prefetch=n_scalars,
            grid=grid,
            in_specs=in_specs,
            out_specs=out_specs,
            scratch_shapes=scratch,
        ),
        compiler_params=pltpu.CompilerParams(vmem_limit_bytes=limit),
        cost_estimate=pl.CostEstimate(flops=flops, bytes_accessed=nbytes, transcendentals=0),
    )


def whole(shape):
    return pl.BlockSpec(shape, lambda *_: (0,) * len(shape))


def shift(x, size, by):
    return lax.ppermute(x, "row", [(i, (i + by) % size) for i in range(size)])


def swap(x, size, by):
    return lax.ppermute(x, "front", [(i, i ^ by) for i in range(size)])


def gather_row(x, n):
    found = [(0, x)]
    up, down = x, x
    for step in range(1, n // 2 + 1):
        up = shift(up, n, 1)
        found.append((-step, up))
        if step < n - step:
            down = shift(down, n, -1)
            found.append((step, down))
    return found


def gather_front(x, n):
    found = {0: x, 1: swap(x, n, 1)}
    for d in range(2, n, 2):
        found[d] = swap(x, n, d)
    for d in range(2, n, 2):
        found[d + 1] = swap(found[d], n, 1)
    return [found[d] for d in range(n)]


def far_offsets(n):
    first = [-(n // 2)] + ([(n - 1) // 2] if n > 2 else [])
    later = [o for o in range(-(n // 2) + 1, (n - 1) // 2) if o]
    return first, later


def scatter_row(first, later, own, n):
    total = own
    for sign, far in ((-1, n // 2), (1, (n - 1) // 2)):
        running = None
        for step in range(far, 0, -1):
            if running is None:
                running = first[sign * step]
            else:
                running = (running.astype(F32) + later[sign * step]).astype(BF16)
            running = shift(running, n, sign)
        if running is not None:
            total = total + running.astype(F32)
    return total


def owner(at_ref, offset, n_row):
    return lax.rem(at_ref[0] + (offset + n_row), n_row)


def column_specs(rows, depth, offsets, n_row, moving=False):
    return [
        pl.BlockSpec((rows, depth), lambda i, at_ref, *_, o=o: (i if moving else 0, owner(at_ref, o, n_row)))
        for o in offsets
    ]


def products(a_refs, x_refs, contract):
    total = None
    for a_ref, x_ref in zip(a_refs, x_refs):
        part = dot(a_ref[...], x_ref[...], contract)
        total = part if total is None else total + part
    return total


def pivot_products(at, pivot, found, n_row, contract, finish, outs, extra=()):
    rows, depth = pivot.shape[0], pivot.shape[1] // n_row
    count = len(found)
    width = outs[0].shape[1]

    def body(at_ref, *refs):
        total = products(refs[:count], refs[count : 2 * count], contract)
        extras = refs[2 * count : 2 * count + len(extra)]
        for ref, value in zip(refs[2 * count + len(extra) :], finish(total, *[e[...] for e in extras])):
            ref[...] = value

    return kernel_call(
        body,
        outs,
        (1,),
        1,
        column_specs(rows, depth, [o for o, _ in found], n_row)
        + [whole(x.shape) for _, x in found]
        + [whole(e.shape) for e in extra],
        [whole(o.shape) for o in outs],
        [],
        2 * rows * depth * width * count,
        2 * rows * depth * count,
    )(at, *[pivot] * count, *[x for _, x in found], *extra)


def border_partial(at, coupling, found, n_row):
    rows, depth = coupling.shape[0], coupling.shape[1] // n_row
    count, width = len(found), found[0][1].shape[1]
    tile = rows // border_steps(rows)

    def body(at_ref, *refs):
        refs[-1][...] = products(refs[:count], refs[count : 2 * count], ((1,), (0,)))

    return kernel_call(
        body,
        jax.ShapeDtypeStruct((rows, width), F32),
        (rows // tile,),
        1,
        column_specs(tile, depth, [o for o, _ in found], n_row, True) + [whole(x.shape) for _, x in found],
        pl.BlockSpec((tile, width), lambda i, *_: (i, 0)),
        [],
        2 * rows * depth * width * count,
        2 * rows * depth * count,
    )(at, *[coupling] * count, *[x for _, x in found])


def border_steps(rows):
    blocks = rows // BLK
    return blocks // next(k for k in (4, 3, 2, 1) if blocks % k == 0)


def border_scatter(at, local_index, coupling, found, partial, n_row, n_front, span_rows):
    rows, depth = coupling.shape[0], coupling.shape[1] // n_row
    count, width = len(found), found[0][1].shape[1]
    tile = rows // border_steps(rows)
    piece_blocks = span_rows // n_front // BLK

    def body(at_ref, index_ref, *refs):
        partial_ref, send_ref, keep_ref = refs[-3], refs[-2], refs[-1]
        step = pl.program_id(0)

        @pl.when(step == 0)
        def _():
            send_ref[...] = jnp.zeros_like(send_ref)
            keep_ref[...] = jnp.zeros_like(keep_ref)

        total = products(refs[:count], refs[count : 2 * count], ((1,), (0,)))
        total = (partial_ref[...] + total).astype(BF16)
        for j in range(tile // BLK):
            target = index_ref[step * (tile // BLK) + j]
            there = lax.div(target, piece_blocks)
            slot = lax.shift_right_logical(there, 1) * piece_blocks + lax.rem(target, piece_blocks)
            place = pl.ds(pl.multiple_of(slot * BLK, BLK), BLK)
            block = total[j * BLK : (j + 1) * BLK]
            away = lax.rem(there + at_ref[1], 2)

            @pl.when(away == 1)
            def _():
                send_ref[place, :] = block

            @pl.when(away == 0)
            def _():
                keep_ref[place, :] = block

    half = jax.ShapeDtypeStruct((span_rows // 2, width), BF16)
    return kernel_call(
        body,
        [half, half],
        (rows // tile,),
        2,
        column_specs(tile, depth, [o for o, _ in found], n_row, True)
        + [whole(x.shape) for _, x in found]
        + [pl.BlockSpec((tile, width), lambda i, *_: (i, 0))],
        [whole(half.shape)] * 2,
        [],
        2 * rows * depth * width * count,
        2 * rows * depth * count,
    )(at, local_index, *[coupling] * count, *[x for _, x in found], partial)


def root_products(at, inverse, pieces, offsets, kinds, n_row, n_front):
    span_rows = inverse.shape[1]
    rows = inverse.shape[0] // n_row
    piece_rows, width = pieces[0].shape
    count = len(offsets)

    def row_block(i, at_ref):
        offset = offsets[0]
        for k in range(1, count):
            offset = jnp.where(i == k, offsets[k], offset)
        return owner(at_ref, offset, n_row), 0

    def body(at_ref, a_ref, *refs):
        piece_refs, out_refs = refs[:n_front], refs[n_front : n_front + count]
        x_ref, sems = refs[-2], refs[-1]
        step = pl.program_id(0)

        @pl.when(step == 0)
        def _():
            copies = []
            for d in range(n_front):
                start = lax.bitwise_xor(at_ref[1], d) * piece_rows
                place = pl.ds(pl.multiple_of(start, piece_rows), piece_rows)
                copies.append(pltpu.make_async_copy(piece_refs[d], x_ref.at[place], sems.at[d]))
            for copy in copies:
                copy.start()
            for copy in copies:
                copy.wait()

        total = dot(a_ref[...], x_ref[...])
        for i in range(count):

            @pl.when(step == i)
            def _():
                out_refs[i][...] = total.astype(out_refs[i].dtype)

    return kernel_call(
        body,
        [jax.ShapeDtypeStruct((rows, width), kind) for kind in kinds],
        (count,),
        1,
        [pl.BlockSpec((rows, span_rows), row_block)] + [ANY] * n_front,
        [whole((rows, width))] * count,
        [pltpu.VMEM((span_rows, width), BF16), pltpu.SemaphoreType.DMA((n_front,))],
        2 * rows * span_rows * width * count,
        2 * rows * span_rows * count,
    )(at, inverse, *pieces)


def border_pick(at, local_index, coupling, pieces, offset, n_row, n_front):
    rows, depth = coupling.shape[0], coupling.shape[1] // n_row
    piece_rows, width = pieces[0].shape
    quarter = piece_rows // n_row
    span_rows = piece_rows * n_front

    def body(at_ref, index_ref, a_ref, *refs):
        piece_refs, out_ref, picked_ref = refs[:n_front], refs[n_front], refs[n_front + 1]
        span_ref, sems = refs[-2], refs[-1]
        copies = []
        for d in range(n_front):
            there = lax.bitwise_xor(at_ref[1], d)
            chip, core = lax.shift_right_logical(there, 1), lax.rem(there, 2)
            for k in range(n_row):
                start = core * (span_rows // 2) + k * piece_rows + chip * quarter
                place = pl.ds(pl.multiple_of(start, quarter), quarter)
                copies.append(
                    pltpu.make_async_copy(
                        piece_refs[d].at[pl.ds(k * quarter, quarter)], span_ref.at[place], sems.at[d * n_row + k]
                    )
                )
        for copy in copies:
            copy.start()
        for copy in copies:
            copy.wait()
        for j in range(rows // BLK):
            source = pl.ds(pl.multiple_of(index_ref[j] * BLK, BLK), BLK)
            picked_ref[:, pl.ds(j * BLK, BLK)] = jnp.transpose(span_ref[source, :])
        out_ref[...] = dot(picked_ref[...], a_ref[...]).astype(BF16)

    return kernel_call(
        body,
        [jax.ShapeDtypeStruct((width, depth), BF16), jax.ShapeDtypeStruct((width, rows), BF16)],
        (1,),
        2,
        column_specs(rows, depth, [offset], n_row) + [ANY] * n_front,
        [whole((width, depth)), whole((width, rows))],
        [pltpu.VMEM((span_rows, width), BF16), pltpu.SemaphoreType.DMA((n_front * n_row,))],
        2 * rows * depth * width,
        2 * rows * depth,
    )(at, local_index, coupling, *pieces)


def border_backward(at, coupling, picked, offsets, kinds, n_row):
    rows, depth = coupling.shape[0], coupling.shape[1] // n_row
    width, count = picked.shape[0], len(offsets)

    def body(at_ref, x_ref, *refs):
        for a_ref, out_ref in zip(refs[:count], refs[count:]):
            out_ref[...] = dot(x_ref[...], a_ref[...]).astype(out_ref.dtype)

    return kernel_call(
        body,
        [jax.ShapeDtypeStruct((width, depth), kind) for kind in kinds],
        (1,),
        1,
        [whole(picked.shape)] + column_specs(rows, depth, offsets, n_row),
        [whole((width, depth))] * count,
        [],
        2 * rows * depth * width * count,
        2 * rows * depth * count,
    )(at, picked, *[coupling] * count)


def solve(n_front, n_row, rhs_front, rhs_root, pivot_inverse, border_coupling, root_inverse, border_map):
    row_at = lax.axis_index("row").astype(jnp.int32)
    front_at = lax.axis_index("front").astype(jnp.int32)
    at = jnp.stack([row_at, front_at])
    span_rows = root_inverse.shape[1]
    piece_rows, width = span_rows // n_front, rhs_front.shape[1]
    local_index = border_map[0] - row_at * (span_rows // BLK)
    first_at, later_at = far_offsets(n_row)
    chips = [[2 * chip + core for chip in range(n_front // 2)] for core in range(2)]
    block = jax.ShapeDtypeStruct((pivot_inverse.shape[0], width), F32)
    half = jax.ShapeDtypeStruct(block.shape, BF16)
    straight, across = ((1,), (0,)), ((1,), (1,))

    found = gather_row(rhs_front, n_row)
    early, last = found[:-1], found[-1:]
    partial = pivot_products(at, pivot_inverse, early, n_row, straight, lambda t: [t], [block])
    inner, inner_half = pivot_products(
        at,
        pivot_inverse,
        last,
        n_row,
        straight,
        lambda t, p: [t + p, (t + p).astype(BF16)],
        [block, half],
        partial,
    )
    found = gather_row(inner_half, n_row)
    early, last = found[:-1], found[-1:]
    partial = border_partial(at, border_coupling, early, n_row)
    send, keep = border_scatter(
        at, local_index, border_coupling, last, partial, n_row, n_front, span_rows
    )
    both = (keep.astype(F32) + swap(send, n_front, 1).astype(F32)).astype(BF16)
    shares = lax.all_to_all(
        both.reshape(n_front // 2, piece_rows, width), "front", 0, 0, axis_index_groups=chips
    )
    own_rhs = lax.dynamic_slice_in_dim(rhs_root, front_at * piece_rows, piece_rows, 0)
    pieces = gather_front((own_rhs - shares.astype(F32).sum(axis=0)).astype(BF16), n_front)

    def root(offsets, kind):
        outs = root_products(at, root_inverse, pieces, offsets, [kind] * len(offsets), n_row, n_front)
        return dict(zip(offsets, outs))

    first = {}
    for offset in first_at:
        first.update(root([offset], BF16))
    rest = root(later_at + [0], F32)
    root_solution = scatter_row(first, rest, rest[0], n_row)
    quarters = root_solution.astype(BF16).reshape(n_row, piece_rows // n_row, width)
    quarters = lax.all_to_all(quarters, "front", 0, 0, axis_index_groups=chips)
    quarters = lax.all_to_all(quarters, "row", 0, 0)
    spans = gather_front(quarters.reshape(piece_rows, width), n_front)

    out, picked = border_pick(at, local_index, border_coupling, spans, first_at[0], n_row, n_front)
    first = {first_at[0]: out}
    for offset in first_at[1:]:
        first[offset] = border_backward(at, border_coupling, picked, [offset], [BF16], n_row)[0]
    offsets = later_at + [0]
    rest = dict(zip(offsets, border_backward(at, border_coupling, picked, offsets, [F32] * len(offsets), n_row)))
    pulled = scatter_row(first, rest, rest[0], n_row).astype(BF16)
    found = gather_row(pulled, n_row)
    early, last = found[:-1], found[-1:]
    partial = pivot_products(
        at, pivot_inverse, early, n_row, across, lambda t, i: [i - t], [block], [inner]
    )
    front_solution = pivot_products(
        at, pivot_inverse, last, n_row, across, lambda t, p: [p - t], [block], partial
    )
    return front_solution[0], root_solution


def solve_plain(n_front, n_row, rhs_front, rhs_root, pivot_inverse, border_coupling, root_inverse, border_map):
    row_at = lax.axis_index("row")
    front_at = lax.axis_index("front")
    width = rhs_front.shape[1]
    inner = dot(pivot_inverse, lax.all_gather(rhs_front, "row", axis=0, tiled=True))
    contrib = dot(border_coupling, lax.all_gather(inner.astype(BF16), "row", axis=0, tiled=True))
    block_local = border_map.shape[1]
    span_rows = root_inverse.shape[1]
    span_blocks = span_rows // BLK
    local_index = border_map[0] - row_at * span_blocks
    select = (local_index[None, :] == jnp.arange(span_blocks, dtype=jnp.int32)[:, None]).astype(F32)
    dense = jnp.einsum(
        "kj,jcn->kcn", select, contrib.reshape(block_local, BLK, width), precision=lax.Precision.HIGHEST
    ).reshape(span_rows, width)
    shares = lax.psum_scatter(dense, "front", scatter_dimension=0, tiled=True)
    own_rhs = lax.dynamic_slice_in_dim(rhs_root, front_at * shares.shape[0], shares.shape[0], 0)
    schur_rhs = lax.all_gather((own_rhs - shares).astype(BF16), "front", axis=0, tiled=True)
    root_solution = lax.psum_scatter(dot(root_inverse, schur_rhs), "row", scatter_dimension=0, tiled=True)
    gathered = lax.all_gather(root_solution.astype(BF16), ("front", "row"), axis=0, tiled=True)
    ranged = lax.dynamic_slice_in_dim(gathered, row_at * span_rows, span_rows, 0)
    picked = jnp.take(ranged.reshape(span_blocks, BLK, width), local_index, axis=0)
    picked = picked.reshape(block_local * BLK, width)
    pulled = lax.psum_scatter(
        dot(border_coupling, picked, ((0,), (0,))), "row", scatter_dimension=0, tiled=True
    ).astype(BF16)
    correction = dot(pivot_inverse, lax.all_gather(pulled, "row", axis=0, tiled=True))
    return inner - correction, root_solution


def solution(mesh):
    in_specs = (
        P(("front", "row"), None),
        P("row", None),
        P(("front", "row"), None),
        P(("front", "row"), None),
        P("front", "row"),
        P("front", "row"),
    )
    out_specs = (P(("front", "row"), None), P(("front", "row"), None))
    n_front, n_row = mesh.shape["front"], mesh.shape["row"]

    def per_device(*arrays):
        root_inverse, width = arrays[4], arrays[0].shape[1]
        fits = (
            n_front == 2 * n_row
            and n_front & (n_front - 1) == 0
            and n_row > 2
            and root_inverse.shape[1] % (n_front * BLK) == 0
            and root_inverse.shape[0] == n_row * (root_inverse.shape[1] // n_front)
            and root_inverse.shape[1] % (n_front * n_row * 16) == 0
            and arrays[2].shape[1] % (n_row * BLK) == 0
            and width % BLK == 0
        )
        if not fits:
            return solve_plain(n_front, n_row, *arrays)
        cut = width * 2 // 3 // BLK * BLK
        parts = [
            solve(n_front, n_row, arrays[0][:, low:high], arrays[1][:, low:high], *arrays[2:])
            for low, high in ((0, cut), (cut, width))
            if high > low
        ]
        return tuple(jnp.concatenate(outs, axis=1) for outs in zip(*parts))

    return jax.shard_map(per_device, mesh=mesh, in_specs=in_specs, out_specs=out_specs, check_vma=False)
```

```python
import math

import jax
import jax.numpy as jnp
from jax import lax
from jax.experimental import pallas as pl
from jax.experimental.pallas import tpu as pltpu
from jax.sharding import PartitionSpec as P

BLK = 128
F32 = jnp.float32
BF16 = jnp.bfloat16
VMEM = pl.BlockSpec(memory_space=pltpu.VMEM)
ANY = pl.BlockSpec(memory_space=pl.ANY)


def dot(a, b, contract=((1,), (0,))):
    return lax.dot_general(a, b, (contract, ((), ())), preferred_element_type=F32)


def spec_bytes(specs):
    return sum(4 * math.prod(s.block_shape) for s in jax.tree.leaves(specs) if s.block_shape is not None)


def kernel_call(body, out_shape, grid, n_scalars, in_specs, out_specs, scratch, flops, nbytes):
    held = sum(2 * math.prod(s.shape) for s in scratch if s.dtype == BF16)
    limit = spec_bytes(in_specs) + 3 * spec_bytes(out_specs) + held + 4 * 1024 * 1024
    return pl.pallas_call(
        body,
        out_shape=out_shape,
        grid_spec=pltpu.PrefetchScalarGridSpec(
            num_scalar_prefetch=n_scalars,
            grid=grid,
            in_specs=in_specs,
            out_specs=out_specs,
            scratch_shapes=scratch,
        ),
        compiler_params=pltpu.CompilerParams(vmem_limit_bytes=limit),
        cost_estimate=pl.CostEstimate(flops=flops, bytes_accessed=nbytes, transcendentals=0),
    )


def in_hbm(x):
    return pltpu.with_memory_space_constraint(x, pltpu.HBM)


def whole(shape):
    return pl.BlockSpec(shape, lambda *_: (0,) * len(shape))


def shift(x, size, by):
    return lax.ppermute(x, "row", [(i, (i + by) % size) for i in range(size)])


def swap(x, size, by):
    return lax.ppermute(x, "front", [(i, i ^ by) for i in range(size)])


def gather_row(x, n):
    found = [(0, x)]
    up, down = x, x
    for step in range(1, n // 2 + 1):
        up = shift(up, n, 1)
        found.append((-step, up))
        if step < n - step:
            down = shift(down, n, -1)
            found.append((step, down))
    return found


def gather_front(x, n):
    rows = x.shape[0]
    by_x, by_y = swap(x, n, 2), swap(x, n, 4)
    corner_low = swap(by_y[: rows // 2], n, 2)
    corner_high = swap(by_x[rows // 2 :], n, 4)
    mine = [(0, 0, x), (1, 0, by_x), (2, 0, by_y), (3, 0, corner_low), (3, rows // 2, corner_high)]
    found = [(chip, 0, low, block) for chip, low, block in mine]
    return found + [(chip, 1, low, swap(block, n, 1)) for chip, low, block in mine]


def far_offsets(n):
    first = [-(n // 2)] + ([(n - 1) // 2] if n > 2 else [])
    later = [o for o in range(-(n // 2) + 1, (n - 1) // 2) if o]
    return first, later


def scatter_row(first, later, own, n):
    total = own
    for sign, far in ((-1, n // 2), (1, (n - 1) // 2)):
        running = None
        for step in range(far, 0, -1):
            if running is None:
                running = first[sign * step]
            else:
                running = (running.astype(F32) + later[sign * step]).astype(BF16)
            running = shift(running, n, sign)
        if running is not None:
            total = total + running.astype(F32)
    return total


def owner(at_ref, offset, n_row):
    return lax.rem(at_ref[0] + (offset + n_row), n_row)


def column_specs(rows, depth, offsets, n_row, moving=False):
    return [
        pl.BlockSpec((rows, depth), lambda i, at_ref, *_, o=o: (i if moving else 0, owner(at_ref, o, n_row)))
        for o in offsets
    ]


def products(a_refs, x_refs, contract):
    total = None
    for a_ref, x_ref in zip(a_refs, x_refs):
        part = dot(a_ref[...], x_ref[...], contract)
        total = part if total is None else total + part
    return total


def pivot_products(at, pivot, found, n_row, contract, finish, outs, extra=()):
    rows, depth = pivot.shape[0], pivot.shape[1] // n_row
    count = len(found)
    width = outs[0].shape[1]

    def body(at_ref, *refs):
        total = products(refs[:count], refs[count : 2 * count], contract)
        extras = refs[2 * count : 2 * count + len(extra)]
        for ref, value in zip(refs[2 * count + len(extra) :], finish(total, *[e[...] for e in extras])):
            ref[...] = value

    return kernel_call(
        body,
        outs,
        (1,),
        1,
        column_specs(rows, depth, [o for o, _ in found], n_row)
        + [whole(x.shape) for _, x in found]
        + [whole(e.shape) for e in extra],
        [whole(o.shape) for o in outs],
        [],
        2 * rows * depth * width * count,
        2 * rows * depth * count,
    )(at, *[in_hbm(pivot)] * count, *[x for _, x in found], *extra)


def border_partial(at, coupling, found, partial, n_row):
    rows, depth = coupling.shape[0], coupling.shape[1] // n_row
    count, width = len(found), found[0][1].shape[1]
    tile = rows // border_steps(rows)

    moving = pl.BlockSpec((tile, width), lambda i, *_: (i, 0))

    def body(at_ref, *refs):
        total = products(refs[:count], refs[count : 2 * count], ((1,), (0,)))
        refs[-1][...] = total if partial is None else refs[-2][...] + total

    return kernel_call(
        body,
        jax.ShapeDtypeStruct((rows, width), F32),
        (rows // tile,),
        1,
        column_specs(tile, depth, [o for o, _ in found], n_row, True)
        + [whole(x.shape) for _, x in found]
        + [moving] * (partial is not None),
        moving,
        [],
        2 * rows * depth * width * count,
        2 * rows * depth * count,
    )(at, *[in_hbm(coupling)] * count, *[x for _, x in found], *([] if partial is None else [partial]))


def border_steps(rows):
    blocks = rows // BLK
    return blocks // next(k for k in (4, 3, 2, 1) if blocks % k == 0)


def border_scatter(at, local_index, coupling, found, partial, n_row, n_front, span_rows):
    rows, depth = coupling.shape[0], coupling.shape[1] // n_row
    count, width = len(found), found[0][1].shape[1]
    tile = rows // border_steps(rows)
    piece_blocks = span_rows // n_front // BLK

    def body(at_ref, index_ref, *refs):
        partial_ref, send_ref, keep_ref = refs[-3], refs[-2], refs[-1]
        step = pl.program_id(0)

        @pl.when(step == 0)
        def _():
            send_ref[...] = jnp.zeros_like(send_ref)
            keep_ref[...] = jnp.zeros_like(keep_ref)

        total = products(refs[:count], refs[count : 2 * count], ((1,), (0,)))
        total = (partial_ref[...] + total).astype(BF16)
        for j in range(tile // BLK):
            target = index_ref[step * (tile // BLK) + j]
            there = lax.div(target, piece_blocks)
            chip = lax.shift_right_logical(lax.bitwise_xor(there, at_ref[1]), 1)
            slot = chip * piece_blocks + lax.rem(target, piece_blocks)
            place = pl.ds(pl.multiple_of(slot * BLK, BLK), BLK)
            block = total[j * BLK : (j + 1) * BLK]
            away = lax.rem(there + at_ref[1], 2)

            @pl.when(away == 1)
            def _():
                send_ref[place, :] = block

            @pl.when(away == 0)
            def _():
                keep_ref[place, :] = block

    half = jax.ShapeDtypeStruct((span_rows // 2, width), BF16)
    return kernel_call(
        body,
        [half, half],
        (rows // tile,),
        2,
        column_specs(tile, depth, [o for o, _ in found], n_row, True)
        + [whole(x.shape) for _, x in found]
        + [pl.BlockSpec((tile, width), lambda i, *_: (i, 0))],
        [whole(half.shape)] * 2,
        [],
        2 * rows * depth * width * count,
        2 * rows * depth * count,
    )(at, local_index, *[in_hbm(coupling)] * count, *[x for _, x in found], partial)


def corner_parts(at, send, came):
    rows, width = send.shape[0] // 4, send.shape[1]
    half = jax.ShapeDtypeStruct((rows // 2, width), BF16)

    def body(at_ref, keep_ref, came_ref, low_ref, high_ref):
        total = (keep_ref[...].astype(F32) + came_ref[...].astype(F32)).astype(BF16)
        low_ref[...] = total[: rows // 2]
        high_ref[...] = total[rows // 2 :]

    block = pl.BlockSpec((rows, width), lambda i, *_: (3, 0))
    return kernel_call(
        body, [half, half], (1,), 1, [block] * 2, [whole(half.shape)] * 2, [], send.size, send.size
    )(at, send, came)


def side_parts(at, keep, came, low, high):
    rows, width = keep.shape[0] // 4, keep.shape[1]
    part = jax.ShapeDtypeStruct((rows, width), BF16)

    def body(at_ref, keep_x, came_x, keep_y, came_y, low_ref, high_ref, x_ref, y_ref):
        first, second = slice(0, rows // 2), slice(rows // 2, rows)
        for keep_ref, came_ref, add_ref, here, other, out_ref in (
            (keep_x, came_x, high_ref, second, first, x_ref),
            (keep_y, came_y, low_ref, first, second, y_ref),
        ):
            out_ref[other, :] = (keep_ref[other, :].astype(F32) + came_ref[other, :].astype(F32)).astype(BF16)
            both = keep_ref[here, :].astype(F32) + came_ref[here, :].astype(F32)
            out_ref[here, :] = (both + add_ref[...].astype(F32)).astype(BF16)

    one, two = (pl.BlockSpec((rows, width), lambda i, *_, k=k: (k, 0)) for k in (1, 2))
    return kernel_call(
        body,
        [part, part],
        (1,),
        1,
        [one, one, two, two] + [whole(low.shape)] * 2,
        [whole(part.shape)] * 2,
        [],
        2 * keep.size,
        3 * keep.size,
    )(at, keep, came, keep, came, low, high)


def own_part(at, rhs_root, keep, came, by_x, by_y):
    rows, width = by_x.shape

    def body(at_ref, rhs_ref, keep_ref, came_ref, x_ref, y_ref, out_ref):
        total = keep_ref[...].astype(F32) + came_ref[...].astype(F32)
        total = total + x_ref[...].astype(F32) + y_ref[...].astype(F32)
        out_ref[...] = (rhs_ref[...] - total).astype(BF16)

    block = pl.BlockSpec((rows, width), lambda i, *_: (0, 0))
    return kernel_call(
        body,
        jax.ShapeDtypeStruct((rows, width), BF16),
        (1,),
        1,
        [pl.BlockSpec((rows, width), lambda i, at_ref: (at_ref[1], 0)), block, block] + [whole(by_x.shape)] * 2,
        whole(by_x.shape),
        [],
        keep.size,
        2 * keep.size,
    )(at, in_hbm(rhs_root), keep, came, by_x, by_y)


def root_products(at, inverse, pieces, offsets, kinds, n_row, n_front):
    span_rows = inverse.shape[1]
    rows = inverse.shape[0] // n_row
    width = pieces[0][3].shape[1]
    piece_rows = span_rows // n_front
    count, many = len(offsets), len(pieces)

    def body(at_ref, a_hbm, *refs):
        piece_refs, out_refs = refs[:many], refs[many : many + count]
        a_ref, x_ref, sems = refs[-3:]
        copies = []
        for (chip, core, low, block), ref in zip(pieces, piece_refs):
            start = lax.bitwise_xor(at_ref[1], 2 * chip + core) * piece_rows + low
            place = pl.ds(pl.multiple_of(start, block.shape[0]), block.shape[0])
            copies.append(pltpu.make_async_copy(ref, x_ref.at[place], sems.at[len(copies)]))
        loads = []
        for i, offset in enumerate(offsets):
            place = pl.ds(pl.multiple_of(owner(at_ref, offset, n_row) * rows, rows), rows)
            loads.append(pltpu.make_async_copy(a_hbm.at[place], a_ref.at[i], sems.at[many + i]))
        for copy in loads[:1] + copies + loads[1:]:
            copy.start()
        for copy in copies:
            copy.wait()
        for i in range(count):
            loads[i].wait()
            out_refs[i][...] = dot(a_ref[i], x_ref[...]).astype(out_refs[i].dtype)

    return kernel_call(
        body,
        [jax.ShapeDtypeStruct((rows, width), kind) for kind in kinds],
        (1,),
        1,
        [ANY] * (1 + many),
        [whole((rows, width))] * count,
        [
            pltpu.VMEM((count, rows, span_rows), BF16),
            pltpu.VMEM((span_rows, width), BF16),
            pltpu.SemaphoreType.DMA((many + count,)),
        ],
        2 * rows * span_rows * width * count,
        2 * rows * span_rows * count,
    )(at, in_hbm(inverse), *[block for *_, block in pieces])


def border_pick(at, local_index, coupling, pieces, offset, n_row, n_front):
    rows, depth = coupling.shape[0], coupling.shape[1] // n_row
    piece_rows, width = pieces[0][3].shape
    quarter = piece_rows // n_row
    span_rows = piece_rows * n_front
    many = len(pieces)

    def body(at_ref, index_ref, a_hbm, *refs):
        piece_refs, out_ref, picked_ref = refs[:many], refs[many], refs[many + 1]
        a_ref, span_ref, sems = refs[-3:]
        columns = pl.ds(pl.multiple_of(owner(at_ref, offset, n_row) * depth, depth), depth)
        load = pltpu.make_async_copy(a_hbm.at[:, columns], a_ref, sems.at[0])
        copies = []
        for (chip, core, low, block), ref in zip(pieces, piece_refs):
            there = lax.bitwise_xor(at_ref[1], 2 * chip + core)
            base = lax.rem(there, 2) * (span_rows // 2) + lax.shift_right_logical(there, 1) * quarter
            for k in range(block.shape[0] // quarter):
                start = base + (low // quarter + k) * piece_rows
                place = pl.ds(pl.multiple_of(start, quarter), quarter)
                copies.append(
                    pltpu.make_async_copy(
                        ref.at[pl.ds(k * quarter, quarter)], span_ref.at[place], sems.at[1 + len(copies)]
                    )
                )
        load.start()
        for copy in copies:
            copy.start()
        for copy in copies:
            copy.wait()
        for j in range(rows // BLK):
            source = pl.ds(pl.multiple_of(index_ref[j] * BLK, BLK), BLK)
            picked_ref[:, pl.ds(j * BLK, BLK)] = jnp.transpose(span_ref[source, :])
        load.wait()
        out_ref[...] = dot(picked_ref[...], a_ref[...]).astype(BF16)

    return kernel_call(
        body,
        [jax.ShapeDtypeStruct((width, depth), BF16), jax.ShapeDtypeStruct((width, rows), BF16)],
        (1,),
        2,
        [ANY] * (1 + many),
        [whole((width, depth)), whole((width, rows))],
        [
            pltpu.VMEM((rows, depth), BF16),
            pltpu.VMEM((span_rows, width), BF16),
            pltpu.SemaphoreType.DMA((1 + n_front * n_row,)),
        ],
        2 * rows * depth * width,
        2 * rows * depth,
    )(at, local_index, in_hbm(coupling), *[block for *_, block in pieces])


def border_backward(at, coupling, picked, offsets, kinds, n_row):
    rows, depth = coupling.shape[0], coupling.shape[1] // n_row
    width, count = picked.shape[0], len(offsets)

    def body(at_ref, x_ref, *refs):
        for a_ref, out_ref in zip(refs[:count], refs[count:]):
            out_ref[...] = dot(x_ref[...], a_ref[...]).astype(out_ref.dtype)

    return kernel_call(
        body,
        [jax.ShapeDtypeStruct((width, depth), kind) for kind in kinds],
        (1,),
        1,
        [whole(picked.shape)] + column_specs(rows, depth, offsets, n_row),
        [whole((width, depth))] * count,
        [],
        2 * rows * depth * width * count,
        2 * rows * depth * count,
    )(at, picked, *[in_hbm(coupling)] * count)


def solve(n_front, n_row, rhs_front, rhs_root, pivot_inverse, border_coupling, root_inverse, border_map):
    row_at = lax.axis_index("row").astype(jnp.int32)
    front_at = lax.axis_index("front").astype(jnp.int32)
    at = jnp.stack([row_at, front_at])
    span_rows = root_inverse.shape[1]
    piece_rows, width = span_rows // n_front, rhs_front.shape[1]
    local_index = border_map[0] - row_at * (span_rows // BLK)
    first_at, later_at = far_offsets(n_row)
    chips = [[2 * chip + core for chip in range(n_front // 2)] for core in range(2)]
    block = jax.ShapeDtypeStruct((pivot_inverse.shape[0], width), F32)
    half = jax.ShapeDtypeStruct(block.shape, BF16)
    straight, across = ((1,), (0,)), ((1,), (1,))

    found = gather_row(rhs_front, n_row)
    early, last = found[:-1], found[-1:]
    partial = pivot_products(at, pivot_inverse, early, n_row, straight, lambda t: [t], [block])
    inner, inner_half = pivot_products(
        at,
        pivot_inverse,
        last,
        n_row,
        straight,
        lambda t, p: [t + p, (t + p).astype(BF16)],
        [block, half],
        partial,
    )
    found = gather_row(inner_half, n_row)
    partial = None
    for some in (found[:2], found[2:-1]):
        if some:
            partial = border_partial(at, border_coupling, some, partial, n_row)
    send, keep = border_scatter(
        at, local_index, border_coupling, found[-1:], partial, n_row, n_front, span_rows
    )
    came = swap(send, n_front, 1)
    low, high = corner_parts(at, keep, came)
    by_x, by_y = side_parts(at, keep, came, swap(low, n_front, 2), swap(high, n_front, 4))
    piece = own_part(at, rhs_root, keep, came, swap(by_x, n_front, 2), swap(by_y, n_front, 4))
    pieces = gather_front(piece, n_front)

    def root(offsets, kind):
        outs = root_products(at, root_inverse, pieces, offsets, [kind] * len(offsets), n_row, n_front)
        return dict(zip(offsets, outs))

    first = {}
    for offset in first_at:
        first.update(root([offset], BF16))
    rest = root(later_at + [0], F32)
    root_solution = scatter_row(first, rest, rest[0], n_row)
    quarters = root_solution.astype(BF16).reshape(n_row, piece_rows // n_row, width)
    quarters = lax.all_to_all(quarters, "front", 0, 0, axis_index_groups=chips)
    quarters = lax.all_to_all(quarters, "row", 0, 0)
    spans = gather_front(quarters.reshape(piece_rows, width), n_front)

    out, picked = border_pick(at, local_index, border_coupling, spans, first_at[0], n_row, n_front)
    first = {first_at[0]: out}
    for offset in first_at[1:]:
        first[offset] = border_backward(at, border_coupling, picked, [offset], [BF16], n_row)[0]
    offsets = later_at + [0]
    rest = dict(zip(offsets, border_backward(at, border_coupling, picked, offsets, [F32] * len(offsets), n_row)))
    pulled = scatter_row(first, rest, rest[0], n_row).astype(BF16)
    found = gather_row(pulled, n_row)
    early, last = found[:-1], found[-1:]
    partial = pivot_products(
        at, pivot_inverse, early, n_row, across, lambda t, i: [i - t], [block], [inner]
    )
    front_solution = pivot_products(
        at, pivot_inverse, last, n_row, across, lambda t, p: [p - t], [block], partial
    )
    return front_solution[0], root_solution


def solve_plain(n_front, n_row, rhs_front, rhs_root, pivot_inverse, border_coupling, root_inverse, border_map):
    row_at = lax.axis_index("row")
    front_at = lax.axis_index("front")
    width = rhs_front.shape[1]
    inner = dot(pivot_inverse, lax.all_gather(rhs_front, "row", axis=0, tiled=True))
    contrib = dot(border_coupling, lax.all_gather(inner.astype(BF16), "row", axis=0, tiled=True))
    block_local = border_map.shape[1]
    span_rows = root_inverse.shape[1]
    span_blocks = span_rows // BLK
    local_index = border_map[0] - row_at * span_blocks
    select = (local_index[None, :] == jnp.arange(span_blocks, dtype=jnp.int32)[:, None]).astype(F32)
    dense = jnp.einsum(
        "kj,jcn->kcn", select, contrib.reshape(block_local, BLK, width), precision=lax.Precision.HIGHEST
    ).reshape(span_rows, width)
    shares = lax.psum_scatter(dense, "front", scatter_dimension=0, tiled=True)
    own_rhs = lax.dynamic_slice_in_dim(rhs_root, front_at * shares.shape[0], shares.shape[0], 0)
    schur_rhs = lax.all_gather((own_rhs - shares).astype(BF16), "front", axis=0, tiled=True)
    root_solution = lax.psum_scatter(dot(root_inverse, schur_rhs), "row", scatter_dimension=0, tiled=True)
    gathered = lax.all_gather(root_solution.astype(BF16), ("front", "row"), axis=0, tiled=True)
    ranged = lax.dynamic_slice_in_dim(gathered, row_at * span_rows, span_rows, 0)
    picked = jnp.take(ranged.reshape(span_blocks, BLK, width), local_index, axis=0)
    picked = picked.reshape(block_local * BLK, width)
    pulled = lax.psum_scatter(
        dot(border_coupling, picked, ((0,), (0,))), "row", scatter_dimension=0, tiled=True
    ).astype(BF16)
    correction = dot(pivot_inverse, lax.all_gather(pulled, "row", axis=0, tiled=True))
    return inner - correction, root_solution


def solution(mesh):
    in_specs = (
        P(("front", "row"), None),
        P("row", None),
        P(("front", "row"), None),
        P(("front", "row"), None),
        P("front", "row"),
        P("front", "row"),
    )
    out_specs = (P(("front", "row"), None), P(("front", "row"), None))
    n_front, n_row = mesh.shape["front"], mesh.shape["row"]

    def per_device(*arrays):
        root_inverse, width = arrays[4], arrays[0].shape[1]
        fits = (
            n_front == 8
            and n_front == 2 * n_row
            and root_inverse.shape[1] % (n_front * BLK) == 0
            and root_inverse.shape[0] == n_row * (root_inverse.shape[1] // n_front)
            and root_inverse.shape[1] % (n_front * n_row * 16) == 0
            and arrays[2].shape[1] % (n_row * BLK) == 0
            and width % BLK == 0
        )
        return (solve if fits else solve_plain)(n_front, n_row, *arrays)

    return jax.shard_map(per_device, mesh=mesh, in_specs=in_specs, out_specs=out_specs, check_vma=False)
```

```python
import math

import jax
import jax.numpy as jnp
from jax import lax
from jax.experimental import pallas as pl
from jax.experimental.pallas import tpu as pltpu
from jax.sharding import PartitionSpec as P

BLK = 128
F32 = jnp.float32
BF16 = jnp.bfloat16
VMEM = pl.BlockSpec(memory_space=pltpu.VMEM)
ANY = pl.BlockSpec(memory_space=pl.ANY)


def dot(a, b, contract=((1,), (0,))):
    return lax.dot_general(a, b, (contract, ((), ())), preferred_element_type=F32)


def in_hbm(x):
    return pltpu.with_memory_space_constraint(x, pltpu.HBM)


def kernel_call(body, outs, scalars, held, placed, scratch, flops, nbytes, final=False):
    size = sum(2 * math.prod(s.shape) for s in scratch if s.dtype == BF16)
    single = not isinstance(outs, list)
    out_shape = [o if final else pltpu.VMEM(o.shape, o.dtype) for o in ([outs] if single else outs)]
    results = pl.pallas_call(
        body,
        out_shape=out_shape,
        grid_spec=pltpu.PrefetchScalarGridSpec(
            num_scalar_prefetch=len(scalars),
            grid=(1,),
            in_specs=[VMEM] * len(held) + [ANY] * len(placed),
            out_specs=[VMEM] * len(out_shape),
            scratch_shapes=scratch,
        ),
        compiler_params=pltpu.CompilerParams(vmem_limit_bytes=size + 12 * 1024 * 1024),
        cost_estimate=pl.CostEstimate(flops=flops, bytes_accessed=nbytes, transcendentals=0),
    )(*scalars, *[pltpu.with_memory_space_constraint(x, pltpu.VMEM) for x in held], *placed)
    return results[0] if single else results


def shift(x, size, by):
    return lax.ppermute(x, "row", [(i, (i + by) % size) for i in range(size)])


def swap(x, size, by):
    return lax.ppermute(x, "front", [(i, i ^ by) for i in range(size)])


def gather_row(x, n):
    found = [(0, x)]
    up, down = x, x
    for step in range(1, n // 2 + 1):
        up = shift(up, n, 1)
        found.append((-step, up))
        if step < n - step:
            down = shift(down, n, -1)
            found.append((step, down))
    return found


def gather_front(x, n):
    rows = x.shape[0]
    by_x, by_y = swap(x, n, 2), swap(x, n, 4)
    corner_low = swap(by_y[: rows // 2], n, 2)
    corner_high = swap(by_x[rows // 2 :], n, 4)
    mine = [(0, 0, x), (1, 0, by_x), (2, 0, by_y), (3, 0, corner_low), (3, rows // 2, corner_high)]
    found = [(chip, 0, low, block) for chip, low, block in mine]
    return found + [(chip, 1, low, swap(block, n, 1)) for chip, low, block in mine]


def to_plane(x, n):
    rows = x.shape[0] // n
    moved = []
    for k in range(n):
        quarter = x[k * rows : (k + 1) * rows]
        if k:
            quarter = swap(quarter, 2 * n, 2 * k)
        perm = [
            ((chip * 2 + core) * n + row, (row * 2 + core) * n + (chip ^ k))
            for chip in range(n)
            for core in range(2)
            for row in range(n)
        ]
        moved.append(lax.ppermute(quarter, ("front", "row"), perm))
    return jnp.concatenate(moved, axis=0)


def far_offsets(n):
    first = [-(n // 2)] + ([(n - 1) // 2] if n > 2 else [])
    later = [o for o in range(-(n // 2) + 1, (n - 1) // 2) if o]
    return first, later


def scatter_row(first, later, own, n):
    total = own
    for sign, far in ((-1, n // 2), (1, (n - 1) // 2)):
        running = None
        for step in range(far, 0, -1):
            if running is None:
                running = first[sign * step]
            else:
                running = (running.astype(F32) + later[sign * step]).astype(BF16)
            running = shift(running, n, sign)
        if running is not None:
            total = total + running.astype(F32)
    return total


def owner(at_ref, offset, n_row):
    return lax.rem(at_ref[0] + (offset + n_row), n_row)


def products(at_ref, a_ref, rows, offsets, x_refs, n_row, contract):
    depth = a_ref.shape[1] // n_row
    total = None
    for offset, x_ref in zip(offsets, x_refs):
        columns = pl.ds(pl.multiple_of(owner(at_ref, offset, n_row) * depth, depth), depth)
        part = dot(a_ref[rows, columns], x_ref[...], contract)
        total = part if total is None else total + part
    return total


def pivot_products(at, pivot, found, n_row, contract, finish, outs, extra=(), final=False):
    count = len(found)
    offsets = [o for o, _ in found]

    def body(at_ref, a_ref, *refs):
        total = products(at_ref, a_ref, slice(None), offsets, refs[:count], n_row, contract)
        extras = refs[count : count + len(extra)]
        for ref, value in zip(refs[count + len(extra) :], finish(total, *[e[...] for e in extras])):
            ref[...] = value

    share = 2 * pivot.size * count // n_row
    held = [pivot] + [x for _, x in found] + list(extra)
    return kernel_call(body, outs, [at], held, [], [], share * outs[0].shape[1], share, final)


def border_tile(rows):
    return BLK * next(k for k in (4, 3, 2, 1) if rows // BLK % k == 0)


def border_partial(at, coupling, found, n_row, partial, rhs_root, piece_rows):
    rows, count, width = coupling.shape[0], len(found), found[0][1].shape[1]
    offsets = [o for o, _ in found]
    tile = border_tile(rows)
    held = [coupling] + [x for _, x in found] + ([] if partial is None else [partial])

    def body(at_ref, a_ref, *refs):
        if partial is None:
            rhs_hbm, out_ref, own_ref, sem = refs[count:]
            place = pl.ds(pl.multiple_of(at_ref[1] * piece_rows, piece_rows), piece_rows)
            copy = pltpu.make_async_copy(rhs_hbm.at[place], own_ref, sem)
            copy.start()
        else:
            partial_ref, out_ref = refs[count:]

        @pl.loop(0, rows // tile)
        def _(i):
            place = pl.ds(pl.multiple_of(i * tile, tile), tile)
            total = products(at_ref, a_ref, place, offsets, refs[:count], n_row, ((1,), (0,)))
            out_ref[place, :] = total if partial is None else partial_ref[place, :] + total

        if partial is None:
            copy.wait()

    share = 2 * coupling.size * count // n_row
    out = jax.ShapeDtypeStruct((rows, width), F32)
    if partial is None:
        outs = [out, jax.ShapeDtypeStruct((piece_rows, width), F32)]
        scratch = [pltpu.SemaphoreType.DMA]
        return kernel_call(body, outs, [at], held, [in_hbm(rhs_root)], scratch, share * width, share)
    return kernel_call(body, out, [at], held, [], [], share * width, share)


def border_scatter(at, local_index, coupling, found, partial, n_row, n_front, span_rows):
    rows, count, width = coupling.shape[0], len(found), found[0][1].shape[1]
    offsets = [o for o, _ in found]
    tile = border_tile(rows)
    piece_blocks = span_rows // n_front // BLK

    def body(at_ref, index_ref, a_ref, *refs):
        partial_ref, send_ref, keep_ref = refs[count:]
        send_ref[...] = jnp.zeros_like(send_ref)
        keep_ref[...] = jnp.zeros_like(keep_ref)

        @pl.loop(0, rows // tile)
        def _(i):
            place = pl.ds(pl.multiple_of(i * tile, tile), tile)
            total = products(at_ref, a_ref, place, offsets, refs[:count], n_row, ((1,), (0,)))
            total = (partial_ref[place, :] + total).astype(BF16)
            for j in range(tile // BLK):
                target = index_ref[i * (tile // BLK) + j]
                there = lax.div(target, piece_blocks)
                chip = lax.shift_right_logical(lax.bitwise_xor(there, at_ref[1]), 1)
                slot = chip * piece_blocks + lax.rem(target, piece_blocks)
                goal = pl.ds(pl.multiple_of(slot * BLK, BLK), BLK)
                block = total[j * BLK : (j + 1) * BLK]
                away = lax.rem(there + at_ref[1], 2)

                @pl.when(away == 1)
                def _():
                    send_ref[goal, :] = block

                @pl.when(away == 0)
                def _():
                    keep_ref[goal, :] = block

    half = jax.ShapeDtypeStruct((span_rows // 2, width), BF16)
    share = 2 * coupling.size * count // n_row
    held = [coupling] + [x for _, x in found] + [partial]
    return kernel_call(body, [half, half], [at, local_index], held, [], [], share * width, share)


def added(*parts):
    total = parts[0].astype(F32)
    for part in parts[1:]:
        total = total + part.astype(F32)
    return total


def corner_parts(keep, came):
    rows, width = keep.shape[0] // 4, keep.shape[1]
    half = jax.ShapeDtypeStruct((rows // 2, width), BF16)

    def body(keep_ref, came_ref, low_ref, high_ref):
        for start, out_ref in ((3 * rows, low_ref), (3 * rows + rows // 2, high_ref)):
            place = slice(start, start + rows // 2)
            out_ref[...] = added(keep_ref[place, :], came_ref[place, :]).astype(BF16)

    return kernel_call(body, [half, half], [], [keep, came], [], [], keep.size, keep.size)


def side_parts(keep, came, low, high):
    rows, width = keep.shape[0] // 4, keep.shape[1]
    part = jax.ShapeDtypeStruct((rows, width), BF16)

    def body(keep_ref, came_ref, low_ref, high_ref, x_ref, y_ref):
        first, second = (0, rows // 2), (rows // 2, rows)
        for slot, add_ref, here, other, out_ref in (
            (1, high_ref, second, first, x_ref),
            (2, low_ref, first, second, y_ref),
        ):
            place = slice(slot * rows + other[0], slot * rows + other[1])
            out_ref[other[0] : other[1], :] = added(keep_ref[place, :], came_ref[place, :]).astype(BF16)
            place = slice(slot * rows + here[0], slot * rows + here[1])
            total = added(keep_ref[place, :], came_ref[place, :], add_ref[...])
            out_ref[here[0] : here[1], :] = total.astype(BF16)

    return kernel_call(body, [part, part], [], [keep, came, low, high], [], [], 2 * keep.size, 2 * keep.size)


def own_part(own_rhs, keep, came, by_x, by_y):
    rows, width = by_x.shape

    def body(rhs_ref, keep_ref, came_ref, x_ref, y_ref, out_ref):
        total = added(keep_ref[:rows, :], came_ref[:rows, :], x_ref[...], y_ref[...])
        out_ref[...] = (rhs_ref[...] - total).astype(BF16)

    out = jax.ShapeDtypeStruct((rows, width), BF16)
    return kernel_call(body, out, [], [own_rhs, keep, came, by_x, by_y], [], [], keep.size, keep.size)


def assemble(pieces, piece_refs, target_ref, sems, base):
    copies = []
    for (chip, core, low, block), ref in zip(pieces, piece_refs):
        start = base(2 * chip + core) + low
        place = pl.ds(pl.multiple_of(start, block.shape[0]), block.shape[0])
        copies.append(pltpu.make_async_copy(ref, target_ref.at[place], sems.at[len(copies)]))
    return copies


def root_products(at, inverse, pieces, offsets, kinds, n_row, n_front):
    span_rows = inverse.shape[1]
    rows = inverse.shape[0] // n_row
    width = pieces[0][3].shape[1]
    piece_rows = span_rows // n_front
    count, many = len(offsets), len(pieces)

    def body(at_ref, *refs):
        piece_refs, a_hbm, out_refs = refs[:many], refs[many], refs[many + 1 : many + 1 + count]
        a_ref, x_ref, sems = refs[-3:]
        copies = assemble(
            pieces, piece_refs, x_ref, sems, lambda d: lax.bitwise_xor(at_ref[1], d) * piece_rows
        )
        loads = []
        for i, offset in enumerate(offsets):
            place = pl.ds(pl.multiple_of(owner(at_ref, offset, n_row) * rows, rows), rows)
            loads.append(pltpu.make_async_copy(a_hbm.at[place], a_ref.at[i], sems.at[many + i]))
        for copy in loads[:1] + copies + loads[1:]:
            copy.start()
        for copy in copies:
            copy.wait()
        for i in range(count):
            loads[i].wait()
            out_refs[i][...] = dot(a_ref[i], x_ref[...]).astype(out_refs[i].dtype)

    outs = [jax.ShapeDtypeStruct((rows, width), kind) for kind in kinds]
    scratch = [
        pltpu.VMEM((count, rows, span_rows), BF16),
        pltpu.VMEM((span_rows, width), BF16),
        pltpu.SemaphoreType.DMA((many + count,)),
    ]
    share = 2 * rows * span_rows * count
    held = [block for *_, block in pieces]
    return kernel_call(body, outs, [at], held, [in_hbm(inverse)], scratch, share * width, share)


def border_pick(at, local_index, coupling, pieces, offset, n_row, n_front):
    rows, depth = coupling.shape[0], coupling.shape[1] // n_row
    piece_rows, width = pieces[0][3].shape
    span_rows = piece_rows * n_front
    many = len(pieces)

    def body(at_ref, index_ref, a_ref, *refs):
        piece_refs, (out_ref, picked_ref, span_ref, sems) = refs[:many], refs[many:]

        def base(d):
            there = lax.bitwise_xor(at_ref[1], d)
            return lax.rem(there, 2) * (span_rows // 2) + lax.shift_right_logical(there, 1) * piece_rows

        copies = assemble(pieces, piece_refs, span_ref, sems, base)
        for copy in copies:
            copy.start()
        for copy in copies:
            copy.wait()
        for j in range(rows // BLK):
            source = pl.ds(pl.multiple_of(index_ref[j] * BLK, BLK), BLK)
            picked_ref[:, pl.ds(j * BLK, BLK)] = jnp.transpose(span_ref[source, :])
        columns = pl.ds(pl.multiple_of(owner(at_ref, offset, n_row) * depth, depth), depth)
        out_ref[...] = dot(picked_ref[...], a_ref[:, columns]).astype(BF16)

    outs = [jax.ShapeDtypeStruct((width, depth), BF16), jax.ShapeDtypeStruct((width, rows), BF16)]
    scratch = [pltpu.VMEM((span_rows, width), BF16), pltpu.SemaphoreType.DMA((many,))]
    share = 2 * rows * depth
    held = [coupling] + [block for *_, block in pieces]
    return kernel_call(body, outs, [at, local_index], held, [], scratch, share * width, share)


def border_backward(at, coupling, picked, offsets, kinds, n_row):
    rows, depth = coupling.shape[0], coupling.shape[1] // n_row
    width, count = picked.shape[0], len(offsets)

    def body(at_ref, x_ref, a_ref, *out_refs):
        for offset, out_ref in zip(offsets, out_refs):
            columns = pl.ds(pl.multiple_of(owner(at_ref, offset, n_row) * depth, depth), depth)
            out_ref[...] = dot(x_ref[...], a_ref[:, columns]).astype(out_ref.dtype)

    outs = [jax.ShapeDtypeStruct((width, depth), kind) for kind in kinds]
    share = 2 * rows * depth * count
    return kernel_call(body, outs, [at], [picked, coupling], [], [], share * width, share)


def solve(n_front, n_row, rhs_front, rhs_root, pivot_inverse, border_coupling, root_inverse, border_map):
    row_at = lax.axis_index("row").astype(jnp.int32)
    front_at = lax.axis_index("front").astype(jnp.int32)
    at = jnp.stack([row_at, front_at])
    span_rows = root_inverse.shape[1]
    piece_rows, width = span_rows // n_front, rhs_front.shape[1]
    local_index = border_map[0] - row_at * (span_rows // BLK)
    first_at, later_at = far_offsets(n_row)
    block = jax.ShapeDtypeStruct((pivot_inverse.shape[0], width), F32)
    half = jax.ShapeDtypeStruct(block.shape, BF16)
    straight, across = ((1,), (0,)), ((1,), (1,))

    found = gather_row(rhs_front, n_row)
    early, last = found[:-1], found[-1:]
    partial = pivot_products(at, pivot_inverse, early, n_row, straight, lambda t: [t], [block])
    inner, inner_half = pivot_products(
        at,
        pivot_inverse,
        last,
        n_row,
        straight,
        lambda t, p: [t + p, (t + p).astype(BF16)],
        [block, half],
        partial,
    )
    found = gather_row(inner_half, n_row)
    partial, own_rhs = border_partial(at, border_coupling, found[:2], n_row, None, rhs_root, piece_rows)
    if found[2:-1]:
        partial = border_partial(at, border_coupling, found[2:-1], n_row, partial, rhs_root, piece_rows)
    send, keep = border_scatter(
        at, local_index, border_coupling, found[-1:], partial, n_row, n_front, span_rows
    )
    came = swap(send, n_front, 1)
    low, high = corner_parts(keep, came)
    by_x, by_y = side_parts(keep, came, swap(low, n_front, 2), swap(high, n_front, 4))
    piece = own_part(own_rhs, keep, came, swap(by_x, n_front, 2), swap(by_y, n_front, 4))
    pieces = gather_front(piece, n_front)

    def root(offsets, kind):
        outs = root_products(at, root_inverse, pieces, offsets, [kind] * len(offsets), n_row, n_front)
        return dict(zip(offsets, outs))

    first = {}
    for offset in first_at:
        first.update(root([offset], BF16))
    rest = root(later_at + [0], F32)
    root_solution = scatter_row(first, rest, rest[0], n_row)
    spans = gather_front(to_plane(root_solution.astype(BF16), n_row), n_front)

    out, picked = border_pick(at, local_index, border_coupling, spans, first_at[0], n_row, n_front)
    first = {first_at[0]: out}
    for offset in first_at[1:]:
        first[offset] = border_backward(at, border_coupling, picked, [offset], [BF16], n_row)[0]
    offsets = later_at + [0]
    rest = dict(zip(offsets, border_backward(at, border_coupling, picked, offsets, [F32] * len(offsets), n_row)))
    pulled = scatter_row(first, rest, rest[0], n_row).astype(BF16)
    found = gather_row(pulled, n_row)
    early, last = found[:-1], found[-1:]
    partial = pivot_products(
        at, pivot_inverse, early, n_row, across, lambda t, i: [i - t], [block], [inner]
    )
    front_solution = pivot_products(
        at, pivot_inverse, last, n_row, across, lambda t, p: [p - t], [block], partial, True
    )
    return front_solution[0], root_solution


def solve_plain(n_front, n_row, rhs_front, rhs_root, pivot_inverse, border_coupling, root_inverse, border_map):
    row_at = lax.axis_index("row")
    front_at = lax.axis_index("front")
    width = rhs_front.shape[1]
    inner = dot(pivot_inverse, lax.all_gather(rhs_front, "row", axis=0, tiled=True))
    contrib = dot(border_coupling, lax.all_gather(inner.astype(BF16), "row", axis=0, tiled=True))
    block_local = border_map.shape[1]
    span_rows = root_inverse.shape[1]
    span_blocks = span_rows // BLK
    local_index = border_map[0] - row_at * span_blocks
    select = (local_index[None, :] == jnp.arange(span_blocks, dtype=jnp.int32)[:, None]).astype(F32)
    dense = jnp.einsum(
        "kj,jcn->kcn", select, contrib.reshape(block_local, BLK, width), precision=lax.Precision.HIGHEST
    ).reshape(span_rows, width)
    shares = lax.psum_scatter(dense, "front", scatter_dimension=0, tiled=True)
    own_rhs = lax.dynamic_slice_in_dim(rhs_root, front_at * shares.shape[0], shares.shape[0], 0)
    schur_rhs = lax.all_gather((own_rhs - shares).astype(BF16), "front", axis=0, tiled=True)
    root_solution = lax.psum_scatter(dot(root_inverse, schur_rhs), "row", scatter_dimension=0, tiled=True)
    gathered = lax.all_gather(root_solution.astype(BF16), ("front", "row"), axis=0, tiled=True)
    ranged = lax.dynamic_slice_in_dim(gathered, row_at * span_rows, span_rows, 0)
    picked = jnp.take(ranged.reshape(span_blocks, BLK, width), local_index, axis=0)
    picked = picked.reshape(block_local * BLK, width)
    pulled = lax.psum_scatter(
        dot(border_coupling, picked, ((0,), (0,))), "row", scatter_dimension=0, tiled=True
    ).astype(BF16)
    correction = dot(pivot_inverse, lax.all_gather(pulled, "row", axis=0, tiled=True))
    return inner - correction, root_solution


def solution(mesh):
    in_specs = (
        P(("front", "row"), None),
        P("row", None),
        P(("front", "row"), None),
        P(("front", "row"), None),
        P("front", "row"),
        P("front", "row"),
    )
    out_specs = (P(("front", "row"), None), P(("front", "row"), None))
    n_front, n_row = mesh.shape["front"], mesh.shape["row"]

    def per_device(*arrays):
        root_inverse, width = arrays[4], arrays[0].shape[1]
        fits = (
            n_front == 8
            and n_front == 2 * n_row
            and root_inverse.shape[1] % (n_front * BLK) == 0
            and root_inverse.shape[0] == n_row * (root_inverse.shape[1] // n_front)
            and root_inverse.shape[1] % (n_front * n_row * 16) == 0
            and arrays[2].shape[1] % (n_row * BLK) == 0
            and width % BLK == 0
        )
        return (solve if fits else solve_plain)(n_front, n_row, *arrays)

    return jax.shard_map(per_device, mesh=mesh, in_specs=in_specs, out_specs=out_specs, check_vma=False)
```

```python
import math

import jax
import jax.numpy as jnp
from jax import lax
from jax.experimental import pallas as pl
from jax.experimental.pallas import tpu as pltpu
from jax.sharding import PartitionSpec as P

BLK = 128
F32 = jnp.float32
BF16 = jnp.bfloat16
VMEM = pl.BlockSpec(memory_space=pltpu.VMEM)
ANY = pl.BlockSpec(memory_space=pl.ANY)


def dot(a, b, contract=((1,), (0,))):
    return lax.dot_general(a, b, (contract, ((), ())), preferred_element_type=F32)


def in_hbm(x):
    return pltpu.with_memory_space_constraint(x, pltpu.HBM)


def kernel_call(body, outs, scalars, held, placed, scratch, flops, nbytes, final=False):
    size = sum(2 * math.prod(s.shape) for s in scratch if s.dtype == BF16)
    single = not isinstance(outs, list)
    out_shape = [o if final else pltpu.VMEM(o.shape, o.dtype) for o in ([outs] if single else outs)]
    results = pl.pallas_call(
        body,
        out_shape=out_shape,
        grid_spec=pltpu.PrefetchScalarGridSpec(
            num_scalar_prefetch=len(scalars),
            grid=(1,),
            in_specs=[VMEM] * len(held) + [ANY] * len(placed),
            out_specs=[VMEM] * len(out_shape),
            scratch_shapes=scratch,
        ),
        compiler_params=pltpu.CompilerParams(vmem_limit_bytes=size + 12 * 1024 * 1024),
        cost_estimate=pl.CostEstimate(flops=flops, bytes_accessed=nbytes, transcendentals=0),
    )(*scalars, *[pltpu.with_memory_space_constraint(x, pltpu.VMEM) for x in held], *placed)
    return results[0] if single else results


def shift(x, size, by):
    return lax.ppermute(x, "row", [(i, (i + by) % size) for i in range(size)])


def swap(x, size, by):
    return lax.ppermute(x, "front", [(i, i ^ by) for i in range(size)])


def gather_row(x, n):
    found = [(0, x)]
    up, down = x, x
    for step in range(1, n // 2 + 1):
        up = shift(up, n, 1)
        found.append((-step, up))
        if step < n - step:
            down = shift(down, n, -1)
            found.append((step, down))
    return found


def gather_front(x, n):
    rows = x.shape[0]
    by_x, by_y = swap(x, n, 2), swap(x, n, 4)
    corner_low = swap(by_y[: rows // 2], n, 2)
    corner_high = swap(by_x[rows // 2 :], n, 4)
    mine = [(0, 0, x), (1, 0, by_x), (2, 0, by_y), (3, 0, corner_low), (3, rows // 2, corner_high)]
    found = [(chip, 0, low, block) for chip, low, block in mine]
    return found + [(chip, 1, low, swap(block, n, 1)) for chip, low, block in mine]


def to_plane(x, n):
    rows = x.shape[0] // n
    moved = []
    for k in range(n):
        quarter = x[k * rows : (k + 1) * rows]
        if k:
            quarter = swap(quarter, 2 * n, 2 * k)
        perm = [
            ((chip * 2 + core) * n + row, (row * 2 + core) * n + (chip ^ k))
            for chip in range(n)
            for core in range(2)
            for row in range(n)
        ]
        moved.append(lax.ppermute(quarter, ("front", "row"), perm))
    return jnp.concatenate(moved, axis=0)


def far_offsets(n):
    first = [-(n // 2)] + ([(n - 1) // 2] if n > 2 else [])
    later = [o for o in range(-(n // 2) + 1, (n - 1) // 2) if o]
    return first, later


def scatter_row(first, later, own, n):
    total = own
    for sign, far in ((-1, n // 2), (1, (n - 1) // 2)):
        running = None
        for step in range(far, 0, -1):
            if running is None:
                running = first[sign * step]
            else:
                running = (running.astype(F32) + later[sign * step]).astype(BF16)
            running = shift(running, n, sign)
        if running is not None:
            total = total + running.astype(F32)
    return total


def owner(at_ref, offset, n_row):
    return lax.rem(at_ref[0] + (offset + n_row), n_row)


def products(at_ref, a_ref, rows, offsets, x_refs, n_row, contract):
    depth = a_ref.shape[1] // n_row
    total = None
    for offset, x_ref in zip(offsets, x_refs):
        columns = pl.ds(pl.multiple_of(owner(at_ref, offset, n_row) * depth, depth), depth)
        part = dot(a_ref[rows, columns], x_ref[...], contract)
        total = part if total is None else total + part
    return total


def pivot_products(at, pivot, found, n_row, contract, finish, outs, extra=(), final=False):
    count = len(found)
    offsets = [o for o, _ in found]

    def body(at_ref, a_ref, *refs):
        total = products(at_ref, a_ref, slice(None), offsets, refs[:count], n_row, contract)
        extras = refs[count : count + len(extra)]
        for ref, value in zip(refs[count + len(extra) :], finish(total, *[e[...] for e in extras])):
            ref[...] = value

    share = 2 * pivot.size * count // n_row
    held = [pivot] + [x for _, x in found] + list(extra)
    return kernel_call(body, outs, [at], held, [], [], share * outs[0].shape[1], share, final)


def border_tile(rows):
    return BLK * next(k for k in (4, 3, 2, 1) if rows // BLK % k == 0)


def border_partial(at, coupling, found, n_row, partial, rhs_root, piece_rows):
    rows, count, width = coupling.shape[0], len(found), found[0][1].shape[1]
    offsets = [o for o, _ in found]
    tile = border_tile(rows)
    held = [coupling] + [x for _, x in found] + ([] if partial is None else [partial])

    def body(at_ref, a_ref, *refs):
        if partial is None:
            rhs_hbm, out_ref, own_ref, sem = refs[count:]
            place = pl.ds(pl.multiple_of(at_ref[1] * piece_rows, piece_rows), piece_rows)
            copy = pltpu.make_async_copy(rhs_hbm.at[place], own_ref, sem)
            copy.start()
        else:
            partial_ref, out_ref = refs[count:]

        @pl.loop(0, rows // tile)
        def _(i):
            place = pl.ds(pl.multiple_of(i * tile, tile), tile)
            total = products(at_ref, a_ref, place, offsets, refs[:count], n_row, ((1,), (0,)))
            out_ref[place, :] = total if partial is None else partial_ref[place, :] + total

        if partial is None:
            copy.wait()

    share = 2 * coupling.size * count // n_row
    out = jax.ShapeDtypeStruct((rows, width), F32)
    if partial is None:
        outs = [out, jax.ShapeDtypeStruct((piece_rows, width), F32)]
        scratch = [pltpu.SemaphoreType.DMA]
        return kernel_call(body, outs, [at], held, [in_hbm(rhs_root)], scratch, share * width, share)
    return kernel_call(body, out, [at], held, [], [], share * width, share)


def border_scatter(at, local_index, coupling, found, partial, n_row, n_front, span_rows):
    rows, count, width = coupling.shape[0], len(found), found[0][1].shape[1]
    offsets = [o for o, _ in found]
    tile = border_tile(rows)
    piece_blocks = span_rows // n_front // BLK

    def body(at_ref, index_ref, a_ref, *refs):
        partial_ref, send_ref, keep_ref = refs[count:]
        send_ref[...] = jnp.zeros_like(send_ref)
        keep_ref[...] = jnp.zeros_like(keep_ref)

        @pl.loop(0, rows // tile)
        def _(i):
            place = pl.ds(pl.multiple_of(i * tile, tile), tile)
            total = products(at_ref, a_ref, place, offsets, refs[:count], n_row, ((1,), (0,)))
            total = (partial_ref[place, :] + total).astype(BF16)
            for j in range(tile // BLK):
                target = index_ref[i * (tile // BLK) + j]
                there = lax.div(target, piece_blocks)
                chip = lax.shift_right_logical(lax.bitwise_xor(there, at_ref[1]), 1)
                slot = chip * piece_blocks + lax.rem(target, piece_blocks)
                goal = pl.ds(pl.multiple_of(slot * BLK, BLK), BLK)
                block = total[j * BLK : (j + 1) * BLK]
                away = lax.rem(there + at_ref[1], 2)

                @pl.when(away == 1)
                def _():
                    send_ref[goal, :] = block

                @pl.when(away == 0)
                def _():
                    keep_ref[goal, :] = block

    half = jax.ShapeDtypeStruct((span_rows // 2, width), BF16)
    share = 2 * coupling.size * count // n_row
    held = [coupling] + [x for _, x in found] + [partial]
    return kernel_call(body, [half, half], [at, local_index], held, [], [], share * width, share)


def added(*parts):
    total = parts[0].astype(F32)
    for part in parts[1:]:
        total = total + part.astype(F32)
    return total


def corner_parts(keep, came):
    rows, width = keep.shape[0] // 4, keep.shape[1]
    half = jax.ShapeDtypeStruct((rows // 2, width), BF16)

    def body(keep_ref, came_ref, low_ref, high_ref):
        for start, out_ref in ((3 * rows, low_ref), (3 * rows + rows // 2, high_ref)):
            place = slice(start, start + rows // 2)
            out_ref[...] = added(keep_ref[place, :], came_ref[place, :]).astype(BF16)

    return kernel_call(body, [half, half], [], [keep, came], [], [], keep.size, keep.size)


def side_parts(keep, came, low, high):
    rows, width = keep.shape[0] // 4, keep.shape[1]
    part = jax.ShapeDtypeStruct((rows, width), BF16)

    def body(keep_ref, came_ref, low_ref, high_ref, x_ref, y_ref):
        first, second = (0, rows // 2), (rows // 2, rows)
        for slot, add_ref, here, other, out_ref in (
            (1, high_ref, second, first, x_ref),
            (2, low_ref, first, second, y_ref),
        ):
            place = slice(slot * rows + other[0], slot * rows + other[1])
            out_ref[other[0] : other[1], :] = added(keep_ref[place, :], came_ref[place, :]).astype(BF16)
            place = slice(slot * rows + here[0], slot * rows + here[1])
            total = added(keep_ref[place, :], came_ref[place, :], add_ref[...])
            out_ref[here[0] : here[1], :] = total.astype(BF16)

    return kernel_call(body, [part, part], [], [keep, came, low, high], [], [], 2 * keep.size, 2 * keep.size)


def own_part(own_rhs, keep, came, by_x, by_y):
    rows, width = by_x.shape

    def body(rhs_ref, keep_ref, came_ref, x_ref, y_ref, out_ref):
        total = added(keep_ref[:rows, :], came_ref[:rows, :], x_ref[...], y_ref[...])
        out_ref[...] = (rhs_ref[...] - total).astype(BF16)

    out = jax.ShapeDtypeStruct((rows, width), BF16)
    return kernel_call(body, out, [], [own_rhs, keep, came, by_x, by_y], [], [], keep.size, keep.size)


def assemble(pieces, piece_refs, target_ref, sems, base):
    copies = []
    for (chip, core, low, block), ref in zip(pieces, piece_refs):
        start = base(2 * chip + core) + low
        place = pl.ds(pl.multiple_of(start, block.shape[0]), block.shape[0])
        copies.append(pltpu.make_async_copy(ref, target_ref.at[place], sems.at[len(copies)]))
    return copies


def root_products(at, inverse, pieces, offsets, kinds, n_row, n_front):
    span_rows = inverse.shape[1]
    rows = inverse.shape[0] // n_row
    width = pieces[0][3].shape[1]
    piece_rows = span_rows // n_front
    count, many = len(offsets), len(pieces)

    def body(at_ref, *refs):
        piece_refs, a_hbm, out_refs = refs[:many], refs[many], refs[many + 1 : many + 1 + count]
        a_ref, x_ref, sems = refs[-3:]
        copies = assemble(
            pieces, piece_refs, x_ref, sems, lambda d: lax.bitwise_xor(at_ref[1], d) * piece_rows
        )
        loads = []
        for i, offset in enumerate(offsets):
            place = pl.ds(pl.multiple_of(owner(at_ref, offset, n_row) * rows, rows), rows)
            loads.append(pltpu.make_async_copy(a_hbm.at[place], a_ref.at[i], sems.at[many + i]))
        for copy in loads[:1] + copies + loads[1:]:
            copy.start()
        for copy in copies:
            copy.wait()
        for i in range(count):
            loads[i].wait()
            out_refs[i][...] = dot(a_ref[i], x_ref[...]).astype(out_refs[i].dtype)

    outs = [jax.ShapeDtypeStruct((rows, width), kind) for kind in kinds]
    scratch = [
        pltpu.VMEM((count, rows, span_rows), BF16),
        pltpu.VMEM((span_rows, width), BF16),
        pltpu.SemaphoreType.DMA((many + count,)),
    ]
    share = 2 * rows * span_rows * count
    held = [block for *_, block in pieces]
    return kernel_call(body, outs, [at], held, [in_hbm(inverse)], scratch, share * width, share)


def border_pick(at, local_index, coupling, pieces, offset, n_row, n_front):
    rows, depth = coupling.shape[0], coupling.shape[1] // n_row
    piece_rows, width = pieces[0][3].shape
    span_rows = piece_rows * n_front
    many = len(pieces)

    def body(at_ref, index_ref, a_ref, *refs):
        piece_refs, (out_ref, picked_ref, span_ref, sems) = refs[:many], refs[many:]

        def base(d):
            there = lax.bitwise_xor(at_ref[1], d)
            return lax.rem(there, 2) * (span_rows // 2) + lax.shift_right_logical(there, 1) * piece_rows

        copies = assemble(pieces, piece_refs, span_ref, sems, base)
        for copy in copies:
            copy.start()
        for copy in copies:
            copy.wait()
        for j in range(rows // BLK):
            source = pl.ds(pl.multiple_of(index_ref[j] * BLK, BLK), BLK)
            picked_ref[:, pl.ds(j * BLK, BLK)] = jnp.transpose(span_ref[source, :])
        columns = pl.ds(pl.multiple_of(owner(at_ref, offset, n_row) * depth, depth), depth)
        out_ref[...] = dot(picked_ref[...], a_ref[:, columns]).astype(BF16)

    outs = [jax.ShapeDtypeStruct((width, depth), BF16), jax.ShapeDtypeStruct((width, rows), BF16)]
    scratch = [pltpu.VMEM((span_rows, width), BF16), pltpu.SemaphoreType.DMA((many,))]
    share = 2 * rows * depth
    held = [coupling] + [block for *_, block in pieces]
    return kernel_call(body, outs, [at, local_index], held, [], scratch, share * width, share)


def border_backward(at, coupling, picked, offsets, kinds, n_row):
    rows, depth = coupling.shape[0], coupling.shape[1] // n_row
    width, count = picked.shape[0], len(offsets)

    def body(at_ref, x_ref, a_ref, *out_refs):
        for offset, out_ref in zip(offsets, out_refs):
            columns = pl.ds(pl.multiple_of(owner(at_ref, offset, n_row) * depth, depth), depth)
            out_ref[...] = dot(x_ref[...], a_ref[:, columns]).astype(out_ref.dtype)

    outs = [jax.ShapeDtypeStruct((width, depth), kind) for kind in kinds]
    share = 2 * rows * depth * count
    return kernel_call(body, outs, [at], [picked, coupling], [], [], share * width, share)


def solve(n_front, n_row, rhs_front, rhs_root, pivot_inverse, border_coupling, root_inverse, border_map):
    row_at = lax.axis_index("row").astype(jnp.int32)
    front_at = lax.axis_index("front").astype(jnp.int32)
    at = jnp.stack([row_at, front_at])
    span_rows = root_inverse.shape[1]
    piece_rows, width = span_rows // n_front, rhs_front.shape[1]
    local_index = border_map[0] - row_at * (span_rows // BLK)
    first_at, later_at = far_offsets(n_row)
    block = jax.ShapeDtypeStruct((pivot_inverse.shape[0], width), F32)
    half = jax.ShapeDtypeStruct(block.shape, BF16)
    straight, across = ((1,), (0,)), ((1,), (1,))

    found = gather_row(rhs_front, n_row)
    early, last = found[:-1], found[-1:]
    partial = pivot_products(at, pivot_inverse, early, n_row, straight, lambda t: [t], [block])
    inner, inner_half = pivot_products(
        at,
        pivot_inverse,
        last,
        n_row,
        straight,
        lambda t, p: [t + p, (t + p).astype(BF16)],
        [block, half],
        partial,
    )
    found = gather_row(inner_half, n_row)
    partial, own_rhs = border_partial(at, border_coupling, found[:2], n_row, None, rhs_root, piece_rows)
    if found[2:-1]:
        partial = border_partial(at, border_coupling, found[2:-1], n_row, partial, rhs_root, piece_rows)
    send, keep = border_scatter(
        at, local_index, border_coupling, found[-1:], partial, n_row, n_front, span_rows
    )
    came = swap(send, n_front, 1)
    low, high = corner_parts(keep, came)
    by_x, by_y = side_parts(keep, came, swap(low, n_front, 2), swap(high, n_front, 4))
    piece = own_part(own_rhs, keep, came, swap(by_x, n_front, 2), swap(by_y, n_front, 4))
    pieces = gather_front(piece, n_front)

    def root(offsets, kind):
        outs = root_products(at, root_inverse, pieces, offsets, [kind] * len(offsets), n_row, n_front)
        return dict(zip(offsets, outs))

    first = {}
    for offset in first_at:
        first.update(root([offset], BF16))
    rest = root(later_at + [0], F32)
    root_solution = scatter_row(first, rest, rest[0], n_row)
    spans = gather_front(to_plane(root_solution.astype(BF16), n_row), n_front)

    out, picked = border_pick(at, local_index, border_coupling, spans, first_at[0], n_row, n_front)
    first = {first_at[0]: out}
    for offset in first_at[1:]:
        first[offset] = border_backward(at, border_coupling, picked, [offset], [BF16], n_row)[0]
    offsets = later_at + [0]
    rest = dict(zip(offsets, border_backward(at, border_coupling, picked, offsets, [F32] * len(offsets), n_row)))
    pulled = scatter_row(first, rest, rest[0], n_row).astype(BF16)
    found = gather_row(pulled, n_row)
    early, last = found[:-1], found[-1:]
    partial = pivot_products(
        at, pivot_inverse, early, n_row, across, lambda t, i: [i - t], [block], [inner]
    )
    front_solution = pivot_products(
        at, pivot_inverse, last, n_row, across, lambda t, p: [p - t], [block], partial, True
    )
    return front_solution[0], root_solution


def solve_plain(n_front, n_row, rhs_front, rhs_root, pivot_inverse, border_coupling, root_inverse, border_map):
    row_at = lax.axis_index("row")
    front_at = lax.axis_index("front")
    width = rhs_front.shape[1]
    inner = dot(pivot_inverse, lax.all_gather(rhs_front, "row", axis=0, tiled=True))
    contrib = dot(border_coupling, lax.all_gather(inner.astype(BF16), "row", axis=0, tiled=True))
    block_local = border_map.shape[1]
    span_rows = root_inverse.shape[1]
    span_blocks = span_rows // BLK
    local_index = border_map[0] - row_at * span_blocks
    select = (local_index[None, :] == jnp.arange(span_blocks, dtype=jnp.int32)[:, None]).astype(F32)
    dense = jnp.einsum(
        "kj,jcn->kcn", select, contrib.reshape(block_local, BLK, width), precision=lax.Precision.HIGHEST
    ).reshape(span_rows, width)
    shares = lax.psum_scatter(dense, "front", scatter_dimension=0, tiled=True)
    own_rhs = lax.dynamic_slice_in_dim(rhs_root, front_at * shares.shape[0], shares.shape[0], 0)
    schur_rhs = lax.all_gather((own_rhs - shares).astype(BF16), "front", axis=0, tiled=True)
    root_solution = lax.psum_scatter(dot(root_inverse, schur_rhs), "row", scatter_dimension=0, tiled=True)
    gathered = lax.all_gather(root_solution.astype(BF16), ("front", "row"), axis=0, tiled=True)
    ranged = lax.dynamic_slice_in_dim(gathered, row_at * span_rows, span_rows, 0)
    picked = jnp.take(ranged.reshape(span_blocks, BLK, width), local_index, axis=0)
    picked = picked.reshape(block_local * BLK, width)
    pulled = lax.psum_scatter(
        dot(border_coupling, picked, ((0,), (0,))), "row", scatter_dimension=0, tiled=True
    ).astype(BF16)
    correction = dot(pivot_inverse, lax.all_gather(pulled, "row", axis=0, tiled=True))
    return inner - correction, root_solution


def solution(mesh):
    in_specs = (
        P(("front", "row"), None),
        P("row", None),
        P(("front", "row"), None),
        P(("front", "row"), None),
        P("front", "row"),
        P("front", "row"),
    )
    out_specs = (P(("front", "row"), None), P(("front", "row"), None))
    n_front, n_row = mesh.shape["front"], mesh.shape["row"]

    def per_device(*arrays):
        root_inverse, width = arrays[4], arrays[0].shape[1]
        fits = (
            n_front == 8
            and n_front == 2 * n_row
            and root_inverse.shape[1] % (n_front * BLK) == 0
            and root_inverse.shape[0] == n_row * (root_inverse.shape[1] // n_front)
            and root_inverse.shape[1] % (n_front * n_row * 16) == 0
            and arrays[2].shape[1] % (n_row * BLK) == 0
            and width % BLK == 0
        )
        if not fits:
            return solve_plain(n_front, n_row, *arrays)
        cut = width * 2 // 3 // BLK * BLK
        parts = [
            solve(n_front, n_row, arrays[0][:, low:high], arrays[1][:, low:high], *arrays[2:])
            for low, high in ((0, cut), (cut, width))
            if high > low
        ]
        return tuple(jnp.concatenate(outs, axis=1) for outs in zip(*parts))

    return jax.shard_map(per_device, mesh=mesh, in_specs=in_specs, out_specs=out_specs, check_vma=False)
```

```python
import math

import jax
import jax.numpy as jnp
from jax import lax
from jax.experimental import pallas as pl
from jax.experimental.pallas import tpu as pltpu
from jax.sharding import PartitionSpec as P

BLK = 128
F32 = jnp.float32
BF16 = jnp.bfloat16
VMEM = pl.BlockSpec(memory_space=pltpu.VMEM)
ANY = pl.BlockSpec(memory_space=pl.ANY)


def dot(a, b, contract=((1,), (0,))):
    return lax.dot_general(a, b, (contract, ((), ())), preferred_element_type=F32)


def in_hbm(x):
    return pltpu.with_memory_space_constraint(x, pltpu.HBM)


def kernel_call(body, outs, scalars, held, placed, scratch, flops, nbytes, final=False, loose=()):
    size = sum(2 * math.prod(s.shape) for s in scratch if s.dtype == BF16)
    single = not isinstance(outs, list)
    out_shape = [o if final else pltpu.VMEM(o.shape, o.dtype) for o in ([outs] if single else outs)]
    results = pl.pallas_call(
        body,
        out_shape=out_shape,
        grid_spec=pltpu.PrefetchScalarGridSpec(
            num_scalar_prefetch=len(scalars),
            grid=(1,),
            in_specs=[VMEM] * (len(held) + len(loose)) + [ANY] * len(placed),
            out_specs=[VMEM] * len(out_shape),
            scratch_shapes=scratch,
        ),
        compiler_params=pltpu.CompilerParams(vmem_limit_bytes=size + 12 * 1024 * 1024),
        cost_estimate=pl.CostEstimate(flops=flops, bytes_accessed=nbytes, transcendentals=0),
    )(*scalars, *[pltpu.with_memory_space_constraint(x, pltpu.VMEM) for x in held], *loose, *placed)
    return results[0] if single else results


def shift(x, size, by):
    return lax.ppermute(x, "row", [(i, (i + by) % size) for i in range(size)])


def swap(x, size, by):
    return lax.ppermute(x, "front", [(i, i ^ by) for i in range(size)])


def gather_row(x, n):
    found = [(0, x)]
    up, down = x, x
    for step in range(1, n // 2 + 1):
        up = shift(up, n, 1)
        found.append((-step, up))
        if step < n - step:
            down = shift(down, n, -1)
            found.append((step, down))
    return found


def gather_front(low, high, n):
    rows = low.shape[0]
    x_high, y_low = swap(high, n, 2), swap(low, n, 4)
    own, low, high = regroup(low, high)
    x_low, y_high = swap(low, n, 2), swap(high, n, 4)
    corner_low, corner_high = swap(y_low, n, 2), swap(x_high, n, 4)
    sides = stack([x_low, x_high, y_low, y_high, corner_low, corner_high])
    found = []
    for core, block, others in ((0, own, sides), (1, swap(own, n, 1), swap(sides, n, 1))):
        found.append((0, core, 0, 2 * rows, block))
        found += [(chip, core, (chip - 1) * 2 * rows, 2 * rows, others) for chip in (1, 2, 3)]
    return found


def to_plane(x, n):
    rows = x.shape[0] // n
    moved = []
    for k in range(n):
        quarter = x[k * rows : (k + 1) * rows]
        if k:
            quarter = swap(quarter, 2 * n, 2 * k)
        perm = [
            ((chip * 2 + core) * n + row, (row * 2 + core) * n + (chip ^ k))
            for chip in range(n)
            for core in range(2)
            for row in range(n)
        ]
        moved.append(lax.ppermute(quarter, ("front", "row"), perm))
    half = n // 2
    return [jnp.concatenate(some, axis=0) for some in (moved[:half], moved[half:])]


def far_offsets(n):
    first = [-(n // 2)] + ([(n - 1) // 2] if n > 2 else [])
    later = [o for o in range(-(n // 2) + 1, (n - 1) // 2) if o]
    return first, later


def scatter_row(first, later, own, n):
    total = own
    for sign, far in ((-1, n // 2), (1, (n - 1) // 2)):
        running = None
        for step in range(far, 0, -1):
            if running is None:
                running = first[sign * step]
            else:
                running = (running.astype(F32) + later[sign * step]).astype(BF16)
            running = shift(running, n, sign)
        if running is not None:
            total = total + running.astype(F32)
    return total


def owner(at_ref, offset, n_row):
    return lax.rem(at_ref[0] + (offset + n_row), n_row)


def products(at_ref, a_ref, rows, offsets, x_refs, n_row, contract):
    depth = a_ref.shape[1] // n_row
    total = None
    for offset, x_ref in zip(offsets, x_refs):
        columns = pl.ds(pl.multiple_of(owner(at_ref, offset, n_row) * depth, depth), depth)
        part = dot(a_ref[rows, columns], x_ref[...], contract)
        total = part if total is None else total + part
    return total


def pivot_products(at, pivot, found, n_row, contract, finish, outs, extra=(), final=False):
    count = len(found)
    offsets = [o for o, _ in found]

    def body(at_ref, a_ref, *refs):
        extras, x_refs = refs[: len(extra)], refs[len(extra) : len(extra) + count]
        total = products(at_ref, a_ref, slice(None), offsets, x_refs, n_row, contract)
        for ref, value in zip(refs[count + len(extra) :], finish(total, *[e[...] for e in extras])):
            ref[...] = value

    share = 2 * pivot.size * count // n_row
    held = [pivot] + list(extra)
    blocks = [x for _, x in found]
    return kernel_call(body, outs, [at], held, [], [], share * outs[0].shape[1], share, final, blocks)


def border_tile(rows):
    return BLK * next(k for k in (4, 3, 2, 1) if rows // BLK % k == 0)


def border_partial(at, coupling, found, n_row, partial, source, fetch_rows):
    rows, count, width = coupling.shape[0], len(found), found[0][1].shape[1]
    offsets = [o for o, _ in found]
    tile = border_tile(rows)
    held = [coupling] + [x for _, x in found] + ([] if partial is None else [partial])

    def body(at_ref, a_ref, *refs):
        source_hbm, out_ref, own_ref, sem = refs[-4:]
        if fetch_rows < source.shape[0]:
            source_hbm = source_hbm.at[pl.ds(pl.multiple_of(at_ref[1] * fetch_rows, fetch_rows), fetch_rows)]
        copy = pltpu.make_async_copy(source_hbm, own_ref, sem)
        copy.start()

        @pl.loop(0, rows // tile)
        def _(i):
            place = pl.ds(pl.multiple_of(i * tile, tile), tile)
            total = products(at_ref, a_ref, place, offsets, refs[:count], n_row, ((1,), (0,)))
            out_ref[place, :] = total if partial is None else refs[count][place, :] + total

        copy.wait()

    share = 2 * coupling.size * count // n_row
    outs = [
        jax.ShapeDtypeStruct((rows, width), F32),
        jax.ShapeDtypeStruct((fetch_rows, source.shape[1]), source.dtype),
    ]
    scratch = [pltpu.SemaphoreType.DMA]
    return kernel_call(body, outs, [at], held, [in_hbm(source)], scratch, share * width, share)


def border_scatter(at, local_index, coupling, found, partial, n_row, n_front, span_rows):
    rows, count, width = coupling.shape[0], len(found), found[0][1].shape[1]
    offsets = [o for o, _ in found]
    tile = border_tile(rows)
    piece_blocks = span_rows // n_front // BLK

    def body(at_ref, index_ref, a_ref, *refs):
        partial_ref, send_ref, keep_ref = refs[count:]
        send_ref[...] = jnp.zeros_like(send_ref)
        keep_ref[...] = jnp.zeros_like(keep_ref)

        @pl.loop(0, rows // tile)
        def _(i):
            place = pl.ds(pl.multiple_of(i * tile, tile), tile)
            total = products(at_ref, a_ref, place, offsets, refs[:count], n_row, ((1,), (0,)))
            total = (partial_ref[place, :] + total).astype(BF16)
            for j in range(tile // BLK):
                target = index_ref[i * (tile // BLK) + j]
                there = lax.div(target, piece_blocks)
                chip = lax.shift_right_logical(lax.bitwise_xor(there, at_ref[1]), 1)
                slot = chip * piece_blocks + lax.rem(target, piece_blocks)
                goal = pl.ds(pl.multiple_of(slot * BLK, BLK), BLK)
                block = total[j * BLK : (j + 1) * BLK]
                away = lax.rem(there + at_ref[1], 2)

                @pl.when(away == 1)
                def _():
                    send_ref[goal, :] = block

                @pl.when(away == 0)
                def _():
                    keep_ref[goal, :] = block

    half = jax.ShapeDtypeStruct((span_rows // 2, width), BF16)
    share = 2 * coupling.size * count // n_row
    held = [coupling] + [x for _, x in found] + [partial]
    return kernel_call(body, [half, half], [at, local_index], held, [], [], share * width, share)


def added(*parts):
    total = parts[0].astype(F32)
    for part in parts[1:]:
        total = total + part.astype(F32)
    return total


def sum_halves(keep, came, halves):
    rows, width = keep.shape[0] // 8, keep.shape[1]
    outs = [jax.ShapeDtypeStruct((rows, width), BF16)] * len(halves)

    def body(keep_ref, came_ref, *out_refs):
        for (chip, which), out_ref in zip(halves, out_refs):
            place = slice((2 * chip + which) * rows, (2 * chip + which + 1) * rows)
            out_ref[...] = added(keep_ref[place, :], came_ref[place, :]).astype(BF16)

    return kernel_call(body, outs, [], [keep, came], [], [], keep.size, keep.size)


def sum_relayed(keep, came, low, high):
    rows, width = low.shape

    def body(keep_ref, came_ref, low_ref, high_ref, x_ref, y_ref):
        for half, add_ref, out_ref in ((3, high_ref, x_ref), (4, low_ref, y_ref)):
            place = slice(half * rows, (half + 1) * rows)
            out_ref[...] = added(keep_ref[place, :], came_ref[place, :], add_ref[...]).astype(BF16)

    outs = [jax.ShapeDtypeStruct((rows, width), BF16)] * 2
    return kernel_call(body, outs, [], [keep, came, low, high], [], [], 2 * keep.size, 2 * keep.size)


def own_part(own_rhs, keep, came, low, high):
    half, width = own_rhs.shape[0] // 2, own_rhs.shape[1]

    def body(rhs_ref, keep_ref, came_ref, *refs):
        *add_refs, low_ref, high_ref = refs
        for start, adds, out_ref in ((0, add_refs[:2], low_ref), (half, add_refs[2:], high_ref)):
            place = slice(start, start + half)
            total = added(keep_ref[place, :], came_ref[place, :], *[ref[...] for ref in adds])
            out_ref[...] = (rhs_ref[place, :] - total).astype(BF16)

    outs = [jax.ShapeDtypeStruct((half, width), BF16)] * 2
    return kernel_call(body, outs, [], [own_rhs, keep, came, *low, *high], [], [], keep.size, keep.size)


def stack(blocks):
    rows, width = blocks[0].shape

    def body(*refs):
        for i, ref in enumerate(refs[:-1]):
            refs[-1][i * rows : (i + 1) * rows, :] = ref[...]

    out = jax.ShapeDtypeStruct((len(blocks) * rows, width), BF16)
    return kernel_call(body, out, [], blocks, [], [], 0, 4 * len(blocks) * rows * width)


def regroup(low, high):
    rows, width = low.shape

    def body(low_ref, high_ref, whole_ref, low_out_ref, high_out_ref):
        for start, half_ref, out_ref in ((0, low_ref, low_out_ref), (rows, high_ref, high_out_ref)):
            out_ref[...] = half_ref[...]
            whole_ref[start : start + rows, :] = half_ref[...]

    outs = [jax.ShapeDtypeStruct((n * rows, width), BF16) for n in (2, 1, 1)]
    return kernel_call(body, outs, [], [low, high], [], [], 0, 8 * low.size)


def assemble(pieces, piece_refs, target_ref, sems, base):
    copies = []
    for (chip, core, row, rows, _), ref in zip(pieces, piece_refs):
        place = pl.ds(pl.multiple_of(base(2 * chip + core), rows), rows)
        source = ref.at[pl.ds(row, rows)]
        copies.append(pltpu.make_async_copy(source, target_ref.at[place], sems.at[len(copies)]))
    return copies


def root_products(at, inverse, pieces, offsets, kinds, n_row, n_front):
    span_rows = inverse.shape[1]
    rows = inverse.shape[0] // n_row
    width = pieces[0][-1].shape[1]
    piece_rows = span_rows // n_front
    count, many = len(offsets), len(pieces)

    def body(at_ref, a_ref, *refs):
        piece_refs, out_refs, (x_ref, sems) = refs[:many], refs[many : many + count], refs[many + count :]
        copies = assemble(
            pieces, piece_refs, x_ref, sems, lambda d: lax.bitwise_xor(at_ref[1], d) * piece_rows
        )
        for copy in copies:
            copy.start()
        for copy in copies:
            copy.wait()
        for offset, out_ref in zip(offsets, out_refs):
            place = pl.ds(pl.multiple_of(owner(at_ref, offset, n_row) * rows, rows), rows)
            out_ref[...] = dot(a_ref[place, :], x_ref[...]).astype(out_ref.dtype)

    outs = [jax.ShapeDtypeStruct((rows, width), kind) for kind in kinds]
    scratch = [pltpu.VMEM((span_rows, width), BF16), pltpu.SemaphoreType.DMA((many,))]
    share = 2 * rows * span_rows * count
    held = [inverse] + [block for *_, block in pieces]
    return kernel_call(body, outs, [at], held, [], scratch, share * width, share)


def border_pick(at, local_index, coupling, pieces, offset, n_row, n_front):
    rows, depth = coupling.shape[0], coupling.shape[1] // n_row
    piece_rows, width = pieces[0][-1].shape
    span_rows = piece_rows * n_front
    many = len(pieces)

    def body(at_ref, index_ref, a_ref, *refs):
        piece_refs, (out_ref, picked_ref, span_ref, sems) = refs[:many], refs[many:]

        def base(d):
            there = lax.bitwise_xor(at_ref[1], d)
            return lax.rem(there, 2) * (span_rows // 2) + lax.shift_right_logical(there, 1) * piece_rows

        copies = assemble(pieces, piece_refs, span_ref, sems, base)
        for copy in copies:
            copy.start()
        for copy in copies:
            copy.wait()
        for j in range(rows // BLK):
            source = pl.ds(pl.multiple_of(index_ref[j] * BLK, BLK), BLK)
            picked_ref[:, pl.ds(j * BLK, BLK)] = jnp.transpose(span_ref[source, :])
        columns = pl.ds(pl.multiple_of(owner(at_ref, offset, n_row) * depth, depth), depth)
        out_ref[...] = dot(picked_ref[...], a_ref[:, columns]).astype(BF16)

    outs = [jax.ShapeDtypeStruct((width, depth), BF16), jax.ShapeDtypeStruct((width, rows), BF16)]
    scratch = [pltpu.VMEM((span_rows, width), BF16), pltpu.SemaphoreType.DMA((many,))]
    share = 2 * rows * depth
    held = [coupling] + [block for *_, block in pieces]
    return kernel_call(body, outs, [at, local_index], held, [], scratch, share * width, share)


def border_backward(at, coupling, picked, offsets, kinds, n_row):
    rows, depth = coupling.shape[0], coupling.shape[1] // n_row
    width, count = picked.shape[0], len(offsets)

    def body(at_ref, x_ref, a_ref, *out_refs):
        for offset, out_ref in zip(offsets, out_refs):
            columns = pl.ds(pl.multiple_of(owner(at_ref, offset, n_row) * depth, depth), depth)
            out_ref[...] = dot(x_ref[...], a_ref[:, columns]).astype(out_ref.dtype)

    outs = [jax.ShapeDtypeStruct((width, depth), kind) for kind in kinds]
    share = 2 * rows * depth * count
    return kernel_call(body, outs, [at], [picked, coupling], [], [], share * width, share)


def solve(n_front, n_row, rhs_front, rhs_root, pivot_inverse, border_coupling, root_inverse, border_map):
    row_at = lax.axis_index("row").astype(jnp.int32)
    front_at = lax.axis_index("front").astype(jnp.int32)
    at = jnp.stack([row_at, front_at])
    span_rows = root_inverse.shape[1]
    piece_rows, width = span_rows // n_front, rhs_front.shape[1]
    local_index = border_map[0] - row_at * (span_rows // BLK)
    first_at, later_at = far_offsets(n_row)
    block = jax.ShapeDtypeStruct((pivot_inverse.shape[0], width), F32)
    half = jax.ShapeDtypeStruct(block.shape, BF16)
    straight, across = ((1,), (0,)), ((1,), (1,))

    found = gather_row(rhs_front, n_row)
    early, last = found[:-1], found[-1:]
    partial = pivot_products(at, pivot_inverse, early, n_row, straight, lambda t: [t], [block])
    inner, inner_half = pivot_products(
        at,
        pivot_inverse,
        last,
        n_row,
        straight,
        lambda t, p: [t + p, (t + p).astype(BF16)],
        [block, half],
        partial,
    )
    found = gather_row(inner_half, n_row)
    partial, own_rhs = border_partial(at, border_coupling, found[:2], n_row, None, rhs_root, piece_rows)
    partial, inverse = border_partial(
        at, border_coupling, found[2:-1], n_row, partial, root_inverse, root_inverse.shape[0]
    )
    send, keep = border_scatter(
        at, local_index, border_coupling, found[-1:], partial, n_row, n_front, span_rows
    )
    came = swap(send, n_front, 1)
    low, high = sum_halves(keep, came, [(3, 0), (3, 1)])
    low, high = swap(low, n_front, 2), swap(high, n_front, 4)
    x_low, y_high = sum_halves(keep, came, [(1, 0), (2, 1)])
    x_low, y_high = swap(x_low, n_front, 2), swap(y_high, n_front, 4)
    x_high, y_low = sum_relayed(keep, came, low, high)
    x_high, y_low = swap(x_high, n_front, 2), swap(y_low, n_front, 4)
    pieces = gather_front(*own_part(own_rhs, keep, came, (x_low, y_low), (x_high, y_high)), n_front)

    def root(offsets, kind):
        outs = root_products(at, inverse, pieces, offsets, [kind] * len(offsets), n_row, n_front)
        return dict(zip(offsets, outs))

    first = {}
    for offset in first_at:
        first.update(root([offset], BF16))
    rest = root(later_at + [0], F32)
    root_solution = scatter_row(first, rest, rest[0], n_row)
    spans = gather_front(*to_plane(root_solution.astype(BF16), n_row), n_front)

    out, picked = border_pick(at, local_index, border_coupling, spans, first_at[0], n_row, n_front)
    first = {first_at[0]: out}
    for offset in first_at[1:]:
        first[offset] = border_backward(at, border_coupling, picked, [offset], [BF16], n_row)[0]
    offsets = later_at + [0]
    rest = dict(zip(offsets, border_backward(at, border_coupling, picked, offsets, [F32] * len(offsets), n_row)))
    pulled = scatter_row(first, rest, rest[0], n_row).astype(BF16)
    found = gather_row(pulled, n_row)
    early, last = found[:-1], found[-1:]
    partial = pivot_products(
        at, pivot_inverse, early, n_row, across, lambda t, i: [i - t], [block], [inner]
    )
    front_solution = pivot_products(
        at, pivot_inverse, last, n_row, across, lambda t, p: [p - t], [block], partial, True
    )
    return front_solution[0], root_solution


def solve_plain(n_front, n_row, rhs_front, rhs_root, pivot_inverse, border_coupling, root_inverse, border_map):
    row_at = lax.axis_index("row")
    front_at = lax.axis_index("front")
    width = rhs_front.shape[1]
    inner = dot(pivot_inverse, lax.all_gather(rhs_front, "row", axis=0, tiled=True))
    contrib = dot(border_coupling, lax.all_gather(inner.astype(BF16), "row", axis=0, tiled=True))
    block_local = border_map.shape[1]
    span_rows = root_inverse.shape[1]
    span_blocks = span_rows // BLK
    local_index = border_map[0] - row_at * span_blocks
    select = (local_index[None, :] == jnp.arange(span_blocks, dtype=jnp.int32)[:, None]).astype(F32)
    dense = jnp.einsum(
        "kj,jcn->kcn", select, contrib.reshape(block_local, BLK, width), precision=lax.Precision.HIGHEST
    ).reshape(span_rows, width)
    shares = lax.psum_scatter(dense, "front", scatter_dimension=0, tiled=True)
    own_rhs = lax.dynamic_slice_in_dim(rhs_root, front_at * shares.shape[0], shares.shape[0], 0)
    schur_rhs = lax.all_gather((own_rhs - shares).astype(BF16), "front", axis=0, tiled=True)
    root_solution = lax.psum_scatter(dot(root_inverse, schur_rhs), "row", scatter_dimension=0, tiled=True)
    gathered = lax.all_gather(root_solution.astype(BF16), ("front", "row"), axis=0, tiled=True)
    ranged = lax.dynamic_slice_in_dim(gathered, row_at * span_rows, span_rows, 0)
    picked = jnp.take(ranged.reshape(span_blocks, BLK, width), local_index, axis=0)
    picked = picked.reshape(block_local * BLK, width)
    pulled = lax.psum_scatter(
        dot(border_coupling, picked, ((0,), (0,))), "row", scatter_dimension=0, tiled=True
    ).astype(BF16)
    correction = dot(pivot_inverse, lax.all_gather(pulled, "row", axis=0, tiled=True))
    return inner - correction, root_solution


def solution(mesh):
    in_specs = (
        P(("front", "row"), None),
        P("row", None),
        P(("front", "row"), None),
        P(("front", "row"), None),
        P("front", "row"),
        P("front", "row"),
    )
    out_specs = (P(("front", "row"), None), P(("front", "row"), None))
    n_front, n_row = mesh.shape["front"], mesh.shape["row"]

    def per_device(*arrays):
        root_inverse, width = arrays[4], arrays[0].shape[1]
        fits = (
            n_front == 8
            and n_front == 2 * n_row
            and root_inverse.shape[1] % (n_front * BLK) == 0
            and root_inverse.shape[0] == n_row * (root_inverse.shape[1] // n_front)
            and root_inverse.shape[1] % (n_front * n_row * 16) == 0
            and arrays[2].shape[1] % (n_row * BLK) == 0
            and width % BLK == 0
        )
        return (solve if fits else solve_plain)(n_front, n_row, *arrays)

    return jax.shard_map(per_device, mesh=mesh, in_specs=in_specs, out_specs=out_specs, check_vma=False)
```

```python
import math

import jax
import jax.numpy as jnp
from jax import lax
from jax.experimental import pallas as pl
from jax.experimental.pallas import tpu as pltpu
from jax.sharding import PartitionSpec as P

BLK = 128
F32 = jnp.float32
BF16 = jnp.bfloat16
VMEM = pl.BlockSpec(memory_space=pltpu.VMEM)
ANY = pl.BlockSpec(memory_space=pl.ANY)


def dot(a, b, contract=((1,), (0,))):
    return lax.dot_general(a, b, (contract, ((), ())), preferred_element_type=F32)


def in_hbm(x):
    return pltpu.with_memory_space_constraint(x, pltpu.HBM)


def kernel_call(body, outs, scalars, held, placed, scratch, flops, nbytes, final=False, loose=()):
    size = sum(2 * math.prod(s.shape) for s in scratch if s.dtype == BF16)
    single = not isinstance(outs, list)
    out_shape = [o if final else pltpu.VMEM(o.shape, o.dtype) for o in ([outs] if single else outs)]
    results = pl.pallas_call(
        body,
        out_shape=out_shape,
        grid_spec=pltpu.PrefetchScalarGridSpec(
            num_scalar_prefetch=len(scalars),
            grid=(1,),
            in_specs=[VMEM] * (len(held) + len(loose)) + [ANY] * len(placed),
            out_specs=[VMEM] * len(out_shape),
            scratch_shapes=scratch,
        ),
        compiler_params=pltpu.CompilerParams(vmem_limit_bytes=size + 12 * 1024 * 1024),
        cost_estimate=pl.CostEstimate(flops=flops, bytes_accessed=nbytes, transcendentals=0),
    )(*scalars, *[pltpu.with_memory_space_constraint(x, pltpu.VMEM) for x in held], *loose, *placed)
    return results[0] if single else results


def shift(x, size, by):
    return lax.ppermute(x, "row", [(i, (i + by) % size) for i in range(size)])


def swap(x, size, by):
    return lax.ppermute(x, "front", [(i, i ^ by) for i in range(size)])


def gather_row(x, n):
    found = [(0, x)]
    up, down = x, x
    for step in range(1, n // 2 + 1):
        up = shift(up, n, 1)
        found.append((-step, up))
        if step < n - step:
            down = shift(down, n, -1)
            found.append((step, down))
    return found


def gather_front(low, high, n):
    rows = low.shape[0]
    x_high, y_low = swap(high, n, 2), swap(low, n, 4)
    low, high = again(low, high)
    x_low, y_high = swap(low, n, 2), swap(high, n, 4)
    corner_low, corner_high = swap(y_low, n, 2), swap(x_high, n, 4)
    mine = stack([low, high, x_low, x_high, y_low, y_high, corner_low, corner_high])
    return [
        (chip, core, chip * 2 * rows, 2 * rows, blocks)
        for core, blocks in ((0, mine), (1, swap(mine, n, 1)))
        for chip in range(4)
    ]


def to_plane(x, n):
    rows = x.shape[0] // n
    moved = []
    for k in range(n):
        quarter = x[k * rows : (k + 1) * rows]
        if k:
            quarter = swap(quarter, 2 * n, 2 * k)
        perm = [
            ((chip * 2 + core) * n + row, (row * 2 + core) * n + (chip ^ k))
            for chip in range(n)
            for core in range(2)
            for row in range(n)
        ]
        moved.append(lax.ppermute(quarter, ("front", "row"), perm))
    half = n // 2
    return [jnp.concatenate(some, axis=0) for some in (moved[:half], moved[half:])]


def far_offsets(n):
    first = [-(n // 2)] + ([(n - 1) // 2] if n > 2 else [])
    later = [o for o in range(-(n // 2) + 1, (n - 1) // 2) if o]
    return first, later


def scatter_row(first, later, own, n):
    total = own
    for sign, far in ((-1, n // 2), (1, (n - 1) // 2)):
        running = None
        for step in range(far, 0, -1):
            if running is None:
                running = first[sign * step]
            else:
                running = (running.astype(F32) + later[sign * step]).astype(BF16)
            running = shift(running, n, sign)
        if running is not None:
            total = total + running.astype(F32)
    return total


def owner(at_ref, offset, n_row):
    return lax.rem(at_ref[0] + (offset + n_row), n_row)


def products(at_ref, a_ref, rows, offsets, x_refs, n_row, contract):
    depth = a_ref.shape[1] // n_row
    total = None
    for offset, x_ref in zip(offsets, x_refs):
        columns = pl.ds(pl.multiple_of(owner(at_ref, offset, n_row) * depth, depth), depth)
        part = dot(a_ref[rows, columns], x_ref[...], contract)
        total = part if total is None else total + part
    return total


def pivot_products(at, pivot, found, n_row, contract, finish, outs, extra=(), final=False):
    count = len(found)
    offsets = [o for o, _ in found]

    def body(at_ref, a_ref, *refs):
        extras, x_refs = refs[: len(extra)], refs[len(extra) : len(extra) + count]
        total = products(at_ref, a_ref, slice(None), offsets, x_refs, n_row, contract)
        for ref, value in zip(refs[count + len(extra) :], finish(total, *[e[...] for e in extras])):
            ref[...] = value

    share = 2 * pivot.size * count // n_row
    held = [pivot] + list(extra)
    blocks = [x for _, x in found]
    return kernel_call(body, outs, [at], held, [], [], share * outs[0].shape[1], share, final, blocks)


def border_tile(rows):
    return BLK * next(k for k in (4, 3, 2, 1) if rows // BLK % k == 0)


def border_partial(at, coupling, found, n_row, partial, source, fetch_rows):
    rows, count, width = coupling.shape[0], len(found), found[0][1].shape[1]
    offsets = [o for o, _ in found]
    tile = border_tile(rows)
    held = [coupling] + [x for _, x in found] + ([] if partial is None else [partial])

    def body(at_ref, a_ref, *refs):
        source_hbm, out_ref, own_ref, sem = refs[-4:]
        if fetch_rows < source.shape[0]:
            source_hbm = source_hbm.at[pl.ds(pl.multiple_of(at_ref[1] * fetch_rows, fetch_rows), fetch_rows)]
        copy = pltpu.make_async_copy(source_hbm, own_ref, sem)
        copy.start()

        @pl.loop(0, rows // tile)
        def _(i):
            place = pl.ds(pl.multiple_of(i * tile, tile), tile)
            total = products(at_ref, a_ref, place, offsets, refs[:count], n_row, ((1,), (0,)))
            out_ref[place, :] = total if partial is None else refs[count][place, :] + total

        copy.wait()

    share = 2 * coupling.size * count // n_row
    outs = [
        jax.ShapeDtypeStruct((rows, width), F32),
        jax.ShapeDtypeStruct((fetch_rows, source.shape[1]), source.dtype),
    ]
    scratch = [pltpu.SemaphoreType.DMA]
    return kernel_call(body, outs, [at], held, [in_hbm(source)], scratch, share * width, share)


def border_scatter(at, local_index, coupling, found, partial, n_row, n_front, span_rows):
    rows, count, width = coupling.shape[0], len(found), found[0][1].shape[1]
    offsets = [o for o, _ in found]
    tile = border_tile(rows)
    piece_blocks = span_rows // n_front // BLK

    def body(at_ref, index_ref, a_ref, *refs):
        partial_ref, send_ref, keep_ref = refs[count:]
        send_ref[...] = jnp.zeros_like(send_ref)
        keep_ref[...] = jnp.zeros_like(keep_ref)

        @pl.loop(0, rows // tile)
        def _(i):
            place = pl.ds(pl.multiple_of(i * tile, tile), tile)
            total = products(at_ref, a_ref, place, offsets, refs[:count], n_row, ((1,), (0,)))
            total = (partial_ref[place, :] + total).astype(BF16)
            for j in range(tile // BLK):
                target = index_ref[i * (tile // BLK) + j]
                there = lax.div(target, piece_blocks)
                chip = lax.shift_right_logical(lax.bitwise_xor(there, at_ref[1]), 1)
                slot = chip * piece_blocks + lax.rem(target, piece_blocks)
                goal = pl.ds(pl.multiple_of(slot * BLK, BLK), BLK)
                block = total[j * BLK : (j + 1) * BLK]
                away = lax.rem(there + at_ref[1], 2)

                @pl.when(away == 1)
                def _():
                    send_ref[goal, :] = block

                @pl.when(away == 0)
                def _():
                    keep_ref[goal, :] = block

    half = jax.ShapeDtypeStruct((span_rows // 2, width), BF16)
    share = 2 * coupling.size * count // n_row
    held = [coupling] + [x for _, x in found] + [partial]
    return kernel_call(body, [half, half], [at, local_index], held, [], [], share * width, share)


def added(*parts):
    total = parts[0].astype(F32)
    for part in parts[1:]:
        total = total + part.astype(F32)
    return total


def sum_halves(keep, came, halves):
    rows, width = keep.shape[0] // 8, keep.shape[1]
    outs = [jax.ShapeDtypeStruct((rows, width), BF16)] * len(halves)

    def body(keep_ref, came_ref, *out_refs):
        for (chip, which), out_ref in zip(halves, out_refs):
            place = slice((2 * chip + which) * rows, (2 * chip + which + 1) * rows)
            out_ref[...] = added(keep_ref[place, :], came_ref[place, :]).astype(BF16)

    return kernel_call(body, outs, [], [keep, came], [], [], keep.size, keep.size)


def sum_relayed(keep, came, low, high):
    rows, width = low.shape

    def body(keep_ref, came_ref, low_ref, high_ref, x_ref, y_ref):
        for half, add_ref, out_ref in ((3, high_ref, x_ref), (4, low_ref, y_ref)):
            place = slice(half * rows, (half + 1) * rows)
            out_ref[...] = added(keep_ref[place, :], came_ref[place, :], add_ref[...]).astype(BF16)

    outs = [jax.ShapeDtypeStruct((rows, width), BF16)] * 2
    return kernel_call(body, outs, [], [keep, came, low, high], [], [], 2 * keep.size, 2 * keep.size)


def own_part(own_rhs, keep, came, low, high):
    half, width = own_rhs.shape[0] // 2, own_rhs.shape[1]

    def body(rhs_ref, keep_ref, came_ref, *refs):
        *add_refs, low_ref, high_ref = refs
        for start, adds, out_ref in ((0, add_refs[:2], low_ref), (half, add_refs[2:], high_ref)):
            place = slice(start, start + half)
            total = added(keep_ref[place, :], came_ref[place, :], *[ref[...] for ref in adds])
            out_ref[...] = (rhs_ref[place, :] - total).astype(BF16)

    outs = [jax.ShapeDtypeStruct((half, width), BF16)] * 2
    return kernel_call(body, outs, [], [own_rhs, keep, came, *low, *high], [], [], keep.size, keep.size)


def stack(blocks):
    rows, width = blocks[0].shape

    def body(*refs):
        for i, ref in enumerate(refs[:-1]):
            refs[-1][i * rows : (i + 1) * rows, :] = ref[...]

    out = jax.ShapeDtypeStruct((len(blocks) * rows, width), BF16)
    return kernel_call(body, out, [], blocks, [], [], 0, 4 * len(blocks) * rows * width)


def again(low, high):
    def body(low_ref, high_ref, low_out_ref, high_out_ref):
        low_out_ref[...] = low_ref[...]
        high_out_ref[...] = high_ref[...]

    outs = [jax.ShapeDtypeStruct(low.shape, BF16)] * 2
    return kernel_call(body, outs, [], [low, high], [], [], 0, 8 * low.size)


def assemble(pieces, piece_refs, target_ref, sems, base):
    copies = []
    for (chip, core, row, rows, _), ref in zip(pieces, piece_refs):
        place = pl.ds(pl.multiple_of(base(2 * chip + core), rows), rows)
        source = ref.at[pl.ds(row, rows)]
        copies.append(pltpu.make_async_copy(source, target_ref.at[place], sems.at[len(copies)]))
    return copies


def root_products(at, inverse, pieces, offsets, kinds, n_row, n_front):
    span_rows = inverse.shape[1]
    rows = inverse.shape[0] // n_row
    width = pieces[0][-1].shape[1]
    piece_rows = span_rows // n_front
    count, many = len(offsets), len(pieces)

    def body(at_ref, a_ref, *refs):
        piece_refs, out_refs, (x_ref, sems) = refs[:many], refs[many : many + count], refs[many + count :]
        copies = assemble(
            pieces, piece_refs, x_ref, sems, lambda d: lax.bitwise_xor(at_ref[1], d) * piece_rows
        )
        for copy in copies:
            copy.start()
        for copy in copies:
            copy.wait()
        for offset, out_ref in zip(offsets, out_refs):
            place = pl.ds(pl.multiple_of(owner(at_ref, offset, n_row) * rows, rows), rows)
            out_ref[...] = dot(a_ref[place, :], x_ref[...]).astype(out_ref.dtype)

    outs = [jax.ShapeDtypeStruct((rows, width), kind) for kind in kinds]
    scratch = [pltpu.VMEM((span_rows, width), BF16), pltpu.SemaphoreType.DMA((many,))]
    share = 2 * rows * span_rows * count
    held = [inverse] + [block for *_, block in pieces]
    return kernel_call(body, outs, [at], held, [], scratch, share * width, share)


def border_pick(at, local_index, coupling, pieces, offset, n_row, n_front):
    rows, depth = coupling.shape[0], coupling.shape[1] // n_row
    piece_rows, width = pieces[0][3], pieces[0][-1].shape[1]
    span_rows = piece_rows * n_front
    many = len(pieces)

    def body(at_ref, index_ref, a_ref, *refs):
        piece_refs, (out_ref, picked_ref, span_ref, sems) = refs[:many], refs[many:]

        def base(d):
            there = lax.bitwise_xor(at_ref[1], d)
            return lax.rem(there, 2) * (span_rows // 2) + lax.shift_right_logical(there, 1) * piece_rows

        copies = assemble(pieces, piece_refs, span_ref, sems, base)
        for copy in copies:
            copy.start()
        for copy in copies:
            copy.wait()
        for j in range(rows // BLK):
            source = pl.ds(pl.multiple_of(index_ref[j] * BLK, BLK), BLK)
            picked_ref[:, pl.ds(j * BLK, BLK)] = jnp.transpose(span_ref[source, :])
        columns = pl.ds(pl.multiple_of(owner(at_ref, offset, n_row) * depth, depth), depth)
        out_ref[...] = dot(picked_ref[...], a_ref[:, columns]).astype(BF16)

    outs = [jax.ShapeDtypeStruct((width, depth), BF16), jax.ShapeDtypeStruct((width, rows), BF16)]
    scratch = [pltpu.VMEM((span_rows, width), BF16), pltpu.SemaphoreType.DMA((many,))]
    share = 2 * rows * depth
    held = [coupling] + [block for *_, block in pieces]
    return kernel_call(body, outs, [at, local_index], held, [], scratch, share * width, share)


def border_backward(at, coupling, picked, offsets, kinds, n_row):
    rows, depth = coupling.shape[0], coupling.shape[1] // n_row
    width, count = picked.shape[0], len(offsets)

    def body(at_ref, x_ref, a_ref, *out_refs):
        for offset, out_ref in zip(offsets, out_refs):
            columns = pl.ds(pl.multiple_of(owner(at_ref, offset, n_row) * depth, depth), depth)
            out_ref[...] = dot(x_ref[...], a_ref[:, columns]).astype(out_ref.dtype)

    outs = [jax.ShapeDtypeStruct((width, depth), kind) for kind in kinds]
    share = 2 * rows * depth * count
    return kernel_call(body, outs, [at], [picked, coupling], [], [], share * width, share)


def solve(n_front, n_row, rhs_front, rhs_root, pivot_inverse, border_coupling, root_inverse, border_map):
    row_at = lax.axis_index("row").astype(jnp.int32)
    front_at = lax.axis_index("front").astype(jnp.int32)
    at = jnp.stack([row_at, front_at])
    span_rows = root_inverse.shape[1]
    piece_rows, width = span_rows // n_front, rhs_front.shape[1]
    local_index = border_map[0] - row_at * (span_rows // BLK)
    first_at, later_at = far_offsets(n_row)
    block = jax.ShapeDtypeStruct((pivot_inverse.shape[0], width), F32)
    half = jax.ShapeDtypeStruct(block.shape, BF16)
    straight, across = ((1,), (0,)), ((1,), (1,))

    found = gather_row(rhs_front, n_row)
    early, last = found[:-1], found[-1:]
    partial = pivot_products(at, pivot_inverse, early, n_row, straight, lambda t: [t], [block])
    inner, inner_half = pivot_products(
        at,
        pivot_inverse,
        last,
        n_row,
        straight,
        lambda t, p: [t + p, (t + p).astype(BF16)],
        [block, half],
        partial,
    )
    found = gather_row(inner_half, n_row)
    partial, own_rhs = border_partial(at, border_coupling, found[:2], n_row, None, rhs_root, piece_rows)
    partial, inverse = border_partial(
        at, border_coupling, found[2:-1], n_row, partial, root_inverse, root_inverse.shape[0]
    )
    send, keep = border_scatter(
        at, local_index, border_coupling, found[-1:], partial, n_row, n_front, span_rows
    )
    came = swap(send, n_front, 1)
    low, high = sum_halves(keep, came, [(3, 0), (3, 1)])
    low, high = swap(low, n_front, 2), swap(high, n_front, 4)
    x_low, y_high = sum_halves(keep, came, [(1, 0), (2, 1)])
    x_low, y_high = swap(x_low, n_front, 2), swap(y_high, n_front, 4)
    x_high, y_low = sum_relayed(keep, came, low, high)
    x_high, y_low = swap(x_high, n_front, 2), swap(y_low, n_front, 4)
    pieces = gather_front(*own_part(own_rhs, keep, came, (x_low, y_low), (x_high, y_high)), n_front)

    def root(offsets, kind):
        outs = root_products(at, inverse, pieces, offsets, [kind] * len(offsets), n_row, n_front)
        return dict(zip(offsets, outs))

    first = {}
    for offset in first_at:
        first.update(root([offset], BF16))
    rest = root(later_at + [0], F32)
    root_solution = scatter_row(first, rest, rest[0], n_row)
    spans = gather_front(*to_plane(root_solution.astype(BF16), n_row), n_front)

    out, picked = border_pick(at, local_index, border_coupling, spans, first_at[0], n_row, n_front)
    first = {first_at[0]: out}
    for offset in first_at[1:]:
        first[offset] = border_backward(at, border_coupling, picked, [offset], [BF16], n_row)[0]
    offsets = later_at + [0]
    rest = dict(zip(offsets, border_backward(at, border_coupling, picked, offsets, [F32] * len(offsets), n_row)))
    pulled = scatter_row(first, rest, rest[0], n_row).astype(BF16)
    found = gather_row(pulled, n_row)
    early, last = found[:-1], found[-1:]
    partial = pivot_products(
        at, pivot_inverse, early, n_row, across, lambda t, i: [i - t], [block], [inner]
    )
    front_solution = pivot_products(
        at, pivot_inverse, last, n_row, across, lambda t, p: [p - t], [block], partial, True
    )
    return front_solution[0], root_solution


def solve_plain(n_front, n_row, rhs_front, rhs_root, pivot_inverse, border_coupling, root_inverse, border_map):
    row_at = lax.axis_index("row")
    front_at = lax.axis_index("front")
    width = rhs_front.shape[1]
    inner = dot(pivot_inverse, lax.all_gather(rhs_front, "row", axis=0, tiled=True))
    contrib = dot(border_coupling, lax.all_gather(inner.astype(BF16), "row", axis=0, tiled=True))
    block_local = border_map.shape[1]
    span_rows = root_inverse.shape[1]
    span_blocks = span_rows // BLK
    local_index = border_map[0] - row_at * span_blocks
    select = (local_index[None, :] == jnp.arange(span_blocks, dtype=jnp.int32)[:, None]).astype(F32)
    dense = jnp.einsum(
        "kj,jcn->kcn", select, contrib.reshape(block_local, BLK, width), precision=lax.Precision.HIGHEST
    ).reshape(span_rows, width)
    shares = lax.psum_scatter(dense, "front", scatter_dimension=0, tiled=True)
    own_rhs = lax.dynamic_slice_in_dim(rhs_root, front_at * shares.shape[0], shares.shape[0], 0)
    schur_rhs = lax.all_gather((own_rhs - shares).astype(BF16), "front", axis=0, tiled=True)
    root_solution = lax.psum_scatter(dot(root_inverse, schur_rhs), "row", scatter_dimension=0, tiled=True)
    gathered = lax.all_gather(root_solution.astype(BF16), ("front", "row"), axis=0, tiled=True)
    ranged = lax.dynamic_slice_in_dim(gathered, row_at * span_rows, span_rows, 0)
    picked = jnp.take(ranged.reshape(span_blocks, BLK, width), local_index, axis=0)
    picked = picked.reshape(block_local * BLK, width)
    pulled = lax.psum_scatter(
        dot(border_coupling, picked, ((0,), (0,))), "row", scatter_dimension=0, tiled=True
    ).astype(BF16)
    correction = dot(pivot_inverse, lax.all_gather(pulled, "row", axis=0, tiled=True))
    return inner - correction, root_solution


def solution(mesh):
    in_specs = (
        P(("front", "row"), None),
        P("row", None),
        P(("front", "row"), None),
        P(("front", "row"), None),
        P("front", "row"),
        P("front", "row"),
    )
    out_specs = (P(("front", "row"), None), P(("front", "row"), None))
    n_front, n_row = mesh.shape["front"], mesh.shape["row"]

    def per_device(*arrays):
        root_inverse, width = arrays[4], arrays[0].shape[1]
        fits = (
            n_front == 8
            and n_front == 2 * n_row
            and root_inverse.shape[1] % (n_front * BLK) == 0
            and root_inverse.shape[0] == n_row * (root_inverse.shape[1] // n_front)
            and root_inverse.shape[1] % (n_front * n_row * 16) == 0
            and arrays[2].shape[1] % (n_row * BLK) == 0
            and width % BLK == 0
        )
        return (solve if fits else solve_plain)(n_front, n_row, *arrays)

    return jax.shard_map(per_device, mesh=mesh, in_specs=in_specs, out_specs=out_specs, check_vma=False)
```

```python
import math

import jax
import jax.numpy as jnp
from jax import lax
from jax.experimental import pallas as pl
from jax.experimental.pallas import tpu as pltpu
from jax.sharding import PartitionSpec as P

BLK = 128
F32 = jnp.float32
BF16 = jnp.bfloat16
VMEM = pl.BlockSpec(memory_space=pltpu.VMEM)
ANY = pl.BlockSpec(memory_space=pl.ANY)


def dot(a, b, contract=((1,), (0,))):
    return lax.dot_general(a, b, (contract, ((), ())), preferred_element_type=F32)


def in_hbm(x):
    return pltpu.with_memory_space_constraint(x, pltpu.HBM)


def kernel_call(body, outs, scalars, held, placed, scratch, flops, nbytes, final=False, loose=()):
    size = sum(2 * math.prod(s.shape) for s in scratch if s.dtype == BF16)
    single = not isinstance(outs, list)
    out_shape = [o if final else pltpu.VMEM(o.shape, o.dtype) for o in ([outs] if single else outs)]
    results = pl.pallas_call(
        body,
        out_shape=out_shape,
        grid_spec=pltpu.PrefetchScalarGridSpec(
            num_scalar_prefetch=len(scalars),
            grid=(1,),
            in_specs=[VMEM] * (len(held) + len(loose)) + [ANY] * len(placed),
            out_specs=[VMEM] * len(out_shape),
            scratch_shapes=scratch,
        ),
        compiler_params=pltpu.CompilerParams(vmem_limit_bytes=size + 12 * 1024 * 1024),
        cost_estimate=pl.CostEstimate(flops=flops, bytes_accessed=nbytes, transcendentals=0),
    )(*scalars, *[pltpu.with_memory_space_constraint(x, pltpu.VMEM) for x in held], *loose, *placed)
    return results[0] if single else results


def shift(x, size, by):
    return lax.ppermute(x, "row", [(i, (i + by) % size) for i in range(size)])


def swap(x, size, by):
    return lax.ppermute(x, "front", [(i, i ^ by) for i in range(size)])


def gather_row(x, n):
    found = [(0, x)]
    up, down = x, x
    for step in range(1, n // 2 + 1):
        up = shift(up, n, 1)
        found.append((-step, up))
        if step < n - step:
            down = shift(down, n, -1)
            found.append((step, down))
    return found


def gather_front(low, high, n):
    x_high, y_low = swap(high, n, 2), swap(low, n, 4)
    low, high = again(low, high)
    x_low, y_high = swap(low, n, 2), swap(high, n, 4)
    corner_low, corner_high = swap(y_low, n, 2), swap(x_high, n, 4)
    mine = stack([low, high, x_low, x_high, y_low, y_high, corner_low, corner_high])
    return mine, swap(mine, n, 1)


def to_plane(x, n):
    rows = x.shape[0] // n
    moved = []
    for k in range(n):
        quarter = x[k * rows : (k + 1) * rows]
        if k:
            quarter = swap(quarter, 2 * n, 2 * k)
        perm = [
            ((chip * 2 + core) * n + row, (row * 2 + core) * n + (chip ^ k))
            for chip in range(n)
            for core in range(2)
            for row in range(n)
        ]
        moved.append(lax.ppermute(quarter, ("front", "row"), perm))
    half = n // 2
    return [jnp.concatenate(some, axis=0) for some in (moved[:half], moved[half:])]


def far_offsets(n):
    first = [-(n // 2)] + ([(n - 1) // 2] if n > 2 else [])
    later = [o for o in range(-(n // 2) + 1, (n - 1) // 2) if o]
    return first, later


def scatter_row(first, later, own, n):
    total = own
    for sign, far in ((-1, n // 2), (1, (n - 1) // 2)):
        running = None
        for step in range(far, 0, -1):
            if running is None:
                running = first[sign * step]
            else:
                running = (running.astype(F32) + later[sign * step]).astype(BF16)
            running = shift(running, n, sign)
        if running is not None:
            total = total + running.astype(F32)
    return total


def owner(at_ref, offset, n_row):
    return lax.rem(at_ref[0] + (offset + n_row), n_row)


def products(at_ref, a_ref, rows, offsets, x_refs, n_row, contract):
    depth = a_ref.shape[1] // n_row
    total = None
    for offset, x_ref in zip(offsets, x_refs):
        columns = pl.ds(pl.multiple_of(owner(at_ref, offset, n_row) * depth, depth), depth)
        part = dot(a_ref[rows, columns], x_ref[...], contract)
        total = part if total is None else total + part
    return total


def pivot_products(at, pivot, found, n_row, contract, finish, outs, extra=(), final=False):
    count = len(found)
    offsets = [o for o, _ in found]

    def body(at_ref, a_ref, *refs):
        extras, x_refs = refs[: len(extra)], refs[len(extra) : len(extra) + count]
        total = products(at_ref, a_ref, slice(None), offsets, x_refs, n_row, contract)
        for ref, value in zip(refs[count + len(extra) :], finish(total, *[e[...] for e in extras])):
            ref[...] = value

    share = 2 * pivot.size * count // n_row
    held = [pivot] + list(extra)
    blocks = [x for _, x in found]
    return kernel_call(body, outs, [at], held, [], [], share * outs[0].shape[1], share, final, blocks)


def border_tile(rows):
    return BLK * next(k for k in (4, 3, 2, 1) if rows // BLK % k == 0)


def border_partial(at, coupling, found, n_row, partial, source, fetch_rows):
    rows, count, width = coupling.shape[0], len(found), found[0][1].shape[1]
    offsets = [o for o, _ in found]
    tile = border_tile(rows)
    held = [coupling] + [x for _, x in found] + ([] if partial is None else [partial])

    def body(at_ref, a_ref, *refs):
        source_hbm, out_ref, own_ref, sem = refs[-4:]
        if fetch_rows < source.shape[0]:
            source_hbm = source_hbm.at[pl.ds(pl.multiple_of(at_ref[1] * fetch_rows, fetch_rows), fetch_rows)]
        copy = pltpu.make_async_copy(source_hbm, own_ref, sem)
        copy.start()

        @pl.loop(0, rows // tile)
        def _(i):
            place = pl.ds(pl.multiple_of(i * tile, tile), tile)
            total = products(at_ref, a_ref, place, offsets, refs[:count], n_row, ((1,), (0,)))
            out_ref[place, :] = total if partial is None else refs[count][place, :] + total

        copy.wait()

    share = 2 * coupling.size * count // n_row
    outs = [
        jax.ShapeDtypeStruct((rows, width), F32),
        jax.ShapeDtypeStruct((fetch_rows, source.shape[1]), source.dtype),
    ]
    scratch = [pltpu.SemaphoreType.DMA]
    return kernel_call(body, outs, [at], held, [in_hbm(source)], scratch, share * width, share)


def border_scatter(at, local_index, coupling, found, partial, n_row, n_front, span_rows):
    rows, count, width = coupling.shape[0], len(found), found[0][1].shape[1]
    offsets = [o for o, _ in found]
    tile = border_tile(rows)
    piece_blocks = span_rows // n_front // BLK

    def body(at_ref, index_ref, a_ref, *refs):
        partial_ref, send_ref, keep_ref = refs[count:]
        send_ref[...] = jnp.zeros_like(send_ref)
        keep_ref[...] = jnp.zeros_like(keep_ref)

        @pl.loop(0, rows // tile)
        def _(i):
            place = pl.ds(pl.multiple_of(i * tile, tile), tile)
            total = products(at_ref, a_ref, place, offsets, refs[:count], n_row, ((1,), (0,)))
            total = (partial_ref[place, :] + total).astype(BF16)
            for j in range(tile // BLK):
                target = index_ref[i * (tile // BLK) + j]
                there = lax.div(target, piece_blocks)
                chip = lax.shift_right_logical(lax.bitwise_xor(there, at_ref[1]), 1)
                slot = chip * piece_blocks + lax.rem(target, piece_blocks)
                goal = pl.ds(pl.multiple_of(slot * BLK, BLK), BLK)
                block = total[j * BLK : (j + 1) * BLK]
                away = lax.rem(there + at_ref[1], 2)

                @pl.when(away == 1)
                def _():
                    send_ref[goal, :] = block

                @pl.when(away == 0)
                def _():
                    keep_ref[goal, :] = block

    half = jax.ShapeDtypeStruct((span_rows // 2, width), BF16)
    share = 2 * coupling.size * count // n_row
    held = [coupling] + [x for _, x in found] + [partial]
    return kernel_call(body, [half, half], [at, local_index], held, [], [], share * width, share)


def added(*parts):
    total = parts[0].astype(F32)
    for part in parts[1:]:
        total = total + part.astype(F32)
    return total


def sum_halves(keep, came, halves):
    rows, width = keep.shape[0] // 8, keep.shape[1]
    outs = [jax.ShapeDtypeStruct((rows, width), BF16)] * len(halves)

    def body(keep_ref, came_ref, *out_refs):
        for (chip, which), out_ref in zip(halves, out_refs):
            place = slice((2 * chip + which) * rows, (2 * chip + which + 1) * rows)
            out_ref[...] = added(keep_ref[place, :], came_ref[place, :]).astype(BF16)

    return kernel_call(body, outs, [], [keep, came], [], [], keep.size, keep.size)


def sum_relayed(keep, came, low, high):
    rows, width = low.shape

    def body(keep_ref, came_ref, low_ref, high_ref, x_ref, y_ref):
        for half, add_ref, out_ref in ((3, high_ref, x_ref), (4, low_ref, y_ref)):
            place = slice(half * rows, (half + 1) * rows)
            out_ref[...] = added(keep_ref[place, :], came_ref[place, :], add_ref[...]).astype(BF16)

    outs = [jax.ShapeDtypeStruct((rows, width), BF16)] * 2
    return kernel_call(body, outs, [], [keep, came, low, high], [], [], 2 * keep.size, 2 * keep.size)


def own_part(own_rhs, keep, came, low, high):
    half, width = own_rhs.shape[0] // 2, own_rhs.shape[1]

    def body(rhs_ref, keep_ref, came_ref, *refs):
        *add_refs, low_ref, high_ref = refs
        for start, adds, out_ref in ((0, add_refs[:2], low_ref), (half, add_refs[2:], high_ref)):
            place = slice(start, start + half)
            total = added(keep_ref[place, :], came_ref[place, :], *[ref[...] for ref in adds])
            out_ref[...] = (rhs_ref[place, :] - total).astype(BF16)

    outs = [jax.ShapeDtypeStruct((half, width), BF16)] * 2
    return kernel_call(body, outs, [], [own_rhs, keep, came, *low, *high], [], [], keep.size, keep.size)


def stack(blocks):
    rows, width = blocks[0].shape

    def body(*refs):
        for i, ref in enumerate(refs[:-1]):
            refs[-1][i * rows : (i + 1) * rows, :] = ref[...]

    out = jax.ShapeDtypeStruct((len(blocks) * rows, width), BF16)
    return kernel_call(body, out, [], blocks, [], [], 0, 4 * len(blocks) * rows * width)


def again(low, high):
    def body(low_ref, high_ref, low_out_ref, high_out_ref):
        low_out_ref[...] = low_ref[...]
        high_out_ref[...] = high_ref[...]

    outs = [jax.ShapeDtypeStruct(low.shape, BF16)] * 2
    return kernel_call(body, outs, [], [low, high], [], [], 0, 8 * low.size)


def root_products(at, inverse, spans, offsets, kinds, n_row, n_front):
    span_rows = inverse.shape[1]
    rows = inverse.shape[0] // n_row
    width = spans[0].shape[1]
    piece_rows = span_rows // n_front
    count = len(offsets)

    def body(at_ref, a_ref, mine_ref, other_ref, *refs):
        out_refs, (x_ref, sems) = refs[:count], refs[count:]
        copies = []
        for core, ref in enumerate((mine_ref, other_ref)):
            for chip in range(n_front // 2):
                start = lax.bitwise_xor(at_ref[1], 2 * chip + core) * piece_rows
                place = pl.ds(pl.multiple_of(start, piece_rows), piece_rows)
                source = ref.at[pl.ds(chip * piece_rows, piece_rows)]
                copies.append(pltpu.make_async_copy(source, x_ref.at[place], sems.at[len(copies)]))
        for copy in copies:
            copy.start()
        for copy in copies:
            copy.wait()
        for offset, out_ref in zip(offsets, out_refs):
            place = pl.ds(pl.multiple_of(owner(at_ref, offset, n_row) * rows, rows), rows)
            out_ref[...] = dot(a_ref[place, :], x_ref[...]).astype(out_ref.dtype)

    outs = [jax.ShapeDtypeStruct((rows, width), kind) for kind in kinds]
    scratch = [pltpu.VMEM((span_rows, width), BF16), pltpu.SemaphoreType.DMA((n_front,))]
    share = 2 * rows * span_rows * count
    return kernel_call(body, outs, [at], [inverse, *spans], [], scratch, share * width, share)


def border_pick(at, local_index, coupling, spans, offset, n_row, n_front):
    rows, depth = coupling.shape[0], coupling.shape[1] // n_row
    (span_rows, width), chips = spans[0].shape, n_front // 2
    piece_blocks = span_rows // chips // BLK

    def body(at_ref, index_ref, a_ref, mine_ref, other_ref, out_ref, picked_ref):
        for j in range(rows // BLK):
            target = index_ref[j]
            core = lax.div(target, chips * piece_blocks)
            within = lax.rem(target, chips * piece_blocks)
            chip = lax.bitwise_xor(lax.div(within, piece_blocks), lax.shift_right_logical(at_ref[1], 1))
            slot = chip * piece_blocks + lax.rem(within, piece_blocks)
            source = pl.ds(pl.multiple_of(slot * BLK, BLK), BLK)
            goal = pl.ds(j * BLK, BLK)
            here = core == lax.rem(at_ref[1], 2)

            @pl.when(here)
            def _():
                picked_ref[:, goal] = jnp.transpose(mine_ref[source, :])

            @pl.when(jnp.logical_not(here))
            def _():
                picked_ref[:, goal] = jnp.transpose(other_ref[source, :])

        columns = pl.ds(pl.multiple_of(owner(at_ref, offset, n_row) * depth, depth), depth)
        out_ref[...] = dot(picked_ref[...], a_ref[:, columns]).astype(BF16)

    outs = [jax.ShapeDtypeStruct((width, depth), BF16), jax.ShapeDtypeStruct((width, rows), BF16)]
    share = 2 * rows * depth
    return kernel_call(body, outs, [at, local_index], [coupling, *spans], [], [], share * width, share)


def border_backward(at, coupling, picked, offsets, kinds, n_row):
    rows, depth = coupling.shape[0], coupling.shape[1] // n_row
    width, count = picked.shape[0], len(offsets)

    def body(at_ref, x_ref, a_ref, *out_refs):
        for offset, out_ref in zip(offsets, out_refs):
            columns = pl.ds(pl.multiple_of(owner(at_ref, offset, n_row) * depth, depth), depth)
            out_ref[...] = dot(x_ref[...], a_ref[:, columns]).astype(out_ref.dtype)

    outs = [jax.ShapeDtypeStruct((width, depth), kind) for kind in kinds]
    share = 2 * rows * depth * count
    return kernel_call(body, outs, [at], [picked, coupling], [], [], share * width, share)


def solve(n_front, n_row, rhs_front, rhs_root, pivot_inverse, border_coupling, root_inverse, border_map):
    row_at = lax.axis_index("row").astype(jnp.int32)
    front_at = lax.axis_index("front").astype(jnp.int32)
    at = jnp.stack([row_at, front_at])
    span_rows = root_inverse.shape[1]
    piece_rows, width = span_rows // n_front, rhs_front.shape[1]
    local_index = border_map[0] - row_at * (span_rows // BLK)
    first_at, later_at = far_offsets(n_row)
    block = jax.ShapeDtypeStruct((pivot_inverse.shape[0], width), F32)
    half = jax.ShapeDtypeStruct(block.shape, BF16)
    straight, across = ((1,), (0,)), ((1,), (1,))

    found = gather_row(rhs_front, n_row)
    early, last = found[:-1], found[-1:]
    partial = pivot_products(at, pivot_inverse, early, n_row, straight, lambda t: [t], [block])
    inner, inner_half = pivot_products(
        at,
        pivot_inverse,
        last,
        n_row,
        straight,
        lambda t, p: [t + p, (t + p).astype(BF16)],
        [block, half],
        partial,
    )
    found = gather_row(inner_half, n_row)
    partial, own_rhs = border_partial(at, border_coupling, found[:2], n_row, None, rhs_root, piece_rows)
    partial, inverse = border_partial(
        at, border_coupling, found[2:-1], n_row, partial, root_inverse, root_inverse.shape[0]
    )
    send, keep = border_scatter(
        at, local_index, border_coupling, found[-1:], partial, n_row, n_front, span_rows
    )
    came = swap(send, n_front, 1)
    low, high = sum_halves(keep, came, [(3, 0), (3, 1)])
    low, high = swap(low, n_front, 2), swap(high, n_front, 4)
    x_low, y_high = sum_halves(keep, came, [(1, 0), (2, 1)])
    x_low, y_high = swap(x_low, n_front, 2), swap(y_high, n_front, 4)
    x_high, y_low = sum_relayed(keep, came, low, high)
    x_high, y_low = swap(x_high, n_front, 2), swap(y_low, n_front, 4)
    pieces = gather_front(*own_part(own_rhs, keep, came, (x_low, y_low), (x_high, y_high)), n_front)

    def root(offsets, kind):
        outs = root_products(at, inverse, pieces, offsets, [kind] * len(offsets), n_row, n_front)
        return dict(zip(offsets, outs))

    first = {}
    for offset in first_at:
        first.update(root([offset], BF16))
    rest = root(later_at + [0], F32)
    root_solution = scatter_row(first, rest, rest[0], n_row)
    spans = gather_front(*to_plane(root_solution.astype(BF16), n_row), n_front)

    out, picked = border_pick(at, local_index, border_coupling, spans, first_at[0], n_row, n_front)
    first = {first_at[0]: out}
    for offset in first_at[1:]:
        first[offset] = border_backward(at, border_coupling, picked, [offset], [BF16], n_row)[0]
    offsets = later_at + [0]
    rest = dict(zip(offsets, border_backward(at, border_coupling, picked, offsets, [F32] * len(offsets), n_row)))
    pulled = scatter_row(first, rest, rest[0], n_row).astype(BF16)
    found = gather_row(pulled, n_row)
    early, last = found[:-1], found[-1:]
    partial = pivot_products(
        at, pivot_inverse, early, n_row, across, lambda t, i: [i - t], [block], [inner]
    )
    front_solution = pivot_products(
        at, pivot_inverse, last, n_row, across, lambda t, p: [p - t], [block], partial, True
    )
    return front_solution[0], root_solution


def solve_plain(n_front, n_row, rhs_front, rhs_root, pivot_inverse, border_coupling, root_inverse, border_map):
    row_at = lax.axis_index("row")
    front_at = lax.axis_index("front")
    width = rhs_front.shape[1]
    inner = dot(pivot_inverse, lax.all_gather(rhs_front, "row", axis=0, tiled=True))
    contrib = dot(border_coupling, lax.all_gather(inner.astype(BF16), "row", axis=0, tiled=True))
    block_local = border_map.shape[1]
    span_rows = root_inverse.shape[1]
    span_blocks = span_rows // BLK
    local_index = border_map[0] - row_at * span_blocks
    select = (local_index[None, :] == jnp.arange(span_blocks, dtype=jnp.int32)[:, None]).astype(F32)
    dense = jnp.einsum(
        "kj,jcn->kcn", select, contrib.reshape(block_local, BLK, width), precision=lax.Precision.HIGHEST
    ).reshape(span_rows, width)
    shares = lax.psum_scatter(dense, "front", scatter_dimension=0, tiled=True)
    own_rhs = lax.dynamic_slice_in_dim(rhs_root, front_at * shares.shape[0], shares.shape[0], 0)
    schur_rhs = lax.all_gather((own_rhs - shares).astype(BF16), "front", axis=0, tiled=True)
    root_solution = lax.psum_scatter(dot(root_inverse, schur_rhs), "row", scatter_dimension=0, tiled=True)
    gathered = lax.all_gather(root_solution.astype(BF16), ("front", "row"), axis=0, tiled=True)
    ranged = lax.dynamic_slice_in_dim(gathered, row_at * span_rows, span_rows, 0)
    picked = jnp.take(ranged.reshape(span_blocks, BLK, width), local_index, axis=0)
    picked = picked.reshape(block_local * BLK, width)
    pulled = lax.psum_scatter(
        dot(border_coupling, picked, ((0,), (0,))), "row", scatter_dimension=0, tiled=True
    ).astype(BF16)
    correction = dot(pivot_inverse, lax.all_gather(pulled, "row", axis=0, tiled=True))
    return inner - correction, root_solution


def solution(mesh):
    in_specs = (
        P(("front", "row"), None),
        P("row", None),
        P(("front", "row"), None),
        P(("front", "row"), None),
        P("front", "row"),
        P("front", "row"),
    )
    out_specs = (P(("front", "row"), None), P(("front", "row"), None))
    n_front, n_row = mesh.shape["front"], mesh.shape["row"]

    def per_device(*arrays):
        root_inverse, width = arrays[4], arrays[0].shape[1]
        fits = (
            n_front == 8
            and n_front == 2 * n_row
            and root_inverse.shape[1] % (n_front * BLK) == 0
            and root_inverse.shape[0] == n_row * (root_inverse.shape[1] // n_front)
            and root_inverse.shape[1] % (n_front * n_row * 16) == 0
            and arrays[2].shape[1] % (n_row * BLK) == 0
            and width % BLK == 0
        )
        return (solve if fits else solve_plain)(n_front, n_row, *arrays)

    return jax.shard_map(per_device, mesh=mesh, in_specs=in_specs, out_specs=out_specs, check_vma=False)
```

```python
import math

import jax
import jax.numpy as jnp
from jax import lax
from jax.experimental import pallas as pl
from jax.experimental.pallas import tpu as pltpu
from jax.sharding import PartitionSpec as P

BLK = 128
F32 = jnp.float32
BF16 = jnp.bfloat16
VMEM = pl.BlockSpec(memory_space=pltpu.VMEM)
ANY = pl.BlockSpec(memory_space=pl.ANY)


def dot(a, b, contract=((1,), (0,))):
    return lax.dot_general(a, b, (contract, ((), ())), preferred_element_type=F32)


def in_hbm(x):
    return pltpu.with_memory_space_constraint(x, pltpu.HBM)


def kernel_call(body, outs, scalars, held, placed, scratch, flops, nbytes, final=False, loose=()):
    size = sum(2 * math.prod(s.shape) for s in scratch if s.dtype == BF16)
    single = not isinstance(outs, list)
    out_shape = [o if final else pltpu.VMEM(o.shape, o.dtype) for o in ([outs] if single else outs)]
    results = pl.pallas_call(
        body,
        out_shape=out_shape,
        grid_spec=pltpu.PrefetchScalarGridSpec(
            num_scalar_prefetch=len(scalars),
            grid=(1,),
            in_specs=[VMEM] * (len(held) + len(loose)) + [ANY] * len(placed),
            out_specs=[VMEM] * len(out_shape),
            scratch_shapes=scratch,
        ),
        compiler_params=pltpu.CompilerParams(vmem_limit_bytes=size + 12 * 1024 * 1024),
        cost_estimate=pl.CostEstimate(flops=flops, bytes_accessed=nbytes, transcendentals=0),
    )(*scalars, *[pltpu.with_memory_space_constraint(x, pltpu.VMEM) for x in held], *loose, *placed)
    return results[0] if single else results


def shift(x, size, by):
    return lax.ppermute(x, "row", [(i, (i + by) % size) for i in range(size)])


def swap(x, size, by):
    return lax.ppermute(x, "front", [(i, i ^ by) for i in range(size)])


def cross(x, n, even, odd):
    return lax.ppermute(x, "front", [(i, i ^ (odd if i % 2 else even)) for i in range(n)])


def gather_row(x, n):
    found = [(0, x)]
    up, down = x, x
    for step in range(1, n // 2 + 1):
        up = shift(up, n, 1)
        found.append((-step, up))
        if step < n - step:
            down = shift(down, n, -1)
            found.append((step, down))
    return found


def gather_front(at, first, second, n):
    rows = first.shape[0]
    near, side = cross(first, n, 2, 4), cross(second, n, 4, 2)
    first, second = again(first, second)
    near_late, side_late = cross(second, n, 2, 4), cross(first, n, 4, 2)
    far, far_late = cross(near, n, 4, 2), cross(side, n, 2, 4)
    blocks = [second, first, near_late, near, side, side_late, far_late, far]
    mine = stack(at, blocks, [0, 1, 2, 3, 4, 5, 6, 7], [1, 0, 5, 4, 3, 2, 7, 6])
    return [
        (chip, core, chip * 2 * rows, 2 * rows, found)
        for core, found in ((0, mine), (1, swap(mine, n, 1)))
        for chip in range(4)
    ]


def to_plane(x, n):
    rows = x.shape[0] // n
    moved = []
    for k in range(n):
        quarter = x[k * rows : (k + 1) * rows]
        if k:
            quarter = swap(quarter, 2 * n, 2 * k)
        perm = [
            ((chip * 2 + core) * n + row, (row * 2 + core) * n + (chip ^ k))
            for chip in range(n)
            for core in range(2)
            for row in range(n)
        ]
        moved.append(lax.ppermute(quarter, ("front", "row"), perm))
    half = n // 2
    return [jnp.concatenate(some, axis=0) for some in (moved[:half], moved[half:])]


def far_offsets(n):
    first = [-(n // 2)] + ([(n - 1) // 2] if n > 2 else [])
    later = [o for o in range(-(n // 2) + 1, (n - 1) // 2) if o]
    return first, later


def scatter_row(first, later, own, n):
    total = own
    for sign, far in ((-1, n // 2), (1, (n - 1) // 2)):
        running = None
        for step in range(far, 0, -1):
            if running is None:
                running = first[sign * step]
            else:
                running = (running.astype(F32) + later[sign * step]).astype(BF16)
            running = shift(running, n, sign)
        if running is not None:
            total = total + running.astype(F32)
    return total


def owner(at_ref, offset, n_row):
    return lax.rem(at_ref[0] + (offset + n_row), n_row)


def products(at_ref, a_ref, rows, offsets, x_refs, n_row, contract):
    depth = a_ref.shape[1] // n_row
    total = None
    for offset, x_ref in zip(offsets, x_refs):
        columns = pl.ds(pl.multiple_of(owner(at_ref, offset, n_row) * depth, depth), depth)
        part = dot(a_ref[rows, columns], x_ref[...], contract)
        total = part if total is None else total + part
    return total


def pivot_products(at, pivot, found, n_row, contract, finish, outs, extra=(), final=False):
    count = len(found)
    offsets = [o for o, _ in found]

    def body(at_ref, a_ref, *refs):
        extras, x_refs = refs[: len(extra)], refs[len(extra) : len(extra) + count]
        total = products(at_ref, a_ref, slice(None), offsets, x_refs, n_row, contract)
        for ref, value in zip(refs[count + len(extra) :], finish(total, *[e[...] for e in extras])):
            ref[...] = value

    share = 2 * pivot.size * count // n_row
    held = [pivot] + list(extra)
    blocks = [x for _, x in found]
    return kernel_call(body, outs, [at], held, [], [], share * outs[0].shape[1], share, final, blocks)


def border_tile(rows):
    return BLK * next(k for k in (4, 3, 2, 1) if rows // BLK % k == 0)


def border_partial(at, coupling, found, n_row, partial, source, fetch_rows):
    rows, count, width = coupling.shape[0], len(found), found[0][1].shape[1]
    offsets = [o for o, _ in found]
    tile = border_tile(rows)
    held = [coupling] + [x for _, x in found] + ([] if partial is None else [partial])

    def body(at_ref, a_ref, *refs):
        source_hbm, out_ref, own_ref, sem = refs[-4:]
        if fetch_rows < source.shape[0]:
            source_hbm = source_hbm.at[pl.ds(pl.multiple_of(at_ref[1] * fetch_rows, fetch_rows), fetch_rows)]
        copy = pltpu.make_async_copy(source_hbm, own_ref, sem)
        copy.start()

        @pl.loop(0, rows // tile)
        def _(i):
            place = pl.ds(pl.multiple_of(i * tile, tile), tile)
            total = products(at_ref, a_ref, place, offsets, refs[:count], n_row, ((1,), (0,)))
            out_ref[place, :] = total if partial is None else refs[count][place, :] + total

        copy.wait()

    share = 2 * coupling.size * count // n_row
    outs = [
        jax.ShapeDtypeStruct((rows, width), F32),
        jax.ShapeDtypeStruct((fetch_rows, source.shape[1]), source.dtype),
    ]
    scratch = [pltpu.SemaphoreType.DMA]
    return kernel_call(body, outs, [at], held, [in_hbm(source)], scratch, share * width, share)


def border_scatter(at, local_index, coupling, found, partial, n_row, n_front, span_rows):
    rows, count, width = coupling.shape[0], len(found), found[0][1].shape[1]
    offsets = [o for o, _ in found]
    tile = border_tile(rows)
    piece_blocks = span_rows // n_front // BLK

    def body(at_ref, index_ref, a_ref, *refs):
        partial_ref, send_ref, keep_ref = refs[count:]
        send_ref[...] = jnp.zeros_like(send_ref)
        keep_ref[...] = jnp.zeros_like(keep_ref)

        @pl.loop(0, rows // tile)
        def _(i):
            place = pl.ds(pl.multiple_of(i * tile, tile), tile)
            total = products(at_ref, a_ref, place, offsets, refs[:count], n_row, ((1,), (0,)))
            total = (partial_ref[place, :] + total).astype(BF16)
            for j in range(tile // BLK):
                target = index_ref[i * (tile // BLK) + j]
                there = lax.div(target, piece_blocks)
                chip = lax.shift_right_logical(lax.bitwise_xor(there, at_ref[1]), 1)
                slot = chip * piece_blocks + lax.rem(target, piece_blocks)
                goal = pl.ds(pl.multiple_of(slot * BLK, BLK), BLK)
                block = total[j * BLK : (j + 1) * BLK]
                away = lax.rem(there + at_ref[1], 2)

                @pl.when(away == 1)
                def _():
                    send_ref[goal, :] = block

                @pl.when(away == 0)
                def _():
                    keep_ref[goal, :] = block

    half = jax.ShapeDtypeStruct((span_rows // 2, width), BF16)
    share = 2 * coupling.size * count // n_row
    held = [coupling] + [x for _, x in found] + [partial]
    return kernel_call(body, [half, half], [at, local_index], held, [], [], share * width, share)


def added(*parts):
    total = parts[0].astype(F32)
    for part in parts[1:]:
        total = total + part.astype(F32)
    return total


def half_rows(at_ref, rows, even, odd):
    place = jnp.where(lax.rem(at_ref[1], 2) == 0, even, odd)
    return pl.ds(pl.multiple_of(place * rows, rows), rows)


def sum_halves(at, keep, came, halves):
    rows, width = keep.shape[0] // 8, keep.shape[1]
    outs = [jax.ShapeDtypeStruct((rows, width), BF16)] * len(halves)
    more = [add for _, _, add in halves if add is not None]

    def body(at_ref, keep_ref, came_ref, *refs):
        more_refs, out_refs = list(refs[: len(more)]), refs[len(more) :]
        for (even, odd, add), out_ref in zip(halves, out_refs):
            place = half_rows(at_ref, rows, even, odd)
            extra = [] if add is None else [more_refs.pop(0)[...]]
            out_ref[...] = added(keep_ref[place, :], came_ref[place, :], *extra).astype(BF16)

    return kernel_call(body, outs, [at], [keep, came, *more], [], [], 2 * keep.size, 2 * keep.size)


def own_part(at, own_rhs, keep, came, first, second):
    rows, width = own_rhs.shape[0] // 2, own_rhs.shape[1]

    def body(at_ref, rhs_ref, keep_ref, came_ref, *refs):
        for i, (even, odd) in enumerate(((1, 0), (0, 1))):
            place = half_rows(at_ref, rows, even, odd)
            adds = [ref[...] for ref in refs[2 * i : 2 * i + 2]]
            total = added(keep_ref[place, :], came_ref[place, :], *adds)
            refs[4 + i][...] = (rhs_ref[place, :] - total).astype(BF16)

    outs = [jax.ShapeDtypeStruct((rows, width), BF16)] * 2
    held = [own_rhs, keep, came, *first, *second]
    return kernel_call(body, outs, [at], held, [], [], keep.size, keep.size)


def stack(at, blocks, even, odd):
    rows, width = blocks[0].shape

    def body(at_ref, *refs):
        for ref, one, two in zip(refs, even, odd):
            refs[-1][half_rows(at_ref, rows, one, two), :] = ref[...]

    out = jax.ShapeDtypeStruct((len(blocks) * rows, width), BF16)
    return kernel_call(body, out, [at], blocks, [], [], 0, 4 * len(blocks) * rows * width)


def by_core(at, low, high):
    def body(at_ref, low_ref, high_ref, first_ref, second_ref):
        even = lax.rem(at_ref[1], 2) == 0

        @pl.when(even)
        def _():
            first_ref[...], second_ref[...] = high_ref[...], low_ref[...]

        @pl.when(jnp.logical_not(even))
        def _():
            first_ref[...], second_ref[...] = low_ref[...], high_ref[...]

    outs = [jax.ShapeDtypeStruct(low.shape, BF16)] * 2
    return kernel_call(body, outs, [at], [low, high], [], [], 0, 8 * low.size)


def again(low, high):
    def body(low_ref, high_ref, low_out_ref, high_out_ref):
        low_out_ref[...] = low_ref[...]
        high_out_ref[...] = high_ref[...]

    outs = [jax.ShapeDtypeStruct(low.shape, BF16)] * 2
    return kernel_call(body, outs, [], [low, high], [], [], 0, 8 * low.size)


def assemble(pieces, piece_refs, target_ref, sems, base):
    copies = []
    for (chip, core, row, rows, _), ref in zip(pieces, piece_refs):
        place = pl.ds(pl.multiple_of(base(2 * chip + core), rows), rows)
        source = ref.at[pl.ds(row, rows)]
        copies.append(pltpu.make_async_copy(source, target_ref.at[place], sems.at[len(copies)]))
    return copies


def root_products(at, inverse, pieces, offsets, kinds, n_row, n_front):
    span_rows = inverse.shape[1]
    rows = inverse.shape[0] // n_row
    width = pieces[0][-1].shape[1]
    piece_rows = span_rows // n_front
    count, many = len(offsets), len(pieces)

    def body(at_ref, a_ref, *refs):
        piece_refs, out_refs, (x_ref, sems) = refs[:many], refs[many : many + count], refs[many + count :]
        copies = assemble(
            pieces, piece_refs, x_ref, sems, lambda d: lax.bitwise_xor(at_ref[1], d) * piece_rows
        )
        for copy in copies:
            copy.start()
        for copy in copies:
            copy.wait()
        for offset, out_ref in zip(offsets, out_refs):
            place = pl.ds(pl.multiple_of(owner(at_ref, offset, n_row) * rows, rows), rows)
            out_ref[...] = dot(a_ref[place, :], x_ref[...]).astype(out_ref.dtype)

    outs = [jax.ShapeDtypeStruct((rows, width), kind) for kind in kinds]
    scratch = [pltpu.VMEM((span_rows, width), BF16), pltpu.SemaphoreType.DMA((many,))]
    share = 2 * rows * span_rows * count
    held = [inverse] + [block for *_, block in pieces]
    return kernel_call(body, outs, [at], held, [], scratch, share * width, share)


def border_pick(at, local_index, coupling, pieces, offset, n_row, n_front):
    rows, depth = coupling.shape[0], coupling.shape[1] // n_row
    piece_rows, width = pieces[0][3], pieces[0][-1].shape[1]
    span_rows = piece_rows * n_front
    many = len(pieces)

    def body(at_ref, index_ref, a_ref, *refs):
        piece_refs, (out_ref, picked_ref, span_ref, sems) = refs[:many], refs[many:]

        def base(d):
            there = lax.bitwise_xor(at_ref[1], d)
            return lax.rem(there, 2) * (span_rows // 2) + lax.shift_right_logical(there, 1) * piece_rows

        copies = assemble(pieces, piece_refs, span_ref, sems, base)
        for copy in copies:
            copy.start()
        for copy in copies:
            copy.wait()
        for j in range(rows // BLK):
            source = pl.ds(pl.multiple_of(index_ref[j] * BLK, BLK), BLK)
            picked_ref[:, pl.ds(j * BLK, BLK)] = jnp.transpose(span_ref[source, :])
        columns = pl.ds(pl.multiple_of(owner(at_ref, offset, n_row) * depth, depth), depth)
        out_ref[...] = dot(picked_ref[...], a_ref[:, columns]).astype(BF16)

    outs = [jax.ShapeDtypeStruct((width, depth), BF16), jax.ShapeDtypeStruct((width, rows), BF16)]
    scratch = [pltpu.VMEM((span_rows, width), BF16), pltpu.SemaphoreType.DMA((many,))]
    share = 2 * rows * depth
    held = [coupling] + [block for *_, block in pieces]
    return kernel_call(body, outs, [at, local_index], held, [], scratch, share * width, share)


def border_backward(at, coupling, picked, offsets, kinds, n_row):
    rows, depth = coupling.shape[0], coupling.shape[1] // n_row
    width, count = picked.shape[0], len(offsets)

    def body(at_ref, x_ref, a_ref, *out_refs):
        for offset, out_ref in zip(offsets, out_refs):
            columns = pl.ds(pl.multiple_of(owner(at_ref, offset, n_row) * depth, depth), depth)
            out_ref[...] = dot(x_ref[...], a_ref[:, columns]).astype(out_ref.dtype)

    outs = [jax.ShapeDtypeStruct((width, depth), kind) for kind in kinds]
    share = 2 * rows * depth * count
    return kernel_call(body, outs, [at], [picked, coupling], [], [], share * width, share)


def solve(n_front, n_row, rhs_front, rhs_root, pivot_inverse, border_coupling, root_inverse, border_map):
    row_at = lax.axis_index("row").astype(jnp.int32)
    front_at = lax.axis_index("front").astype(jnp.int32)
    at = jnp.stack([row_at, front_at])
    span_rows = root_inverse.shape[1]
    piece_rows, width = span_rows // n_front, rhs_front.shape[1]
    local_index = border_map[0] - row_at * (span_rows // BLK)
    first_at, later_at = far_offsets(n_row)
    block = jax.ShapeDtypeStruct((pivot_inverse.shape[0], width), F32)
    half = jax.ShapeDtypeStruct(block.shape, BF16)
    straight, across = ((1,), (0,)), ((1,), (1,))

    found = gather_row(rhs_front, n_row)
    early, last = found[:-1], found[-1:]
    partial = pivot_products(at, pivot_inverse, early, n_row, straight, lambda t: [t], [block])
    inner, inner_half = pivot_products(
        at,
        pivot_inverse,
        last,
        n_row,
        straight,
        lambda t, p: [t + p, (t + p).astype(BF16)],
        [block, half],
        partial,
    )
    found = gather_row(inner_half, n_row)
    partial, own_rhs = border_partial(at, border_coupling, found[:2], n_row, None, rhs_root, piece_rows)
    partial, inverse = border_partial(
        at, border_coupling, found[2:-1], n_row, partial, root_inverse, root_inverse.shape[0]
    )
    send, keep = border_scatter(
        at, local_index, border_coupling, found[-1:], partial, n_row, n_front, span_rows
    )
    came = swap(send, n_front, 1)
    low, high = sum_halves(at, keep, came, [(6, 7, None), (7, 6, None)])
    near, side = cross(low, n_front, 2, 4), cross(high, n_front, 4, 2)
    plain = sum_halves(at, keep, came, [(2, 5, None), (5, 2, None)])
    near_plain, side_plain = cross(plain[0], n_front, 2, 4), cross(plain[1], n_front, 4, 2)
    relayed = sum_halves(at, keep, came, [(4, 3, near), (3, 4, side)])
    side_sum, near_sum = cross(relayed[0], n_front, 4, 2), cross(relayed[1], n_front, 2, 4)
    halves = own_part(at, own_rhs, keep, came, (side_plain, near_sum), (near_plain, side_sum))
    pieces = gather_front(at, *halves, n_front)

    def root(offsets, kind):
        outs = root_products(at, inverse, pieces, offsets, [kind] * len(offsets), n_row, n_front)
        return dict(zip(offsets, outs))

    first = {}
    for offset in first_at:
        first.update(root([offset], BF16))
    rest = root(later_at + [0], F32)
    root_solution = scatter_row(first, rest, rest[0], n_row)
    spans = gather_front(at, *by_core(at, *to_plane(root_solution.astype(BF16), n_row)), n_front)

    out, picked = border_pick(at, local_index, border_coupling, spans, first_at[0], n_row, n_front)
    first = {first_at[0]: out}
    for offset in first_at[1:]:
        first[offset] = border_backward(at, border_coupling, picked, [offset], [BF16], n_row)[0]
    offsets = later_at + [0]
    rest = dict(zip(offsets, border_backward(at, border_coupling, picked, offsets, [F32] * len(offsets), n_row)))
    pulled = scatter_row(first, rest, rest[0], n_row).astype(BF16)
    found = gather_row(pulled, n_row)
    early, last = found[:-1], found[-1:]
    partial = pivot_products(
        at, pivot_inverse, early, n_row, across, lambda t, i: [i - t], [block], [inner]
    )
    front_solution = pivot_products(
        at, pivot_inverse, last, n_row, across, lambda t, p: [p - t], [block], partial, True
    )
    return front_solution[0], root_solution


def solve_plain(n_front, n_row, rhs_front, rhs_root, pivot_inverse, border_coupling, root_inverse, border_map):
    row_at = lax.axis_index("row")
    front_at = lax.axis_index("front")
    width = rhs_front.shape[1]
    inner = dot(pivot_inverse, lax.all_gather(rhs_front, "row", axis=0, tiled=True))
    contrib = dot(border_coupling, lax.all_gather(inner.astype(BF16), "row", axis=0, tiled=True))
    block_local = border_map.shape[1]
    span_rows = root_inverse.shape[1]
    span_blocks = span_rows // BLK
    local_index = border_map[0] - row_at * span_blocks
    select = (local_index[None, :] == jnp.arange(span_blocks, dtype=jnp.int32)[:, None]).astype(F32)
    dense = jnp.einsum(
        "kj,jcn->kcn", select, contrib.reshape(block_local, BLK, width), precision=lax.Precision.HIGHEST
    ).reshape(span_rows, width)
    shares = lax.psum_scatter(dense, "front", scatter_dimension=0, tiled=True)
    own_rhs = lax.dynamic_slice_in_dim(rhs_root, front_at * shares.shape[0], shares.shape[0], 0)
    schur_rhs = lax.all_gather((own_rhs - shares).astype(BF16), "front", axis=0, tiled=True)
    root_solution = lax.psum_scatter(dot(root_inverse, schur_rhs), "row", scatter_dimension=0, tiled=True)
    gathered = lax.all_gather(root_solution.astype(BF16), ("front", "row"), axis=0, tiled=True)
    ranged = lax.dynamic_slice_in_dim(gathered, row_at * span_rows, span_rows, 0)
    picked = jnp.take(ranged.reshape(span_blocks, BLK, width), local_index, axis=0)
    picked = picked.reshape(block_local * BLK, width)
    pulled = lax.psum_scatter(
        dot(border_coupling, picked, ((0,), (0,))), "row", scatter_dimension=0, tiled=True
    ).astype(BF16)
    correction = dot(pivot_inverse, lax.all_gather(pulled, "row", axis=0, tiled=True))
    return inner - correction, root_solution


def solution(mesh):
    in_specs = (
        P(("front", "row"), None),
        P("row", None),
        P(("front", "row"), None),
        P(("front", "row"), None),
        P("front", "row"),
        P("front", "row"),
    )
    out_specs = (P(("front", "row"), None), P(("front", "row"), None))
    n_front, n_row = mesh.shape["front"], mesh.shape["row"]

    def per_device(*arrays):
        root_inverse, width = arrays[4], arrays[0].shape[1]
        fits = (
            n_front == 8
            and n_front == 2 * n_row
            and root_inverse.shape[1] % (n_front * BLK) == 0
            and root_inverse.shape[0] == n_row * (root_inverse.shape[1] // n_front)
            and root_inverse.shape[1] % (n_front * n_row * 16) == 0
            and arrays[2].shape[1] % (n_row * BLK) == 0
            and width % BLK == 0
        )
        return (solve if fits else solve_plain)(n_front, n_row, *arrays)

    return jax.shard_map(per_device, mesh=mesh, in_specs=in_specs, out_specs=out_specs, check_vma=False)
```

```python
import math

import jax
import jax.numpy as jnp
from jax import lax
from jax.experimental import pallas as pl
from jax.experimental.pallas import tpu as pltpu
from jax.sharding import PartitionSpec as P

BLK = 128
F32 = jnp.float32
BF16 = jnp.bfloat16
PLACE = ("row", "front")
VMEM = pl.BlockSpec(memory_space=pltpu.VMEM)
ANY = pl.BlockSpec(memory_space=pl.ANY)


def dot(a, b, contract=((1,), (0,))):
    return lax.dot_general(a, b, (contract, ((), ())), preferred_element_type=F32)


def in_hbm(x):
    return pltpu.with_memory_space_constraint(x, pltpu.HBM)


def kernel_call(body, outs, scalars, held, placed, scratch, flops, nbytes, final=False, loose=()):
    size = sum(2 * math.prod(s.shape) for s in scratch if s.dtype == BF16)
    if scalars and scalars[0] is PLACE:
        scalars = scalars[1:]

        def placed_body(*refs):
            body([lax.axis_index(name) for name in PLACE], *refs)

    else:
        placed_body = body
    single = not isinstance(outs, list)
    out_shape = [o if final else pltpu.VMEM(o.shape, o.dtype) for o in ([outs] if single else outs)]
    results = pl.pallas_call(
        placed_body,
        out_shape=out_shape,
        grid_spec=pltpu.PrefetchScalarGridSpec(
            num_scalar_prefetch=len(scalars),
            grid=(1,),
            in_specs=[VMEM] * (len(held) + len(loose)) + [ANY] * len(placed),
            out_specs=[VMEM] * len(out_shape),
            scratch_shapes=scratch,
        ),
        compiler_params=pltpu.CompilerParams(vmem_limit_bytes=size + 12 * 1024 * 1024),
        cost_estimate=pl.CostEstimate(flops=flops, bytes_accessed=nbytes, transcendentals=0),
    )(*scalars, *[pltpu.with_memory_space_constraint(x, pltpu.VMEM) for x in held], *loose, *placed)
    return results[0] if single else results


def shift(x, size, by):
    return lax.ppermute(x, "row", [(i, (i + by) % size) for i in range(size)])


def swap(x, size, by):
    return lax.ppermute(x, "front", [(i, i ^ by) for i in range(size)])


def cross(x, n, even, odd):
    return lax.ppermute(x, "front", [(i, i ^ (odd if i % 2 else even)) for i in range(n)])


def gather_row(x, n):
    found = [(0, x)]
    up, down = x, x
    for step in range(1, n // 2 + 1):
        up = shift(up, n, 1)
        found.append((-step, up))
        if step < n - step:
            down = shift(down, n, -1)
            found.append((step, down))
    return found


def gather_front(at, first, second, n):
    rows = first.shape[0]
    near, side = cross(first, n, 2, 4), cross(second, n, 4, 2)
    first, second = again(first, second)
    near_late, side_late = cross(second, n, 2, 4), cross(first, n, 4, 2)
    far, far_late = cross(near, n, 4, 2), cross(side, n, 2, 4)
    blocks = [second, first, near_late, near, side, side_late, far_late, far]
    mine = stack(at, blocks, [0, 1, 2, 3, 4, 5, 6, 7], [1, 0, 5, 4, 3, 2, 7, 6])
    return [
        (chip, core, chip * 2 * rows, 2 * rows, found)
        for core, found in ((0, mine), (1, swap(mine, n, 1)))
        for chip in range(4)
    ]


def to_plane(x, n):
    rows = x.shape[0] // n
    moved = []
    for k in range(n):
        quarter = x[k * rows : (k + 1) * rows]
        if k:
            quarter = swap(quarter, 2 * n, 2 * k)
        perm = [
            ((chip * 2 + core) * n + row, (row * 2 + core) * n + (chip ^ k))
            for chip in range(n)
            for core in range(2)
            for row in range(n)
        ]
        moved.append(lax.ppermute(quarter, ("front", "row"), perm))
    half = n // 2
    return [jnp.concatenate(some, axis=0) for some in (moved[:half], moved[half:])]


def far_offsets(n):
    first = [-(n // 2)] + ([(n - 1) // 2] if n > 2 else [])
    later = [o for o in range(-(n // 2) + 1, (n - 1) // 2) if o]
    return first, later


def scatter_row(first, later, own, n):
    total = own
    for sign, far in ((-1, n // 2), (1, (n - 1) // 2)):
        running = None
        for step in range(far, 0, -1):
            if running is None:
                running = first[sign * step]
            else:
                running = (running.astype(F32) + later[sign * step]).astype(BF16)
            running = shift(running, n, sign)
        if running is not None:
            total = total + running.astype(F32)
    return total


def owner(at_ref, offset, n_row):
    return lax.rem(at_ref[0] + (offset + n_row), n_row)


def products(at_ref, a_ref, rows, offsets, x_refs, n_row, contract):
    depth = a_ref.shape[1] // n_row
    total = None
    for offset, x_ref in zip(offsets, x_refs):
        columns = pl.ds(pl.multiple_of(owner(at_ref, offset, n_row) * depth, depth), depth)
        part = dot(a_ref[rows, columns], x_ref[...], contract)
        total = part if total is None else total + part
    return total


def pivot_products(at, pivot, found, n_row, contract, finish, outs, extra=(), final=False):
    count = len(found)
    offsets = [o for o, _ in found]

    def body(at_ref, a_ref, *refs):
        extras, x_refs = refs[: len(extra)], refs[len(extra) : len(extra) + count]
        total = products(at_ref, a_ref, slice(None), offsets, x_refs, n_row, contract)
        for ref, value in zip(refs[count + len(extra) :], finish(total, *[e[...] for e in extras])):
            ref[...] = value

    share = 2 * pivot.size * count // n_row
    held = [pivot] + list(extra)
    blocks = [x for _, x in found]
    return kernel_call(body, outs, [at], held, [], [], share * outs[0].shape[1], share, final, blocks)


def border_tile(rows):
    return BLK * next(k for k in (4, 3, 2, 1) if rows // BLK % k == 0)


def border_partial(at, coupling, found, n_row, partial, source, fetch_rows):
    rows, count, width = coupling.shape[0], len(found), found[0][1].shape[1]
    offsets = [o for o, _ in found]
    tile = border_tile(rows)
    held = [coupling] + [x for _, x in found] + ([] if partial is None else [partial])

    def body(at_ref, a_ref, *refs):
        source_hbm, out_ref, own_ref, sem = refs[-4:]
        if fetch_rows < source.shape[0]:
            source_hbm = source_hbm.at[pl.ds(pl.multiple_of(at_ref[1] * fetch_rows, fetch_rows), fetch_rows)]
        copy = pltpu.make_async_copy(source_hbm, own_ref, sem)
        copy.start()

        @pl.loop(0, rows // tile)
        def _(i):
            place = pl.ds(pl.multiple_of(i * tile, tile), tile)
            total = products(at_ref, a_ref, place, offsets, refs[:count], n_row, ((1,), (0,)))
            out_ref[place, :] = total if partial is None else refs[count][place, :] + total

        copy.wait()

    share = 2 * coupling.size * count // n_row
    outs = [
        jax.ShapeDtypeStruct((rows, width), F32),
        jax.ShapeDtypeStruct((fetch_rows, source.shape[1]), source.dtype),
    ]
    scratch = [pltpu.SemaphoreType.DMA]
    return kernel_call(body, outs, [at], held, [in_hbm(source)], scratch, share * width, share)


def border_scatter(at, local_index, coupling, found, partial, n_row, n_front, span_rows):
    rows, count, width = coupling.shape[0], len(found), found[0][1].shape[1]
    offsets = [o for o, _ in found]
    tile = border_tile(rows)
    piece_blocks = span_rows // n_front // BLK

    def body(at_ref, index_ref, a_ref, *refs):
        partial_ref, send_ref, keep_ref = refs[count:]
        send_ref[...] = jnp.zeros_like(send_ref)
        keep_ref[...] = jnp.zeros_like(keep_ref)

        @pl.loop(0, rows // tile)
        def _(i):
            place = pl.ds(pl.multiple_of(i * tile, tile), tile)
            total = products(at_ref, a_ref, place, offsets, refs[:count], n_row, ((1,), (0,)))
            total = (partial_ref[place, :] + total).astype(BF16)
            for j in range(tile // BLK):
                target = index_ref[i * (tile // BLK) + j]
                there = lax.div(target, piece_blocks)
                chip = lax.shift_right_logical(lax.bitwise_xor(there, at_ref[1]), 1)
                slot = chip * piece_blocks + lax.rem(target, piece_blocks)
                goal = pl.ds(pl.multiple_of(slot * BLK, BLK), BLK)
                block = total[j * BLK : (j + 1) * BLK]
                away = lax.rem(there + at_ref[1], 2)

                @pl.when(away == 1)
                def _():
                    send_ref[goal, :] = block

                @pl.when(away == 0)
                def _():
                    keep_ref[goal, :] = block

    half = jax.ShapeDtypeStruct((span_rows // 2, width), BF16)
    share = 2 * coupling.size * count // n_row
    held = [coupling] + [x for _, x in found] + [partial]
    return kernel_call(body, [half, half], [at, local_index], held, [], [], share * width, share)


def added(*parts):
    total = parts[0].astype(F32)
    for part in parts[1:]:
        total = total + part.astype(F32)
    return total


def half_rows(at_ref, rows, even, odd):
    place = jnp.where(lax.rem(at_ref[1], 2) == 0, even, odd)
    return pl.ds(pl.multiple_of(place * rows, rows), rows)


def sum_halves(at, keep, came, halves):
    rows, width = keep.shape[0] // 8, keep.shape[1]
    outs = [jax.ShapeDtypeStruct((rows, width), BF16)] * len(halves)
    more = [add for _, _, add in halves if add is not None]

    def body(at_ref, keep_ref, came_ref, *refs):
        more_refs, out_refs = list(refs[: len(more)]), refs[len(more) :]
        for (even, odd, add), out_ref in zip(halves, out_refs):
            place = half_rows(at_ref, rows, even, odd)
            extra = [] if add is None else [more_refs.pop(0)[...]]
            out_ref[...] = added(keep_ref[place, :], came_ref[place, :], *extra).astype(BF16)

    return kernel_call(body, outs, [at], [keep, came, *more], [], [], 2 * keep.size, 2 * keep.size)


def own_part(at, own_rhs, keep, came, first, second):
    rows, width = own_rhs.shape[0] // 2, own_rhs.shape[1]

    def body(at_ref, rhs_ref, keep_ref, came_ref, *refs):
        for i, (even, odd) in enumerate(((1, 0), (0, 1))):
            place = half_rows(at_ref, rows, even, odd)
            adds = [ref[...] for ref in refs[2 * i : 2 * i + 2]]
            total = added(keep_ref[place, :], came_ref[place, :], *adds)
            refs[4 + i][...] = (rhs_ref[place, :] - total).astype(BF16)

    outs = [jax.ShapeDtypeStruct((rows, width), BF16)] * 2
    held = [own_rhs, keep, came, *first, *second]
    return kernel_call(body, outs, [at], held, [], [], keep.size, keep.size)


def stack(at, blocks, even, odd):
    rows, width = blocks[0].shape

    def body(at_ref, *refs):
        for ref, one, two in zip(refs, even, odd):
            refs[-1][half_rows(at_ref, rows, one, two), :] = ref[...]

    out = jax.ShapeDtypeStruct((len(blocks) * rows, width), BF16)
    return kernel_call(body, out, [at], blocks, [], [], 0, 4 * len(blocks) * rows * width)


def by_core(at, low, high):
    def body(at_ref, low_ref, high_ref, first_ref, second_ref):
        even = lax.rem(at_ref[1], 2) == 0

        @pl.when(even)
        def _():
            first_ref[...], second_ref[...] = high_ref[...], low_ref[...]

        @pl.when(jnp.logical_not(even))
        def _():
            first_ref[...], second_ref[...] = low_ref[...], high_ref[...]

    outs = [jax.ShapeDtypeStruct(low.shape, BF16)] * 2
    return kernel_call(body, outs, [at], [low, high], [], [], 0, 8 * low.size)


def again(low, high):
    def body(low_ref, high_ref, low_out_ref, high_out_ref):
        low_out_ref[...] = low_ref[...]
        high_out_ref[...] = high_ref[...]

    outs = [jax.ShapeDtypeStruct(low.shape, BF16)] * 2
    return kernel_call(body, outs, [], [low, high], [], [], 0, 8 * low.size)


def assemble(pieces, piece_refs, target_ref, sems, base):
    copies = []
    for (chip, core, row, rows, _), ref in zip(pieces, piece_refs):
        place = pl.ds(pl.multiple_of(base(2 * chip + core), rows), rows)
        source = ref.at[pl.ds(row, rows)]
        copies.append(pltpu.make_async_copy(source, target_ref.at[place], sems.at[len(copies)]))
    return copies


def root_products(at, inverse, pieces, offsets, kinds, n_row, n_front):
    span_rows = inverse.shape[1]
    rows = inverse.shape[0] // n_row
    width = pieces[0][-1].shape[1]
    piece_rows = span_rows // n_front
    count, many = len(offsets), len(pieces)

    def body(at_ref, a_ref, *refs):
        piece_refs, out_refs, (x_ref, sems) = refs[:many], refs[many : many + count], refs[many + count :]
        copies = assemble(
            pieces, piece_refs, x_ref, sems, lambda d: lax.bitwise_xor(at_ref[1], d) * piece_rows
        )
        for copy in copies:
            copy.start()
        for copy in copies:
            copy.wait()
        for offset, out_ref in zip(offsets, out_refs):
            place = pl.ds(pl.multiple_of(owner(at_ref, offset, n_row) * rows, rows), rows)
            out_ref[...] = dot(a_ref[place, :], x_ref[...]).astype(out_ref.dtype)

    outs = [jax.ShapeDtypeStruct((rows, width), kind) for kind in kinds]
    scratch = [pltpu.VMEM((span_rows, width), BF16), pltpu.SemaphoreType.DMA((many,))]
    share = 2 * rows * span_rows * count
    held = [inverse] + [block for *_, block in pieces]
    return kernel_call(body, outs, [at], held, [], scratch, share * width, share)


def border_pick(at, local_index, coupling, pieces, offset, n_row, n_front):
    rows, depth = coupling.shape[0], coupling.shape[1] // n_row
    piece_rows, width = pieces[0][3], pieces[0][-1].shape[1]
    span_rows = piece_rows * n_front
    many = len(pieces)

    def body(at_ref, index_ref, a_ref, *refs):
        piece_refs, (out_ref, picked_ref, span_ref, sems) = refs[:many], refs[many:]

        def base(d):
            there = lax.bitwise_xor(at_ref[1], d)
            return lax.rem(there, 2) * (span_rows // 2) + lax.shift_right_logical(there, 1) * piece_rows

        copies = assemble(pieces, piece_refs, span_ref, sems, base)
        for copy in copies:
            copy.start()
        for copy in copies:
            copy.wait()
        for j in range(rows // BLK):
            source = pl.ds(pl.multiple_of(index_ref[j] * BLK, BLK), BLK)
            picked_ref[:, pl.ds(j * BLK, BLK)] = jnp.transpose(span_ref[source, :])
        columns = pl.ds(pl.multiple_of(owner(at_ref, offset, n_row) * depth, depth), depth)
        out_ref[...] = dot(picked_ref[...], a_ref[:, columns]).astype(BF16)

    outs = [jax.ShapeDtypeStruct((width, depth), BF16), jax.ShapeDtypeStruct((width, rows), BF16)]
    scratch = [pltpu.VMEM((span_rows, width), BF16), pltpu.SemaphoreType.DMA((many,))]
    share = 2 * rows * depth
    held = [coupling] + [block for *_, block in pieces]
    return kernel_call(body, outs, [at, local_index], held, [], scratch, share * width, share)


def border_backward(at, coupling, picked, offsets, kinds, n_row):
    rows, depth = coupling.shape[0], coupling.shape[1] // n_row
    width, count = picked.shape[0], len(offsets)

    def body(at_ref, x_ref, a_ref, *out_refs):
        for offset, out_ref in zip(offsets, out_refs):
            columns = pl.ds(pl.multiple_of(owner(at_ref, offset, n_row) * depth, depth), depth)
            out_ref[...] = dot(x_ref[...], a_ref[:, columns]).astype(out_ref.dtype)

    outs = [jax.ShapeDtypeStruct((width, depth), kind) for kind in kinds]
    share = 2 * rows * depth * count
    return kernel_call(body, outs, [at], [picked, coupling], [], [], share * width, share)


def solve(n_front, n_row, rhs_front, rhs_root, pivot_inverse, border_coupling, root_inverse, border_map):
    row_at = lax.axis_index("row").astype(jnp.int32)
    at = PLACE
    span_rows = root_inverse.shape[1]
    piece_rows, width = span_rows // n_front, rhs_front.shape[1]
    local_index = border_map[0] - row_at * (span_rows // BLK)
    first_at, later_at = far_offsets(n_row)
    block = jax.ShapeDtypeStruct((pivot_inverse.shape[0], width), F32)
    half = jax.ShapeDtypeStruct(block.shape, BF16)
    straight, across = ((1,), (0,)), ((1,), (1,))

    found = gather_row(rhs_front, n_row)
    early, last = found[:-1], found[-1:]
    partial = pivot_products(at, pivot_inverse, early, n_row, straight, lambda t: [t], [block])
    inner, inner_half = pivot_products(
        at,
        pivot_inverse,
        last,
        n_row,
        straight,
        lambda t, p: [t + p, (t + p).astype(BF16)],
        [block, half],
        partial,
    )
    found = gather_row(inner_half, n_row)
    partial, own_rhs = border_partial(at, border_coupling, found[:2], n_row, None, rhs_root, piece_rows)
    partial, inverse = border_partial(
        at, border_coupling, found[2:-1], n_row, partial, root_inverse, root_inverse.shape[0]
    )
    send, keep = border_scatter(
        at, local_index, border_coupling, found[-1:], partial, n_row, n_front, span_rows
    )
    came = swap(send, n_front, 1)
    low, high = sum_halves(at, keep, came, [(6, 7, None), (7, 6, None)])
    near, side = cross(low, n_front, 2, 4), cross(high, n_front, 4, 2)
    plain = sum_halves(at, keep, came, [(2, 5, None), (5, 2, None)])
    near_plain, side_plain = cross(plain[0], n_front, 2, 4), cross(plain[1], n_front, 4, 2)
    relayed = sum_halves(at, keep, came, [(4, 3, near), (3, 4, side)])
    side_sum, near_sum = cross(relayed[0], n_front, 4, 2), cross(relayed[1], n_front, 2, 4)
    halves = own_part(at, own_rhs, keep, came, (side_plain, near_sum), (near_plain, side_sum))
    pieces = gather_front(at, *halves, n_front)

    def root(offsets, kind):
        outs = root_products(at, inverse, pieces, offsets, [kind] * len(offsets), n_row, n_front)
        return dict(zip(offsets, outs))

    first = {}
    for offset in first_at:
        first.update(root([offset], BF16))
    rest = root(later_at + [0], F32)
    root_solution = scatter_row(first, rest, rest[0], n_row)
    spans = gather_front(at, *by_core(at, *to_plane(root_solution.astype(BF16), n_row)), n_front)

    out, picked = border_pick(at, local_index, border_coupling, spans, first_at[0], n_row, n_front)
    first = {first_at[0]: out}
    for offset in first_at[1:]:
        first[offset] = border_backward(at, border_coupling, picked, [offset], [BF16], n_row)[0]
    offsets = later_at + [0]
    rest = dict(zip(offsets, border_backward(at, border_coupling, picked, offsets, [F32] * len(offsets), n_row)))
    pulled = scatter_row(first, rest, rest[0], n_row).astype(BF16)
    found = gather_row(pulled, n_row)
    early, last = found[:-1], found[-1:]
    partial = pivot_products(
        at, pivot_inverse, early, n_row, across, lambda t, i: [i - t], [block], [inner]
    )
    front_solution = pivot_products(
        at, pivot_inverse, last, n_row, across, lambda t, p: [p - t], [block], partial, True
    )
    return front_solution[0], root_solution


def solve_plain(n_front, n_row, rhs_front, rhs_root, pivot_inverse, border_coupling, root_inverse, border_map):
    row_at = lax.axis_index("row")
    front_at = lax.axis_index("front")
    width = rhs_front.shape[1]
    inner = dot(pivot_inverse, lax.all_gather(rhs_front, "row", axis=0, tiled=True))
    contrib = dot(border_coupling, lax.all_gather(inner.astype(BF16), "row", axis=0, tiled=True))
    block_local = border_map.shape[1]
    span_rows = root_inverse.shape[1]
    span_blocks = span_rows // BLK
    local_index = border_map[0] - row_at * span_blocks
    select = (local_index[None, :] == jnp.arange(span_blocks, dtype=jnp.int32)[:, None]).astype(F32)
    dense = jnp.einsum(
        "kj,jcn->kcn", select, contrib.reshape(block_local, BLK, width), precision=lax.Precision.HIGHEST
    ).reshape(span_rows, width)
    shares = lax.psum_scatter(dense, "front", scatter_dimension=0, tiled=True)
    own_rhs = lax.dynamic_slice_in_dim(rhs_root, front_at * shares.shape[0], shares.shape[0], 0)
    schur_rhs = lax.all_gather((own_rhs - shares).astype(BF16), "front", axis=0, tiled=True)
    root_solution = lax.psum_scatter(dot(root_inverse, schur_rhs), "row", scatter_dimension=0, tiled=True)
    gathered = lax.all_gather(root_solution.astype(BF16), ("front", "row"), axis=0, tiled=True)
    ranged = lax.dynamic_slice_in_dim(gathered, row_at * span_rows, span_rows, 0)
    picked = jnp.take(ranged.reshape(span_blocks, BLK, width), local_index, axis=0)
    picked = picked.reshape(block_local * BLK, width)
    pulled = lax.psum_scatter(
        dot(border_coupling, picked, ((0,), (0,))), "row", scatter_dimension=0, tiled=True
    ).astype(BF16)
    correction = dot(pivot_inverse, lax.all_gather(pulled, "row", axis=0, tiled=True))
    return inner - correction, root_solution


def solution(mesh):
    in_specs = (
        P(("front", "row"), None),
        P("row", None),
        P(("front", "row"), None),
        P(("front", "row"), None),
        P("front", "row"),
        P("front", "row"),
    )
    out_specs = (P(("front", "row"), None), P(("front", "row"), None))
    n_front, n_row = mesh.shape["front"], mesh.shape["row"]

    def per_device(*arrays):
        root_inverse, width = arrays[4], arrays[0].shape[1]
        fits = (
            n_front == 8
            and n_front == 2 * n_row
            and root_inverse.shape[1] % (n_front * BLK) == 0
            and root_inverse.shape[0] == n_row * (root_inverse.shape[1] // n_front)
            and root_inverse.shape[1] % (n_front * n_row * 16) == 0
            and arrays[2].shape[1] % (n_row * BLK) == 0
            and width % BLK == 0
        )
        return (solve if fits else solve_plain)(n_front, n_row, *arrays)

    return jax.shard_map(per_device, mesh=mesh, in_specs=in_specs, out_specs=out_specs, check_vma=False)
```

```python
import math

import jax
import jax.numpy as jnp
from jax import lax
from jax.experimental import pallas as pl
from jax.experimental.pallas import tpu as pltpu
from jax.sharding import PartitionSpec as P

BLK = 128
F32 = jnp.float32
BF16 = jnp.bfloat16
PLACE = ("row", "front")
VMEM = pl.BlockSpec(memory_space=pltpu.VMEM)
ANY = pl.BlockSpec(memory_space=pl.ANY)


def dot(a, b, contract=((1,), (0,))):
    return lax.dot_general(a, b, (contract, ((), ())), preferred_element_type=F32)


def in_hbm(x):
    return pltpu.with_memory_space_constraint(x, pltpu.HBM)


def kernel_call(body, outs, scalars, held, placed, scratch, flops, nbytes, final=False, loose=()):
    size = sum(2 * math.prod(s.shape) for s in scratch if s.dtype == BF16)
    if scalars and scalars[0] is PLACE:
        scalars = scalars[1:]

        def placed_body(*refs):
            body([lax.axis_index(name) for name in PLACE], *refs)

    else:
        placed_body = body
    single = not isinstance(outs, list)
    out_shape = [o if final else pltpu.VMEM(o.shape, o.dtype) for o in ([outs] if single else outs)]
    results = pl.pallas_call(
        placed_body,
        out_shape=out_shape,
        grid_spec=pltpu.PrefetchScalarGridSpec(
            num_scalar_prefetch=len(scalars),
            grid=(1,),
            in_specs=[VMEM] * (len(held) + len(loose)) + [ANY] * len(placed),
            out_specs=[VMEM] * len(out_shape),
            scratch_shapes=scratch,
        ),
        compiler_params=pltpu.CompilerParams(vmem_limit_bytes=size + 12 * 1024 * 1024),
        cost_estimate=pl.CostEstimate(flops=flops, bytes_accessed=nbytes, transcendentals=0),
    )(*scalars, *[pltpu.with_memory_space_constraint(x, pltpu.VMEM) for x in held], *loose, *placed)
    return results[0] if single else results


def shift(x, size, by):
    return lax.ppermute(x, "row", [(i, (i + by) % size) for i in range(size)])


def swap(x, size, by):
    return lax.ppermute(x, "front", [(i, i ^ by) for i in range(size)])


def gather_row(x, n):
    found = [(0, x)]
    up, down = x, x
    for step in range(1, n // 2 + 1):
        up = shift(up, n, 1)
        found.append((-step, up))
        if step < n - step:
            down = shift(down, n, -1)
            found.append((step, down))
    return found


def gather_front(low, high, n):
    rows = low.shape[0]
    x_high, y_low = swap(high, n, 2), swap(low, n, 4)
    low, high = again(low, high)
    x_low, y_high = swap(low, n, 2), swap(high, n, 4)
    corner_low, corner_high = swap(y_low, n, 2), swap(x_high, n, 4)
    mine = stack([low, high, x_low, x_high, y_low, y_high, corner_low, corner_high])
    return [
        (chip, core, chip * 2 * rows, 2 * rows, blocks)
        for core, blocks in ((0, mine), (1, swap(mine, n, 1)))
        for chip in range(4)
    ]


def to_plane(x, n):
    rows = x.shape[0] // n
    moved = []
    for k in range(n):
        quarter = x[k * rows : (k + 1) * rows]
        if k:
            quarter = swap(quarter, 2 * n, 2 * k)
        perm = [
            ((chip * 2 + core) * n + row, (row * 2 + core) * n + (chip ^ k))
            for chip in range(n)
            for core in range(2)
            for row in range(n)
        ]
        moved.append(lax.ppermute(quarter, ("front", "row"), perm))
    half = n // 2
    return [jnp.concatenate(some, axis=0) for some in (moved[:half], moved[half:])]


def far_offsets(n):
    first = [-(n // 2)] + ([(n - 1) // 2] if n > 2 else [])
    later = [o for o in range(-(n // 2) + 1, (n - 1) // 2) if o]
    return first, later


def scatter_row(first, later, own, n):
    total = own
    for sign, far in ((-1, n // 2), (1, (n - 1) // 2)):
        running = None
        for step in range(far, 0, -1):
            if running is None:
                running = first[sign * step]
            else:
                running = (running.astype(F32) + later[sign * step]).astype(BF16)
            running = shift(running, n, sign)
        if running is not None:
            total = total + running.astype(F32)
    return total


def owner(at_ref, offset, n_row):
    return lax.rem(at_ref[0] + (offset + n_row), n_row)


def products(at_ref, a_ref, rows, offsets, x_refs, n_row, contract):
    depth = a_ref.shape[1] // n_row
    total = None
    for offset, x_ref in zip(offsets, x_refs):
        columns = pl.ds(pl.multiple_of(owner(at_ref, offset, n_row) * depth, depth), depth)
        part = dot(a_ref[rows, columns], x_ref[...], contract)
        total = part if total is None else total + part
    return total


def pivot_products(at, pivot, found, n_row, contract, finish, outs, extra=(), final=False):
    count = len(found)
    offsets = [o for o, _ in found]

    def body(at_ref, a_ref, *refs):
        extras, x_refs = refs[: len(extra)], refs[len(extra) : len(extra) + count]
        total = products(at_ref, a_ref, slice(None), offsets, x_refs, n_row, contract)
        for ref, value in zip(refs[count + len(extra) :], finish(total, *[e[...] for e in extras])):
            ref[...] = value

    share = 2 * pivot.size * count // n_row
    held = [pivot] + list(extra)
    blocks = [x for _, x in found]
    return kernel_call(body, outs, [at], held, [], [], share * outs[0].shape[1], share, final, blocks)


def border_tile(rows):
    return BLK * next(k for k in (4, 3, 2, 1) if rows // BLK % k == 0)


def border_partial(at, coupling, found, n_row, partial, source, fetch_rows):
    rows, count, width = coupling.shape[0], len(found), found[0][1].shape[1]
    offsets = [o for o, _ in found]
    tile = border_tile(rows)
    held = [coupling] + [x for _, x in found] + ([] if partial is None else [partial])

    def body(at_ref, a_ref, *refs):
        source_hbm, out_ref, own_ref, sem = refs[-4:]
        if fetch_rows < source.shape[0]:
            source_hbm = source_hbm.at[pl.ds(pl.multiple_of(at_ref[1] * fetch_rows, fetch_rows), fetch_rows)]
        copy = pltpu.make_async_copy(source_hbm, own_ref, sem)
        copy.start()

        @pl.loop(0, rows // tile)
        def _(i):
            place = pl.ds(pl.multiple_of(i * tile, tile), tile)
            total = products(at_ref, a_ref, place, offsets, refs[:count], n_row, ((1,), (0,)))
            out_ref[place, :] = total if partial is None else refs[count][place, :] + total

        copy.wait()

    share = 2 * coupling.size * count // n_row
    outs = [
        jax.ShapeDtypeStruct((rows, width), F32),
        jax.ShapeDtypeStruct((fetch_rows, source.shape[1]), source.dtype),
    ]
    scratch = [pltpu.SemaphoreType.DMA]
    return kernel_call(body, outs, [at], held, [in_hbm(source)], scratch, share * width, share)


def border_scatter(at, local_index, coupling, found, partial, n_row, n_front, span_rows):
    rows, count, width = coupling.shape[0], len(found), found[0][1].shape[1]
    offsets = [o for o, _ in found]
    tile = border_tile(rows)
    piece_blocks = span_rows // n_front // BLK

    def body(at_ref, index_ref, a_ref, *refs):
        partial_ref, send_ref, keep_ref = refs[count:]
        send_ref[...] = jnp.zeros_like(send_ref)
        keep_ref[...] = jnp.zeros_like(keep_ref)

        @pl.loop(0, rows // tile)
        def _(i):
            place = pl.ds(pl.multiple_of(i * tile, tile), tile)
            total = products(at_ref, a_ref, place, offsets, refs[:count], n_row, ((1,), (0,)))
            total = (partial_ref[place, :] + total).astype(BF16)
            for j in range(tile // BLK):
                target = index_ref[i * (tile // BLK) + j]
                there = lax.div(target, piece_blocks)
                chip = lax.shift_right_logical(lax.bitwise_xor(there, at_ref[1]), 1)
                slot = chip * piece_blocks + lax.rem(target, piece_blocks)
                goal = pl.ds(pl.multiple_of(slot * BLK, BLK), BLK)
                block = total[j * BLK : (j + 1) * BLK]
                away = lax.rem(there + at_ref[1], 2)

                @pl.when(away == 1)
                def _():
                    send_ref[goal, :] = block

                @pl.when(away == 0)
                def _():
                    keep_ref[goal, :] = block

    half = jax.ShapeDtypeStruct((span_rows // 2, width), BF16)
    share = 2 * coupling.size * count // n_row
    held = [coupling] + [x for _, x in found] + [partial]
    return kernel_call(body, [half, half], [at, local_index], held, [], [], share * width, share)


def added(*parts):
    total = parts[0].astype(F32)
    for part in parts[1:]:
        total = total + part.astype(F32)
    return total


def sum_halves(keep, came, halves):
    rows, width = keep.shape[0] // 8, keep.shape[1]
    outs = [jax.ShapeDtypeStruct((rows, width), BF16)] * len(halves)

    def body(keep_ref, came_ref, *out_refs):
        for (chip, which), out_ref in zip(halves, out_refs):
            place = slice((2 * chip + which) * rows, (2 * chip + which + 1) * rows)
            out_ref[...] = added(keep_ref[place, :], came_ref[place, :]).astype(BF16)

    return kernel_call(body, outs, [], [keep, came], [], [], keep.size, keep.size)


def sum_relayed(keep, came, low, high):
    rows, width = low.shape

    def body(keep_ref, came_ref, low_ref, high_ref, x_ref, y_ref):
        for half, add_ref, out_ref in ((3, high_ref, x_ref), (4, low_ref, y_ref)):
            place = slice(half * rows, (half + 1) * rows)
            out_ref[...] = added(keep_ref[place, :], came_ref[place, :], add_ref[...]).astype(BF16)

    outs = [jax.ShapeDtypeStruct((rows, width), BF16)] * 2
    return kernel_call(body, outs, [], [keep, came, low, high], [], [], 2 * keep.size, 2 * keep.size)


def own_part(own_rhs, keep, came, low, high):
    half, width = own_rhs.shape[0] // 2, own_rhs.shape[1]

    def body(rhs_ref, keep_ref, came_ref, *refs):
        *add_refs, low_ref, high_ref = refs
        for start, adds, out_ref in ((0, add_refs[:2], low_ref), (half, add_refs[2:], high_ref)):
            place = slice(start, start + half)
            total = added(keep_ref[place, :], came_ref[place, :], *[ref[...] for ref in adds])
            out_ref[...] = (rhs_ref[place, :] - total).astype(BF16)

    outs = [jax.ShapeDtypeStruct((half, width), BF16)] * 2
    return kernel_call(body, outs, [], [own_rhs, keep, came, *low, *high], [], [], keep.size, keep.size)


def stack(blocks):
    rows, width = blocks[0].shape

    def body(*refs):
        for i, ref in enumerate(refs[:-1]):
            refs[-1][i * rows : (i + 1) * rows, :] = ref[...]

    out = jax.ShapeDtypeStruct((len(blocks) * rows, width), BF16)
    return kernel_call(body, out, [], blocks, [], [], 0, 4 * len(blocks) * rows * width)


def again(low, high):
    def body(low_ref, high_ref, low_out_ref, high_out_ref):
        low_out_ref[...] = low_ref[...]
        high_out_ref[...] = high_ref[...]

    outs = [jax.ShapeDtypeStruct(low.shape, BF16)] * 2
    return kernel_call(body, outs, [], [low, high], [], [], 0, 8 * low.size)


def assemble(pieces, piece_refs, target_ref, sems, base):
    copies = []
    for (chip, core, row, rows, _), ref in zip(pieces, piece_refs):
        place = pl.ds(pl.multiple_of(base(2 * chip + core), rows), rows)
        source = ref.at[pl.ds(row, rows)]
        copies.append(pltpu.make_async_copy(source, target_ref.at[place], sems.at[len(copies)]))
    return copies


def root_products(at, inverse, pieces, offsets, kinds, n_row, n_front):
    span_rows = inverse.shape[1]
    rows = inverse.shape[0] // n_row
    width = pieces[0][-1].shape[1]
    piece_rows = span_rows // n_front
    count, many = len(offsets), len(pieces)

    def body(at_ref, a_ref, *refs):
        piece_refs, out_refs, (x_ref, sems) = refs[:many], refs[many : many + count], refs[many + count :]
        copies = assemble(
            pieces, piece_refs, x_ref, sems, lambda d: lax.bitwise_xor(at_ref[1], d) * piece_rows
        )
        for copy in copies:
            copy.start()
        for copy in copies:
            copy.wait()
        for offset, out_ref in zip(offsets, out_refs):
            place = pl.ds(pl.multiple_of(owner(at_ref, offset, n_row) * rows, rows), rows)
            out_ref[...] = dot(a_ref[place, :], x_ref[...]).astype(out_ref.dtype)

    outs = [jax.ShapeDtypeStruct((rows, width), kind) for kind in kinds]
    scratch = [pltpu.VMEM((span_rows, width), BF16), pltpu.SemaphoreType.DMA((many,))]
    share = 2 * rows * span_rows * count
    held = [inverse] + [block for *_, block in pieces]
    return kernel_call(body, outs, [at], held, [], scratch, share * width, share)


def border_pick(at, local_index, coupling, pieces, offset, n_row, n_front):
    rows, depth = coupling.shape[0], coupling.shape[1] // n_row
    piece_rows, width = pieces[0][3], pieces[0][-1].shape[1]
    span_rows = piece_rows * n_front
    many = len(pieces)

    def body(at_ref, index_ref, a_ref, *refs):
        piece_refs, (out_ref, picked_ref, span_ref, sems) = refs[:many], refs[many:]

        def base(d):
            there = lax.bitwise_xor(at_ref[1], d)
            return lax.rem(there, 2) * (span_rows // 2) + lax.shift_right_logical(there, 1) * piece_rows

        copies = assemble(pieces, piece_refs, span_ref, sems, base)
        for copy in copies:
            copy.start()
        for copy in copies:
            copy.wait()
        for j in range(rows // BLK):
            source = pl.ds(pl.multiple_of(index_ref[j] * BLK, BLK), BLK)
            picked_ref[:, pl.ds(j * BLK, BLK)] = jnp.transpose(span_ref[source, :])
        columns = pl.ds(pl.multiple_of(owner(at_ref, offset, n_row) * depth, depth), depth)
        out_ref[...] = dot(picked_ref[...], a_ref[:, columns]).astype(BF16)

    outs = [jax.ShapeDtypeStruct((width, depth), BF16), jax.ShapeDtypeStruct((width, rows), BF16)]
    scratch = [pltpu.VMEM((span_rows, width), BF16), pltpu.SemaphoreType.DMA((many,))]
    share = 2 * rows * depth
    held = [coupling] + [block for *_, block in pieces]
    return kernel_call(body, outs, [at, local_index], held, [], scratch, share * width, share)


def border_backward(at, coupling, picked, offsets, kinds, n_row):
    rows, depth = coupling.shape[0], coupling.shape[1] // n_row
    width, count = picked.shape[0], len(offsets)

    def body(at_ref, x_ref, a_ref, *out_refs):
        for offset, out_ref in zip(offsets, out_refs):
            columns = pl.ds(pl.multiple_of(owner(at_ref, offset, n_row) * depth, depth), depth)
            out_ref[...] = dot(x_ref[...], a_ref[:, columns]).astype(out_ref.dtype)

    outs = [jax.ShapeDtypeStruct((width, depth), kind) for kind in kinds]
    share = 2 * rows * depth * count
    return kernel_call(body, outs, [at], [picked, coupling], [], [], share * width, share)


def solve(n_front, n_row, rhs_front, rhs_root, pivot_inverse, border_coupling, root_inverse, border_map):
    row_at = lax.axis_index("row").astype(jnp.int32)
    at = PLACE
    span_rows = root_inverse.shape[1]
    piece_rows, width = span_rows // n_front, rhs_front.shape[1]
    local_index = border_map[0] - row_at * (span_rows // BLK)
    first_at, later_at = far_offsets(n_row)
    block = jax.ShapeDtypeStruct((pivot_inverse.shape[0], width), F32)
    half = jax.ShapeDtypeStruct(block.shape, BF16)
    straight, across = ((1,), (0,)), ((1,), (1,))

    found = gather_row(rhs_front, n_row)
    early, last = found[:-1], found[-1:]
    partial = pivot_products(at, pivot_inverse, early, n_row, straight, lambda t: [t], [block])
    inner, inner_half = pivot_products(
        at,
        pivot_inverse,
        last,
        n_row,
        straight,
        lambda t, p: [t + p, (t + p).astype(BF16)],
        [block, half],
        partial,
    )
    found = gather_row(inner_half, n_row)
    partial, own_rhs = border_partial(at, border_coupling, found[:2], n_row, None, rhs_root, piece_rows)
    partial, inverse = border_partial(
        at, border_coupling, found[2:-1], n_row, partial, root_inverse, root_inverse.shape[0]
    )
    send, keep = border_scatter(
        at, local_index, border_coupling, found[-1:], partial, n_row, n_front, span_rows
    )
    came = swap(send, n_front, 1)
    low, high = sum_halves(keep, came, [(3, 0), (3, 1)])
    low, high = swap(low, n_front, 2), swap(high, n_front, 4)
    x_low, y_high = sum_halves(keep, came, [(1, 0), (2, 1)])
    x_low, y_high = swap(x_low, n_front, 2), swap(y_high, n_front, 4)
    x_high, y_low = sum_relayed(keep, came, low, high)
    x_high, y_low = swap(x_high, n_front, 2), swap(y_low, n_front, 4)
    pieces = gather_front(*own_part(own_rhs, keep, came, (x_low, y_low), (x_high, y_high)), n_front)

    def root(offsets, kind):
        outs = root_products(at, inverse, pieces, offsets, [kind] * len(offsets), n_row, n_front)
        return dict(zip(offsets, outs))

    first = {}
    for offset in first_at:
        first.update(root([offset], BF16))
    rest = root(later_at + [0], F32)
    root_solution = scatter_row(first, rest, rest[0], n_row)
    spans = gather_front(*to_plane(root_solution.astype(BF16), n_row), n_front)

    out, picked = border_pick(at, local_index, border_coupling, spans, first_at[0], n_row, n_front)
    first = {first_at[0]: out}
    for offset in first_at[1:]:
        first[offset] = border_backward(at, border_coupling, picked, [offset], [BF16], n_row)[0]
    offsets = later_at + [0]
    rest = dict(zip(offsets, border_backward(at, border_coupling, picked, offsets, [F32] * len(offsets), n_row)))
    pulled = scatter_row(first, rest, rest[0], n_row).astype(BF16)
    found = gather_row(pulled, n_row)
    early, last = found[:-1], found[-1:]
    partial = pivot_products(
        at, pivot_inverse, early, n_row, across, lambda t, i: [i - t], [block], [inner]
    )
    front_solution = pivot_products(
        at, pivot_inverse, last, n_row, across, lambda t, p: [p - t], [block], partial, True
    )
    return front_solution[0], root_solution


def solve_plain(n_front, n_row, rhs_front, rhs_root, pivot_inverse, border_coupling, root_inverse, border_map):
    row_at = lax.axis_index("row")
    front_at = lax.axis_index("front")
    width = rhs_front.shape[1]
    inner = dot(pivot_inverse, lax.all_gather(rhs_front, "row", axis=0, tiled=True))
    contrib = dot(border_coupling, lax.all_gather(inner.astype(BF16), "row", axis=0, tiled=True))
    block_local = border_map.shape[1]
    span_rows = root_inverse.shape[1]
    span_blocks = span_rows // BLK
    local_index = border_map[0] - row_at * span_blocks
    select = (local_index[None, :] == jnp.arange(span_blocks, dtype=jnp.int32)[:, None]).astype(F32)
    dense = jnp.einsum(
        "kj,jcn->kcn", select, contrib.reshape(block_local, BLK, width), precision=lax.Precision.HIGHEST
    ).reshape(span_rows, width)
    shares = lax.psum_scatter(dense, "front", scatter_dimension=0, tiled=True)
    own_rhs = lax.dynamic_slice_in_dim(rhs_root, front_at * shares.shape[0], shares.shape[0], 0)
    schur_rhs = lax.all_gather((own_rhs - shares).astype(BF16), "front", axis=0, tiled=True)
    root_solution = lax.psum_scatter(dot(root_inverse, schur_rhs), "row", scatter_dimension=0, tiled=True)
    gathered = lax.all_gather(root_solution.astype(BF16), ("front", "row"), axis=0, tiled=True)
    ranged = lax.dynamic_slice_in_dim(gathered, row_at * span_rows, span_rows, 0)
    picked = jnp.take(ranged.reshape(span_blocks, BLK, width), local_index, axis=0)
    picked = picked.reshape(block_local * BLK, width)
    pulled = lax.psum_scatter(
        dot(border_coupling, picked, ((0,), (0,))), "row", scatter_dimension=0, tiled=True
    ).astype(BF16)
    correction = dot(pivot_inverse, lax.all_gather(pulled, "row", axis=0, tiled=True))
    return inner - correction, root_solution


def solution(mesh):
    in_specs = (
        P(("front", "row"), None),
        P("row", None),
        P(("front", "row"), None),
        P(("front", "row"), None),
        P("front", "row"),
        P("front", "row"),
    )
    out_specs = (P(("front", "row"), None), P(("front", "row"), None))
    n_front, n_row = mesh.shape["front"], mesh.shape["row"]

    def per_device(*arrays):
        root_inverse, width = arrays[4], arrays[0].shape[1]
        fits = (
            n_front == 8
            and n_front == 2 * n_row
            and root_inverse.shape[1] % (n_front * BLK) == 0
            and root_inverse.shape[0] == n_row * (root_inverse.shape[1] // n_front)
            and root_inverse.shape[1] % (n_front * n_row * 16) == 0
            and arrays[2].shape[1] % (n_row * BLK) == 0
            and width % BLK == 0
        )
        return (solve if fits else solve_plain)(n_front, n_row, *arrays)

    return jax.shard_map(per_device, mesh=mesh, in_specs=in_specs, out_specs=out_specs, check_vma=False)
```

```python
import math

import jax
import jax.numpy as jnp
from jax import lax
from jax.experimental import pallas as pl
from jax.experimental.pallas import tpu as pltpu
from jax.sharding import PartitionSpec as P

BLK = 128
F32 = jnp.float32
BF16 = jnp.bfloat16
PLACE = ("row", "front")
VMEM = pl.BlockSpec(memory_space=pltpu.VMEM)
ANY = pl.BlockSpec(memory_space=pl.ANY)


def dot(a, b, contract=((1,), (0,))):
    return lax.dot_general(a, b, (contract, ((), ())), preferred_element_type=F32)


def in_hbm(x):
    return pltpu.with_memory_space_constraint(x, pltpu.HBM)


def kernel_call(body, outs, scalars, held, placed, scratch, flops, nbytes, final=False, loose=()):
    size = sum(2 * math.prod(s.shape) for s in scratch if s.dtype == BF16)
    if scalars and scalars[0] is PLACE:
        scalars = scalars[1:]

        def placed_body(*refs):
            body([lax.axis_index(name) for name in PLACE], *refs)

    else:
        placed_body = body
    single = not isinstance(outs, list)
    out_shape = [o if final else pltpu.VMEM(o.shape, o.dtype) for o in ([outs] if single else outs)]
    results = pl.pallas_call(
        placed_body,
        out_shape=out_shape,
        grid_spec=pltpu.PrefetchScalarGridSpec(
            num_scalar_prefetch=len(scalars),
            grid=(1,),
            in_specs=[VMEM] * (len(held) + len(loose)) + [ANY] * len(placed),
            out_specs=[VMEM] * len(out_shape),
            scratch_shapes=scratch,
        ),
        compiler_params=pltpu.CompilerParams(vmem_limit_bytes=size + 12 * 1024 * 1024),
        cost_estimate=pl.CostEstimate(flops=flops, bytes_accessed=nbytes, transcendentals=0),
    )(*scalars, *[pltpu.with_memory_space_constraint(x, pltpu.VMEM) for x in held], *loose, *placed)
    return results[0] if single else results


def shift(x, size, by):
    return lax.ppermute(x, "row", [(i, (i + by) % size) for i in range(size)])


def swap(x, size, by):
    return lax.ppermute(x, "front", [(i, i ^ by) for i in range(size)])


def gather_row(x, n):
    found = [(0, x)]
    up, down = x, x
    for step in range(1, n // 2 + 1):
        up = shift(up, n, 1)
        found.append((-step, up))
        if step < n - step:
            down = shift(down, n, -1)
            found.append((step, down))
    return found


def gather_front(low, high, n):
    rows = low.shape[0]
    x_high, y_low = swap(high, n, 2), swap(low, n, 4)
    low, high = again(low, high)
    x_low, y_high = swap(low, n, 2), swap(high, n, 4)
    corner_low, corner_high = swap(y_low, n, 2), swap(x_high, n, 4)
    mine = stack([low, high, x_low, x_high, y_low, y_high, corner_low, corner_high])
    return [
        (chip, core, chip * 2 * rows, 2 * rows, blocks)
        for core, blocks in ((0, mine), (1, swap(mine, n, 1)))
        for chip in range(4)
    ]


def to_plane(x, n):
    rows = x.shape[0] // n
    moved = []
    for k in range(n):
        quarter = x[k * rows : (k + 1) * rows]
        if k:
            quarter = swap(quarter, 2 * n, 2 * k)
        perm = [
            ((chip * 2 + core) * n + row, (row * 2 + core) * n + (chip ^ k))
            for chip in range(n)
            for core in range(2)
            for row in range(n)
        ]
        moved.append(lax.ppermute(quarter, ("front", "row"), perm))
    half = n // 2
    return [jnp.concatenate(some, axis=0) for some in (moved[:half], moved[half:])]


def far_offsets(n):
    first = [-(n // 2)] + ([(n - 1) // 2] if n > 2 else [])
    later = [o for o in range(-(n // 2) + 1, (n - 1) // 2) if o]
    return first, later


def scatter_row(first, later, own, n):
    total = own
    for sign, far in ((-1, n // 2), (1, (n - 1) // 2)):
        running = None
        for step in range(far, 0, -1):
            if running is None:
                running = first[sign * step]
            else:
                running = (running.astype(F32) + later[sign * step]).astype(BF16)
            running = shift(running, n, sign)
        if running is not None:
            total = total + running.astype(F32)
    return total


def owner(at_ref, offset, n_row):
    return lax.rem(at_ref[0] + (offset + n_row), n_row)


def products(at_ref, a_ref, rows, offsets, x_refs, n_row, contract):
    depth = a_ref.shape[1] // n_row
    total = None
    for offset, x_ref in zip(offsets, x_refs):
        columns = pl.ds(pl.multiple_of(owner(at_ref, offset, n_row) * depth, depth), depth)
        part = dot(a_ref[rows, columns], x_ref[...], contract)
        total = part if total is None else total + part
    return total


def pivot_products(at, pivot, found, n_row, contract, finish, outs, extra=(), final=False):
    count = len(found)
    offsets = [o for o, _ in found]

    def body(at_ref, a_ref, *refs):
        extras, x_refs = refs[: len(extra)], refs[len(extra) : len(extra) + count]
        total = products(at_ref, a_ref, slice(None), offsets, x_refs, n_row, contract)
        for ref, value in zip(refs[count + len(extra) :], finish(total, *[e[...] for e in extras])):
            ref[...] = value

    share = 2 * pivot.size * count // n_row
    held = [pivot] + list(extra)
    blocks = [x for _, x in found]
    return kernel_call(body, outs, [at], held, [], [], share * outs[0].shape[1], share, final, blocks)


def border_tile(rows):
    return BLK * next(k for k in (6, 4, 3, 2, 1) if rows // BLK % k == 0)


def border_partial(at, coupling, found, n_row, partial, source, fetch_rows):
    rows, count, width = coupling.shape[0], len(found), found[0][1].shape[1]
    offsets = [o for o, _ in found]
    tile = border_tile(rows)
    held = [coupling] + [x for _, x in found] + ([] if partial is None else [partial])

    def body(at_ref, a_ref, *refs):
        source_hbm, out_ref, own_ref, sem = refs[-4:]
        if fetch_rows < source.shape[0]:
            source_hbm = source_hbm.at[pl.ds(pl.multiple_of(at_ref[1] * fetch_rows, fetch_rows), fetch_rows)]
        copy = pltpu.make_async_copy(source_hbm, own_ref, sem)
        copy.start()

        @pl.loop(0, rows // tile)
        def _(i):
            place = pl.ds(pl.multiple_of(i * tile, tile), tile)
            total = products(at_ref, a_ref, place, offsets, refs[:count], n_row, ((1,), (0,)))
            out_ref[place, :] = total if partial is None else refs[count][place, :] + total

        copy.wait()

    share = 2 * coupling.size * count // n_row
    outs = [
        jax.ShapeDtypeStruct((rows, width), F32),
        jax.ShapeDtypeStruct((fetch_rows, source.shape[1]), source.dtype),
    ]
    scratch = [pltpu.SemaphoreType.DMA]
    return kernel_call(body, outs, [at], held, [in_hbm(source)], scratch, share * width, share)


def border_scatter(at, local_index, coupling, found, partial, n_row, n_front, span_rows):
    rows, count, width = coupling.shape[0], len(found), found[0][1].shape[1]
    offsets = [o for o, _ in found]
    tile = border_tile(rows)
    piece_blocks = span_rows // n_front // BLK

    def body(at_ref, index_ref, a_ref, *refs):
        partial_ref, send_ref, keep_ref = refs[count:]
        send_ref[...] = jnp.zeros_like(send_ref)
        keep_ref[...] = jnp.zeros_like(keep_ref)

        @pl.loop(0, rows // tile)
        def _(i):
            place = pl.ds(pl.multiple_of(i * tile, tile), tile)
            total = products(at_ref, a_ref, place, offsets, refs[:count], n_row, ((1,), (0,)))
            total = (partial_ref[place, :] + total).astype(BF16)
            for j in range(tile // BLK):
                target = index_ref[i * (tile // BLK) + j]
                there = lax.div(target, piece_blocks)
                chip = lax.shift_right_logical(lax.bitwise_xor(there, at_ref[1]), 1)
                slot = chip * piece_blocks + lax.rem(target, piece_blocks)
                goal = pl.ds(pl.multiple_of(slot * BLK, BLK), BLK)
                block = total[j * BLK : (j + 1) * BLK]
                away = lax.rem(there + at_ref[1], 2)

                @pl.when(away == 1)
                def _():
                    send_ref[goal, :] = block

                @pl.when(away == 0)
                def _():
                    keep_ref[goal, :] = block

    half = jax.ShapeDtypeStruct((span_rows // 2, width), BF16)
    share = 2 * coupling.size * count // n_row
    held = [coupling] + [x for _, x in found] + [partial]
    return kernel_call(body, [half, half], [at, local_index], held, [], [], share * width, share)


def added(*parts):
    total = parts[0].astype(F32)
    for part in parts[1:]:
        total = total + part.astype(F32)
    return total


def sum_halves(keep, came, halves):
    rows, width = keep.shape[0] // 8, keep.shape[1]
    outs = [jax.ShapeDtypeStruct((rows, width), BF16)] * len(halves)

    def body(keep_ref, came_ref, *out_refs):
        for (chip, which), out_ref in zip(halves, out_refs):
            place = slice((2 * chip + which) * rows, (2 * chip + which + 1) * rows)
            out_ref[...] = added(keep_ref[place, :], came_ref[place, :]).astype(BF16)

    return kernel_call(body, outs, [], [keep, came], [], [], keep.size, keep.size)


def sum_relayed(keep, came, low, high):
    rows, width = low.shape

    def body(keep_ref, came_ref, low_ref, high_ref, x_ref, y_ref):
        for half, add_ref, out_ref in ((3, high_ref, x_ref), (4, low_ref, y_ref)):
            place = slice(half * rows, (half + 1) * rows)
            out_ref[...] = added(keep_ref[place, :], came_ref[place, :], add_ref[...]).astype(BF16)

    outs = [jax.ShapeDtypeStruct((rows, width), BF16)] * 2
    return kernel_call(body, outs, [], [keep, came, low, high], [], [], 2 * keep.size, 2 * keep.size)


def own_part(own_rhs, keep, came, low, high):
    half, width = own_rhs.shape[0] // 2, own_rhs.shape[1]

    def body(rhs_ref, keep_ref, came_ref, *refs):
        *add_refs, low_ref, high_ref = refs
        for start, adds, out_ref in ((0, add_refs[:2], low_ref), (half, add_refs[2:], high_ref)):
            place = slice(start, start + half)
            total = added(keep_ref[place, :], came_ref[place, :], *[ref[...] for ref in adds])
            out_ref[...] = (rhs_ref[place, :] - total).astype(BF16)

    outs = [jax.ShapeDtypeStruct((half, width), BF16)] * 2
    return kernel_call(body, outs, [], [own_rhs, keep, came, *low, *high], [], [], keep.size, keep.size)


def stack(blocks):
    rows, width = blocks[0].shape

    def body(*refs):
        for i, ref in enumerate(refs[:-1]):
            refs[-1][i * rows : (i + 1) * rows, :] = ref[...]

    out = jax.ShapeDtypeStruct((len(blocks) * rows, width), BF16)
    return kernel_call(body, out, [], blocks, [], [], 0, 4 * len(blocks) * rows * width)


def again(low, high):
    def body(low_ref, high_ref, low_out_ref, high_out_ref):
        low_out_ref[...] = low_ref[...]
        high_out_ref[...] = high_ref[...]

    outs = [jax.ShapeDtypeStruct(low.shape, BF16)] * 2
    return kernel_call(body, outs, [], [low, high], [], [], 0, 8 * low.size)


def assemble(pieces, piece_refs, target_ref, sems, base):
    copies = []
    for (chip, core, row, rows, _), ref in zip(pieces, piece_refs):
        place = pl.ds(pl.multiple_of(base(2 * chip + core), rows), rows)
        source = ref.at[pl.ds(row, rows)]
        copies.append(pltpu.make_async_copy(source, target_ref.at[place], sems.at[len(copies)]))
    return copies


def root_products(at, inverse, pieces, offsets, kinds, n_row, n_front):
    span_rows = inverse.shape[1]
    rows = inverse.shape[0] // n_row
    width = pieces[0][-1].shape[1]
    piece_rows = span_rows // n_front
    count, many = len(offsets), len(pieces)

    def body(at_ref, a_ref, *refs):
        piece_refs, out_refs, (x_ref, sems) = refs[:many], refs[many : many + count], refs[many + count :]
        copies = assemble(
            pieces, piece_refs, x_ref, sems, lambda d: lax.bitwise_xor(at_ref[1], d) * piece_rows
        )
        for copy in copies:
            copy.start()
        for copy in copies:
            copy.wait()
        for offset, out_ref in zip(offsets, out_refs):
            place = pl.ds(pl.multiple_of(owner(at_ref, offset, n_row) * rows, rows), rows)
            out_ref[...] = dot(a_ref[place, :], x_ref[...]).astype(out_ref.dtype)

    outs = [jax.ShapeDtypeStruct((rows, width), kind) for kind in kinds]
    scratch = [pltpu.VMEM((span_rows, width), BF16), pltpu.SemaphoreType.DMA((many,))]
    share = 2 * rows * span_rows * count
    held = [inverse] + [block for *_, block in pieces]
    return kernel_call(body, outs, [at], held, [], scratch, share * width, share)


def border_pick(at, local_index, coupling, pieces, offset, n_row, n_front):
    rows, depth = coupling.shape[0], coupling.shape[1] // n_row
    piece_rows, width = pieces[0][3], pieces[0][-1].shape[1]
    span_rows = piece_rows * n_front
    many = len(pieces)

    def body(at_ref, index_ref, a_ref, *refs):
        piece_refs, (out_ref, picked_ref, span_ref, sems) = refs[:many], refs[many:]

        def base(d):
            there = lax.bitwise_xor(at_ref[1], d)
            return lax.rem(there, 2) * (span_rows // 2) + lax.shift_right_logical(there, 1) * piece_rows

        copies = assemble(pieces, piece_refs, span_ref, sems, base)
        for copy in copies:
            copy.start()
        for copy in copies:
            copy.wait()
        for j in range(rows // BLK):
            source = pl.ds(pl.multiple_of(index_ref[j] * BLK, BLK), BLK)
            picked_ref[:, pl.ds(j * BLK, BLK)] = jnp.transpose(span_ref[source, :])
        columns = pl.ds(pl.multiple_of(owner(at_ref, offset, n_row) * depth, depth), depth)
        out_ref[...] = dot(picked_ref[...], a_ref[:, columns]).astype(BF16)

    outs = [jax.ShapeDtypeStruct((width, depth), BF16), jax.ShapeDtypeStruct((width, rows), BF16)]
    scratch = [pltpu.VMEM((span_rows, width), BF16), pltpu.SemaphoreType.DMA((many,))]
    share = 2 * rows * depth
    held = [coupling] + [block for *_, block in pieces]
    return kernel_call(body, outs, [at, local_index], held, [], scratch, share * width, share)


def border_backward(at, coupling, picked, offsets, kinds, n_row):
    rows, depth = coupling.shape[0], coupling.shape[1] // n_row
    width, count = picked.shape[0], len(offsets)

    def body(at_ref, x_ref, a_ref, *out_refs):
        for offset, out_ref in zip(offsets, out_refs):
            columns = pl.ds(pl.multiple_of(owner(at_ref, offset, n_row) * depth, depth), depth)
            out_ref[...] = dot(x_ref[...], a_ref[:, columns]).astype(out_ref.dtype)

    outs = [jax.ShapeDtypeStruct((width, depth), kind) for kind in kinds]
    share = 2 * rows * depth * count
    return kernel_call(body, outs, [at], [picked, coupling], [], [], share * width, share)


def solve(n_front, n_row, rhs_front, rhs_root, pivot_inverse, border_coupling, root_inverse, border_map):
    row_at = lax.axis_index("row").astype(jnp.int32)
    at = PLACE
    span_rows = root_inverse.shape[1]
    piece_rows, width = span_rows // n_front, rhs_front.shape[1]
    local_index = border_map[0] - row_at * (span_rows // BLK)
    first_at, later_at = far_offsets(n_row)
    block = jax.ShapeDtypeStruct((pivot_inverse.shape[0], width), F32)
    half = jax.ShapeDtypeStruct(block.shape, BF16)
    straight, across = ((1,), (0,)), ((1,), (1,))

    found = gather_row(rhs_front, n_row)
    early, last = found[:-1], found[-1:]
    partial = pivot_products(at, pivot_inverse, early, n_row, straight, lambda t: [t], [block])
    inner, inner_half = pivot_products(
        at,
        pivot_inverse,
        last,
        n_row,
        straight,
        lambda t, p: [t + p, (t + p).astype(BF16)],
        [block, half],
        partial,
    )
    found = gather_row(inner_half, n_row)
    partial, own_rhs = border_partial(at, border_coupling, found[:2], n_row, None, rhs_root, piece_rows)
    partial, inverse = border_partial(
        at, border_coupling, found[2:-1], n_row, partial, root_inverse, root_inverse.shape[0]
    )
    send, keep = border_scatter(
        at, local_index, border_coupling, found[-1:], partial, n_row, n_front, span_rows
    )
    came = swap(send, n_front, 1)
    low, high = sum_halves(keep, came, [(3, 0), (3, 1)])
    low, high = swap(low, n_front, 2), swap(high, n_front, 4)
    x_low, y_high = sum_halves(keep, came, [(1, 0), (2, 1)])
    x_low, y_high = swap(x_low, n_front, 2), swap(y_high, n_front, 4)
    x_high, y_low = sum_relayed(keep, came, low, high)
    x_high, y_low = swap(x_high, n_front, 2), swap(y_low, n_front, 4)
    pieces = gather_front(*own_part(own_rhs, keep, came, (x_low, y_low), (x_high, y_high)), n_front)

    def root(offsets, kind):
        outs = root_products(at, inverse, pieces, offsets, [kind] * len(offsets), n_row, n_front)
        return dict(zip(offsets, outs))

    first = {}
    for offset in first_at:
        first.update(root([offset], BF16))
    rest = root(later_at + [0], F32)
    root_solution = scatter_row(first, rest, rest[0], n_row)
    spans = gather_front(*to_plane(root_solution.astype(BF16), n_row), n_front)

    out, picked = border_pick(at, local_index, border_coupling, spans, first_at[0], n_row, n_front)
    first = {first_at[0]: out}
    for offset in first_at[1:]:
        first[offset] = border_backward(at, border_coupling, picked, [offset], [BF16], n_row)[0]
    offsets = later_at + [0]
    rest = dict(zip(offsets, border_backward(at, border_coupling, picked, offsets, [F32] * len(offsets), n_row)))
    pulled = scatter_row(first, rest, rest[0], n_row).astype(BF16)
    found = gather_row(pulled, n_row)
    early, last = found[:-1], found[-1:]
    partial = pivot_products(
        at, pivot_inverse, early, n_row, across, lambda t, i: [i - t], [block], [inner]
    )
    front_solution = pivot_products(
        at, pivot_inverse, last, n_row, across, lambda t, p: [p - t], [block], partial, True
    )
    return front_solution[0], root_solution


def solve_plain(n_front, n_row, rhs_front, rhs_root, pivot_inverse, border_coupling, root_inverse, border_map):
    row_at = lax.axis_index("row")
    front_at = lax.axis_index("front")
    width = rhs_front.shape[1]
    inner = dot(pivot_inverse, lax.all_gather(rhs_front, "row", axis=0, tiled=True))
    contrib = dot(border_coupling, lax.all_gather(inner.astype(BF16), "row", axis=0, tiled=True))
    block_local = border_map.shape[1]
    span_rows = root_inverse.shape[1]
    span_blocks = span_rows // BLK
    local_index = border_map[0] - row_at * span_blocks
    select = (local_index[None, :] == jnp.arange(span_blocks, dtype=jnp.int32)[:, None]).astype(F32)
    dense = jnp.einsum(
        "kj,jcn->kcn", select, contrib.reshape(block_local, BLK, width), precision=lax.Precision.HIGHEST
    ).reshape(span_rows, width)
    shares = lax.psum_scatter(dense, "front", scatter_dimension=0, tiled=True)
    own_rhs = lax.dynamic_slice_in_dim(rhs_root, front_at * shares.shape[0], shares.shape[0], 0)
    schur_rhs = lax.all_gather((own_rhs - shares).astype(BF16), "front", axis=0, tiled=True)
    root_solution = lax.psum_scatter(dot(root_inverse, schur_rhs), "row", scatter_dimension=0, tiled=True)
    gathered = lax.all_gather(root_solution.astype(BF16), ("front", "row"), axis=0, tiled=True)
    ranged = lax.dynamic_slice_in_dim(gathered, row_at * span_rows, span_rows, 0)
    picked = jnp.take(ranged.reshape(span_blocks, BLK, width), local_index, axis=0)
    picked = picked.reshape(block_local * BLK, width)
    pulled = lax.psum_scatter(
        dot(border_coupling, picked, ((0,), (0,))), "row", scatter_dimension=0, tiled=True
    ).astype(BF16)
    correction = dot(pivot_inverse, lax.all_gather(pulled, "row", axis=0, tiled=True))
    return inner - correction, root_solution


def solution(mesh):
    in_specs = (
        P(("front", "row"), None),
        P("row", None),
        P(("front", "row"), None),
        P(("front", "row"), None),
        P("front", "row"),
        P("front", "row"),
    )
    out_specs = (P(("front", "row"), None), P(("front", "row"), None))
    n_front, n_row = mesh.shape["front"], mesh.shape["row"]

    def per_device(*arrays):
        root_inverse, width = arrays[4], arrays[0].shape[1]
        fits = (
            n_front == 8
            and n_front == 2 * n_row
            and root_inverse.shape[1] % (n_front * BLK) == 0
            and root_inverse.shape[0] == n_row * (root_inverse.shape[1] // n_front)
            and root_inverse.shape[1] % (n_front * n_row * 16) == 0
            and arrays[2].shape[1] % (n_row * BLK) == 0
            and width % BLK == 0
        )
        return (solve if fits else solve_plain)(n_front, n_row, *arrays)

    return jax.shard_map(per_device, mesh=mesh, in_specs=in_specs, out_specs=out_specs, check_vma=False)
```
